32 devices in a mesh: ctx: 8 (over z, x), head: 4 (over y, core).
Axes of the slice: x: 2, y: 2, z: 4, core: 2. Of those that a mesh axis runs over, the one named last changes fastest.
Arguments:
- queries: bfloat16 [1024, 8192], P('ctx', 'head'), may hold values from -7 to 7
- span_kv: bfloat16 [1024, 8, 256], P('ctx', 'head'), may hold values from -7 to 7
- cache_kv: bfloat16 [32768, 8, 256], P('ctx', 'head'), may hold values from -6 to 6
- verticals: int32 [8, 64], P('head'), may hold values from 0 to 511, as said below
- offsets: int32 [8, 8], P('head'), may hold values from 0 to 7, as said below
Outputs:
- attended: bfloat16 [1024, 8192], P(('ctx', 'head'))
The draws below stay inside these ranges and needn't reach their ends.
Inputs may be any that keep to these rules, and one draw needn't show every extreme that they name: `verticals`: each row holds 64 distinct cache blocks. Cache block b lies in the cache of index b // 64 of ctx; at most 16 blocks of one row lie in one index's cache, and in every row some index holds exactly 16. Each row holds 8 distinct offsets, 0 among them; some row holds 7.
All inputs are finite; a program needn't handle non-finite values.
Results may differ from the reference program's by a relative error of at most 0.0065.
Values may be sent and summed in bfloat16 or wider, within the bound.
No kernel may reach another device: no remote copies, remote signals or barrier semaphores. Data moves between devices by JAX's collectives and lax.ppermute only.
A program may use at most 192 MiB of HBM per device.

```python
import jax
import jax.numpy as jnp
from jax import lax

QH = 64
KVH = 8
HD = 128
BLK = 64
CACHE_DEV = 4096
NV = 64
NS = 8
VCAP = 16
SMAX = 8
SPAN = 1024
CACHE = 32768
N_CTX = 8


def draw_verticals(key, part):
    owner_total = N_CTX
    per_owner = CACHE_DEV // BLK
    slot_total = owner_total * VCAP

    def one_head(head_key):
        key_one, key_two, key_three, key_four = jax.random.split(head_key, 4)
        full_owner = jax.random.randint(key_one, (), 0, owner_total)
        slot_order = jax.random.permutation(key_two, slot_total)
        priority = jnp.where(slot_order // VCAP == full_owner, 0, 1) * slot_total + jnp.arange(slot_total)
        chosen = slot_order[jnp.argsort(priority)][:NV]
        chosen = chosen[jax.random.permutation(key_four, NV)]
        tables = jax.vmap(lambda table_key: jax.random.permutation(table_key, per_owner))(jax.random.split(key_three, owner_total))
        owner_id = chosen // VCAP
        slot_id = chosen % VCAP
        return (owner_id * per_owner + tables[owner_id, slot_id]).astype(jnp.int32)
    return jax.vmap(one_head)(jax.random.split(key, KVH))


def draw_offsets(key, part):
    key_one, key_two = jax.random.split(key)
    chosen_head = jax.random.randint(key_one, (), 0, KVH)

    def one_head(head_key, head_index):
        key_first, key_second = jax.random.split(head_key)
        chosen_offsets = jax.random.permutation(key_first, SMAX - 1)[:NS - 1] + 1
        forced = jnp.where(jnp.any(chosen_offsets == SMAX - 1), chosen_offsets, chosen_offsets.at[NS - 2].set(SMAX - 1))
        chosen_offsets = jnp.where(head_index == chosen_head, forced, chosen_offsets)
        offset_row = jnp.concatenate([jnp.zeros((1,), jnp.int32), chosen_offsets.astype(jnp.int32)])
        return offset_row[jax.random.permutation(key_second, NS)]
    return jax.vmap(one_head)(jax.random.split(key_two, KVH), jnp.arange(KVH))


def draw_queries(key, part):
    key_one = jax.random.fold_in(jax.random.fold_in(key, 3), 0)
    values_base = jnp.clip(jax.random.normal(key_one, (SPAN, QH, HD)), -6.0, 6.0)
    return values_base.reshape(SPAN, QH * HD).astype(jnp.bfloat16)


def draw_span_kv(key, part):
    key_one = jax.random.fold_in(jax.random.fold_in(key, 5), 0)
    values_base = jnp.clip(jax.random.normal(key_one, (SPAN, KVH, 2 * HD)), -6.0, 6.0)
    return values_base.astype(jnp.bfloat16)


def steps_of(key, shape, shards, least, largest):
    def one(axis_at, parts):
        steps = jax.random.uniform(jax.random.fold_in(jax.random.fold_in(key, 6), axis_at), (parts,), jnp.float32, least / len(shards), largest / len(shards))
        return jnp.repeat(jnp.exp(steps), shape[axis_at] // parts).reshape((-1,) + (1,) * (len(shape) - axis_at - 1))

    factor_of = one(*shards[0])
    for cut in shards[1:]:
        factor_of = factor_of * one(*cut)
    return factor_of


def gaussian(stream_key, dims, deviation, reach, cuts=(), held_as=jnp.bfloat16):
    values = deviation * jax.random.normal(stream_key, dims, jnp.float32)
    if cuts:
        values = values * steps_of(stream_key, dims, cuts, -0.22, 0.18)
    return jnp.clip(values, -reach, reach).astype(held_as)


def setup_inputs(seed: int = 0) -> dict:
    seeds = jax.random.split(jax.random.key(seed), 6)
    return {
        "queries": draw_queries(jax.random.fold_in(seeds[5], 71), 0),
        "span_kv": draw_span_kv(jax.random.fold_in(seeds[5], 71), 0),
        "cache_kv": gaussian(seeds[2], (CACHE, KVH, 2 * HD), 1.0, 6.0, ((0, 8), (1, 4))),
        "verticals": draw_verticals(jax.random.fold_in(seeds[5], 71), 0),
        "offsets": draw_offsets(jax.random.fold_in(seeds[5], 71), 0),
    }


def reference(queries, span_kv, cache_kv, verticals, offsets):
    span_blocks = SPAN // BLK
    group_size = QH // KVH
    score_scale = HD ** -0.5
    cache_blocked = cache_kv.reshape(CACHE // BLK, BLK, KVH, 2 * HD)
    span_blocked = span_kv.reshape(span_blocks, BLK, KVH, 2 * HD)
    query_blocked = queries.reshape(span_blocks, BLK, KVH, group_size, HD)
    causal = jnp.arange(BLK)[None, :] <= jnp.arange(BLK)[:, None]

    def per_head(head_index):
        cache_head = lax.dynamic_index_in_dim(cache_blocked, head_index, 2, False)
        span_head = lax.dynamic_index_in_dim(span_blocked, head_index, 2, False)
        query_head = lax.dynamic_index_in_dim(query_blocked, head_index, 2, False)
        vertical_ids = lax.dynamic_index_in_dim(verticals, head_index, 0, False)
        head_offsets = lax.dynamic_index_in_dim(offsets, head_index, 0, False)
        vertical_rows = jnp.take(cache_head, vertical_ids, axis=0).reshape(NV * BLK, 2 * HD).astype(jnp.float32)

        def per_block(block_index):
            query_block = lax.dynamic_index_in_dim(query_head, block_index, 0, False).astype(jnp.float32)
            source_block = block_index - head_offsets
            source_live = source_block >= 0
            slash_rows = jnp.take(span_head, jnp.maximum(source_block, 0), axis=0).astype(jnp.float32)
            vertical_scores = jnp.einsum("qgd,kd->gqk", query_block, vertical_rows[:, :HD]) * score_scale
            slash_scores = jnp.einsum("qgd,skd->gqsk", query_block, slash_rows[..., :HD]) * score_scale
            allowed = source_live[:, None, None] & ((head_offsets[:, None, None] > 0) | causal[None])
            allowed = jnp.transpose(allowed, (1, 0, 2))
            slash_scores = jnp.where(allowed[None], slash_scores, -jnp.inf)
            row_top = jnp.maximum(jnp.max(vertical_scores, axis=-1), jnp.max(slash_scores, axis=(-2, -1)))
            vertical_weights = jnp.exp(vertical_scores - row_top[..., None])
            slash_weights = jnp.exp(slash_scores - row_top[..., None, None])
            row_total = jnp.sum(vertical_weights, axis=-1) + jnp.sum(slash_weights, axis=(-2, -1))
            weighted = jnp.einsum("gqk,kd->gqd", vertical_weights.astype(jnp.bfloat16).astype(jnp.float32), vertical_rows[:, HD:])
            weighted = weighted + jnp.einsum("gqsk,skd->gqd", slash_weights.astype(jnp.bfloat16).astype(jnp.float32), slash_rows[..., HD:])
            normalized = weighted / row_total[..., None]
            return jnp.transpose(normalized, (1, 0, 2)).astype(jnp.bfloat16)

        return lax.map(per_block, jnp.arange(span_blocks, dtype=jnp.int32))

    result = lax.map(per_head, jnp.arange(KVH, dtype=jnp.int32))
    return jnp.transpose(result, (1, 2, 0, 3, 4)).reshape(SPAN, QH * HD)
```

```python
import functools

import jax
import jax.numpy as jnp
from jax import lax
from jax.experimental import pallas as pl
from jax.experimental.pallas import tpu as pltpu
from jax.sharding import PartitionSpec as P

BLK = 64
NV = 64
MASKED = -1e30
LOG2E = 1.4426950408889634


def collect_kernel(owners, cap, verticals, cache, span, mine, theirs, sem, span_sem):
    me = lax.axis_index("ctx")
    upper = me // (owners // 2)
    cache_blocks = cache.shape[1] // BLK
    tokens = span.shape[1]
    first = me * cache_blocks
    tail = pl.ds(cap * BLK, tokens)
    for place, target in ((0, mine), (1, theirs)):
        head = upper if place == 0 else 1 - upper
        pltpu.make_async_copy(span.at[head], target.at[tail], span_sem.at[place]).start()

        def visit(n, count):
            block = verticals[head, n] - first
            hit = (block >= 0) & (block < cache_blocks) & (count < cap)

            @pl.when(hit)
            def _():
                pltpu.make_async_copy(
                    cache.at[head, pl.ds(pl.multiple_of(block * BLK, BLK), BLK)],
                    target.at[pl.ds(pl.multiple_of(count * BLK, BLK), BLK)],
                    sem.at[place],
                ).start()

            return count + hit.astype(jnp.int32)

        found = lax.fori_loop(0, NV, visit, jnp.int32(0))

        def done(n, carry):
            pltpu.make_async_copy(
                cache.at[head, pl.ds(0, BLK)], target.at[pl.ds(0, BLK)], sem.at[place]
            ).wait()
            return carry

        lax.fori_loop(0, found, done, 0)
    for place, target in ((0, mine), (1, theirs)):
        pltpu.make_async_copy(span.at[0], target.at[tail], span_sem.at[place]).wait()


def attend_kernel(
    owners, cap, group, depth, width,
    verticals, offsets, q_near, q_far, near, far, out,
    keys, span, slash, bias, counts, sem, span_sem,
):
    me = lax.axis_index("ctx")
    half = owners // 2
    upper = me // half
    head = upper
    tokens = q_near.shape[0]
    blocks = tokens // BLK
    slash_count = offsets.shape[1]
    cache_blocks = counts.shape[0]
    rows = group * BLK
    factor = LOG2E * depth**-0.5

    def clear(n, carry):
        counts[n] = 0
        return carry

    lax.fori_loop(0, owners, clear, 0)

    def tally(n, carry):
        owner = verticals[head, n] // width
        counts[owner] = counts[owner] + 1
        return carry

    lax.fori_loop(0, NV, tally, 0)
    place = jnp.int32(0)
    for source, base in ((near, upper * half), (far, (1 - upper) * half)):

        def fetch_owner(k, place):
            owner = base + k
            pltpu.make_async_copy(
                source.at[k, pl.ds(cap * BLK, tokens)],
                span.at[pl.ds(pl.multiple_of(owner * tokens, BLK), tokens)],
                span_sem,
            ).start()
            live = jnp.minimum(counts[owner], cap)

            def fetch(n, place):
                pltpu.make_async_copy(
                    source.at[k, pl.ds(pl.multiple_of(n * BLK, BLK), BLK)],
                    keys.at[pl.ds(pl.multiple_of(place * BLK, BLK), BLK)],
                    sem,
                ).start()
                return place + 1

            return lax.fori_loop(0, live, fetch, place)

        place = lax.fori_loop(0, half, fetch_owner, place)
    pltpu.make_async_copy(span, span, span_sem).wait()
    pltpu.make_async_copy(keys, keys, sem).wait()

    q_at = lax.broadcasted_iota(jnp.int32, (BLK, BLK), 0)
    k_at = lax.broadcasted_iota(jnp.int32, (BLK, BLK), 1)
    behind = k_at <= q_at
    chunk = 1024
    for side, q_ref in ((0, q_near), (1, q_far)):
        index = me if side == 0 else (me + half) % owners
        slot = upper if side == 0 else 1 - upper
        for block in range(blocks):
            at = index * blocks + block
            for s in range(slash_count):
                offset = offsets[head, s]
                source_block = at - offset
                alive = source_block >= 0
                start = pl.multiple_of(jnp.maximum(source_block, 0) * BLK, BLK)
                slash[s * BLK : (s + 1) * BLK, :] = span[pl.ds(start, BLK), :]
                allowed = alive & ((offset > 0) | behind)
                bias[:, s * BLK : (s + 1) * BLK] = jnp.where(allowed, 0.0, MASKED)
            q = jnp.concatenate(
                [q_ref[block * BLK : (block + 1) * BLK, j * depth : (j + 1) * depth] for j in range(group)], 0
            )
            scores = lax.dot_general(
                q, slash[:, :depth], (((1,), (1,)), ((), ())), preferred_element_type=jnp.float32
            )
            scores = scores.reshape(group, BLK, slash_count * BLK) * factor + bias[...][None]
            scores = scores.reshape(rows, slash_count * BLK)
            top = jnp.max(scores, axis=1, keepdims=True)
            weights = jnp.exp2(scores - top)
            total = jnp.sum(weights, axis=1, keepdims=True)
            acc = jnp.dot(weights.astype(jnp.bfloat16), slash[:, depth:], preferred_element_type=jnp.float32)
            for c in range(NV * BLK // chunk):
                span_of = slice(c * chunk, (c + 1) * chunk)
                scores = lax.dot_general(
                    q, keys[span_of, :depth], (((1,), (1,)), ((), ())), preferred_element_type=jnp.float32
                ) * factor
                new_top = jnp.maximum(top, jnp.max(scores, axis=1, keepdims=True))
                weights = jnp.exp2(scores - new_top)
                keep = jnp.exp2(top - new_top)
                total = total * keep + jnp.sum(weights, axis=1, keepdims=True)
                acc = acc * keep + jnp.dot(
                    weights.astype(jnp.bfloat16), keys[span_of, depth:], preferred_element_type=jnp.float32
                )
                top = new_top
            result = (acc / total).astype(out.dtype)
            piece = out.shape[2]
            per_block = BLK // piece
            for j in range(group):
                for h in range(per_block):
                    out[block * per_block + h, slot, :, j * depth : (j + 1) * depth] = result[
                        j * BLK + h * piece : j * BLK + (h + 1) * piece
                    ]


def body(queries, span_kv, cache_kv, verticals, offsets):
    tokens = queries.shape[0]
    heads_kv, row_width = span_kv.shape[1:]
    depth = row_width // 2
    columns = queries.shape[1] // heads_kv
    group = columns // depth
    owners = lax.axis_size("ctx")
    head_groups = lax.axis_size("head")
    half = owners // 2
    cache_rows = cache_kv.shape[0]
    cache_blocks = cache_rows // BLK
    cap = max(2, 2 * NV // owners)
    me = lax.axis_index("ctx")
    upper = me // half

    across = [(i, (i + half) % owners) for i in range(owners)]
    send_q = lax.dynamic_slice_in_dim(queries, (1 - upper) * columns, columns, 1)
    q_near = lax.dynamic_slice_in_dim(queries, upper * columns, columns, 1)
    rows = cap * BLK + tokens
    payload = jax.ShapeDtypeStruct((rows, row_width), queries.dtype)
    mine, theirs = pl.pallas_call(
        functools.partial(collect_kernel, owners, cap),
        out_shape=(payload, payload),
        grid_spec=pltpu.PrefetchScalarGridSpec(
            num_scalar_prefetch=1,
            grid=(1,),
            in_specs=[pl.BlockSpec(memory_space=pl.ANY)] * 2,
            out_specs=[pl.BlockSpec(memory_space=pl.ANY)] * 2,
            scratch_shapes=[pltpu.SemaphoreType.DMA((2,)), pltpu.SemaphoreType.DMA((2,))],
        ),
        name="collect_slots",
    )(verticals, jnp.transpose(cache_kv, (1, 0, 2)), jnp.transpose(span_kv, (1, 0, 2)))
    crossed = lax.ppermute(theirs, "ctx", across)
    q_far = lax.ppermute(send_q, "ctx", across)
    halves = [list(range(half)), list(range(half, owners))]
    near = lax.all_gather(mine, "ctx", axis=0, axis_index_groups=halves)
    far = lax.all_gather(crossed, "ctx", axis=0, axis_index_groups=halves)

    piece = tokens // head_groups
    attended = pl.pallas_call(
        functools.partial(attend_kernel, owners, cap, group, depth, cache_blocks),
        out_shape=jax.ShapeDtypeStruct((head_groups, 2, piece, columns), queries.dtype),
        grid_spec=pltpu.PrefetchScalarGridSpec(
            num_scalar_prefetch=2,
            grid=(1,),
            in_specs=[
                pl.BlockSpec(memory_space=pltpu.VMEM),
                pl.BlockSpec(memory_space=pltpu.VMEM),
                pl.BlockSpec(memory_space=pl.ANY),
                pl.BlockSpec(memory_space=pl.ANY),
            ],
            out_specs=pl.BlockSpec(memory_space=pltpu.VMEM),
            scratch_shapes=[
                pltpu.VMEM((NV * BLK, row_width), queries.dtype),
                pltpu.VMEM((owners * tokens, row_width), queries.dtype),
                pltpu.VMEM((offsets.shape[1] * BLK, row_width), queries.dtype),
                pltpu.VMEM((BLK, offsets.shape[1] * BLK), jnp.float32),
                pltpu.SMEM((owners,), jnp.int32),
                pltpu.SemaphoreType.DMA,
                pltpu.SemaphoreType.DMA,
            ],
        ),
        compiler_params=pltpu.CompilerParams(vmem_limit_bytes=48 * 1024 * 1024),
        name="attend",
    )(verticals, offsets, q_near, q_far, near, far)
    attended = attended.reshape(head_groups * 2 * piece, columns)
    groups = [
        [(a * half + i) * head_groups + h for h in range(head_groups) for a in range(2)] for i in range(half)
    ]
    return lax.all_to_all(
        attended, ("ctx", "head"), split_axis=0, concat_axis=1, axis_index_groups=groups, tiled=True
    )


def solution(mesh):
    in_specs = (
        P("ctx", "head"),
        P("ctx", "head", None),
        P("ctx", "head", None),
        P("head", None),
        P("head", None),
    )
    out_specs = P(("ctx", "head"), None)
    return jax.shard_map(body, mesh=mesh, in_specs=in_specs, out_specs=out_specs, check_vma=False)
```

```python
import functools

import jax
import jax.numpy as jnp
from jax import lax
from jax.experimental import pallas as pl
from jax.experimental.pallas import tpu as pltpu
from jax.sharding import PartitionSpec as P

BLK = 64
NV = 64
MASKED = -1e30
LOG2E = 1.4426950408889634


def collect_kernel(owners, cap, verticals, cache, span, mine, theirs, raw, sem):
    me = lax.axis_index("ctx")
    upper = me // (owners // 2)
    cache_blocks = cache.shape[0] // BLK
    first = me * cache_blocks

    def block_copy(block, place, slot):
        return pltpu.make_async_copy(
            cache.at[pl.ds(pl.multiple_of(block * BLK, BLK), BLK)], raw.at[place, slot], sem.at[place, slot]
        )

    found = []
    for place in range(2):
        head = upper if place == 0 else 1 - upper

        def visit(n, count):
            block = verticals[head, n] - first
            hit = (block >= 0) & (block < cache_blocks) & (count < cap)

            @pl.when(hit)
            def _():
                block_copy(block, place, count).start()

            return count + hit.astype(jnp.int32)

        found.append(lax.fori_loop(0, NV, visit, jnp.int32(0)))
    for own in range(2):

        @pl.when(upper == own)
        def _():
            mine[cap * BLK :, :] = span[:, own, :]
            theirs[cap * BLK :, :] = span[:, 1 - own, :]
            for place, target in ((0, mine), (1, theirs)):
                head = own if place == 0 else 1 - own

                def unpack(slot, carry):
                    block_copy(0, place, slot).wait()
                    target[pl.ds(pl.multiple_of(slot * BLK, BLK), BLK), :] = raw[place, slot, :, head, :]
                    return carry

                lax.fori_loop(0, found[place], unpack, 0)


def attend_kernel(
    owners, cap, group, depth, width,
    verticals, offsets, q_near, q_far, *rest,
):
    near, far = rest[: owners // 2], rest[owners // 2 : owners]
    out, keys, span, slash, bias, counts, sem, span_sem = rest[owners:]
    me = lax.axis_index("ctx")
    half = owners // 2
    upper = me // half
    head = upper
    tokens = q_near.shape[0]
    blocks = tokens // BLK
    slash_count = offsets.shape[1]
    cache_blocks = counts.shape[0]
    rows = group * BLK
    factor = LOG2E * depth**-0.5

    def clear(n, carry):
        counts[n] = 0
        return carry

    lax.fori_loop(0, owners, clear, 0)

    def tally(n, carry):
        owner = verticals[head, n] // width
        counts[owner] = counts[owner] + 1
        return carry

    lax.fori_loop(0, NV, tally, 0)
    place = jnp.int32(0)
    for pieces, base in ((near, upper * half), (far, (1 - upper) * half)):
        for m, source in enumerate(pieces):
            owner = base + ((me % half) ^ m)
            pltpu.make_async_copy(
                source.at[pl.ds(cap * BLK, tokens)],
                span.at[pl.ds(pl.multiple_of(owner * tokens, BLK), tokens)],
                span_sem,
            ).start()

            def fetch(n, place):
                pltpu.make_async_copy(
                    source.at[pl.ds(pl.multiple_of(n * BLK, BLK), BLK)],
                    keys.at[pl.ds(pl.multiple_of(place * BLK, BLK), BLK)],
                    sem,
                ).start()
                return place + 1

            place = lax.fori_loop(0, jnp.minimum(counts[owner], cap), fetch, place)
    pltpu.make_async_copy(span, span, span_sem).wait()
    pltpu.make_async_copy(keys, keys, sem).wait()

    q_at = lax.broadcasted_iota(jnp.int32, (BLK, BLK), 0)
    k_at = lax.broadcasted_iota(jnp.int32, (BLK, BLK), 1)
    behind = k_at <= q_at
    chunk = 1024
    for side, q_ref in ((0, q_near), (1, q_far)):
        index = me if side == 0 else (me + half) % owners
        slot = upper if side == 0 else 1 - upper
        for block in range(blocks):
            at = index * blocks + block
            for s in range(slash_count):
                offset = offsets[head, s]
                source_block = at - offset
                alive = source_block >= 0
                start = pl.multiple_of(jnp.maximum(source_block, 0) * BLK, BLK)
                slash[s * BLK : (s + 1) * BLK, :] = span[pl.ds(start, BLK), :]
                allowed = alive & ((offset > 0) | behind)
                bias[:, s * BLK : (s + 1) * BLK] = jnp.where(allowed, 0.0, MASKED)
            q = jnp.concatenate(
                [q_ref[block * BLK : (block + 1) * BLK, j * depth : (j + 1) * depth] for j in range(group)], 0
            )
            scores = lax.dot_general(
                q, slash[:, :depth], (((1,), (1,)), ((), ())), preferred_element_type=jnp.float32
            )
            scores = scores.reshape(group, BLK, slash_count * BLK) * factor + bias[...][None]
            scores = scores.reshape(rows, slash_count * BLK)
            top = jnp.max(scores, axis=1, keepdims=True)
            weights = jnp.exp2(scores - top)
            total = jnp.sum(weights, axis=1, keepdims=True)
            acc = jnp.dot(weights.astype(jnp.bfloat16), slash[:, depth:], preferred_element_type=jnp.float32)
            for c in range(NV * BLK // chunk):
                span_of = slice(c * chunk, (c + 1) * chunk)
                scores = lax.dot_general(
                    q, keys[span_of, :depth], (((1,), (1,)), ((), ())), preferred_element_type=jnp.float32
                ) * factor
                new_top = jnp.maximum(top, jnp.max(scores, axis=1, keepdims=True))
                weights = jnp.exp2(scores - new_top)
                keep = jnp.exp2(top - new_top)
                total = total * keep + jnp.sum(weights, axis=1, keepdims=True)
                acc = acc * keep + jnp.dot(
                    weights.astype(jnp.bfloat16), keys[span_of, depth:], preferred_element_type=jnp.float32
                )
                top = new_top
            result = (acc / total).astype(out.dtype)
            piece = out.shape[2]
            per_block = BLK // piece
            for j in range(group):
                for h in range(per_block):
                    out[block * per_block + h, slot, :, j * depth : (j + 1) * depth] = result[
                        j * BLK + h * piece : j * BLK + (h + 1) * piece
                    ]


def gather_half(x, half):
    pieces = {0: x}
    bit = half // 2
    while bit:
        pairs = [(i, i ^ bit) for i in range(2 * half)]
        pieces.update({m | bit: lax.ppermute(piece, "ctx", pairs) for m, piece in pieces.items()})
        bit //= 2
    return [pieces[m] for m in range(half)]


def body(queries, span_kv, cache_kv, verticals, offsets):
    tokens = queries.shape[0]
    heads_kv, row_width = span_kv.shape[1:]
    depth = row_width // 2
    columns = queries.shape[1] // heads_kv
    group = columns // depth
    owners = lax.axis_size("ctx")
    head_groups = lax.axis_size("head")
    half = owners // 2
    cache_rows = cache_kv.shape[0]
    cache_blocks = cache_rows // BLK
    cap = max(2, 2 * NV // owners)
    me = lax.axis_index("ctx")
    upper = me // half

    across = [(i, (i + half) % owners) for i in range(owners)]
    send_q = lax.dynamic_slice_in_dim(queries, (1 - upper) * columns, columns, 1)
    q_near = lax.dynamic_slice_in_dim(queries, upper * columns, columns, 1)
    rows = cap * BLK + tokens
    payload = jax.ShapeDtypeStruct((rows, row_width), queries.dtype)
    q_far = lax.ppermute(send_q, "ctx", across)
    mine, theirs = pl.pallas_call(
        functools.partial(collect_kernel, owners, cap),
        out_shape=(payload, payload),
        grid_spec=pltpu.PrefetchScalarGridSpec(
            num_scalar_prefetch=1,
            grid=(1,),
            in_specs=[pl.BlockSpec(memory_space=pl.ANY), pl.BlockSpec(memory_space=pltpu.VMEM)],
            out_specs=[pl.BlockSpec(memory_space=pltpu.VMEM)] * 2,
            scratch_shapes=[
                pltpu.VMEM((2, cap, BLK, heads_kv, row_width), queries.dtype),
                pltpu.SemaphoreType.DMA((2, cap)),
            ],
        ),
        compiler_params=pltpu.CompilerParams(vmem_limit_bytes=60 * 1024 * 1024),
        name="collect_slots",
    )(verticals, cache_kv, span_kv)
    crossed = lax.ppermute(theirs, "ctx", across)
    near, far = gather_half(mine, half), gather_half(crossed, half)

    piece = tokens // head_groups
    attended = pl.pallas_call(
        functools.partial(attend_kernel, owners, cap, group, depth, cache_blocks),
        out_shape=jax.ShapeDtypeStruct((head_groups, 2, piece, columns), queries.dtype),
        grid_spec=pltpu.PrefetchScalarGridSpec(
            num_scalar_prefetch=2,
            grid=(1,),
            in_specs=[
                pl.BlockSpec(memory_space=pltpu.VMEM),
                pl.BlockSpec(memory_space=pltpu.VMEM),
            ]
            + [pl.BlockSpec(memory_space=pl.ANY)] * owners,
            out_specs=pl.BlockSpec(memory_space=pltpu.VMEM),
            scratch_shapes=[
                pltpu.VMEM((NV * BLK, row_width), queries.dtype),
                pltpu.VMEM((owners * tokens, row_width), queries.dtype),
                pltpu.VMEM((offsets.shape[1] * BLK, row_width), queries.dtype),
                pltpu.VMEM((BLK, offsets.shape[1] * BLK), jnp.float32),
                pltpu.SMEM((owners,), jnp.int32),
                pltpu.SemaphoreType.DMA,
                pltpu.SemaphoreType.DMA,
            ],
        ),
        compiler_params=pltpu.CompilerParams(vmem_limit_bytes=48 * 1024 * 1024),
        name="attend",
    )(verticals, offsets, q_near, q_far, *near, *far)
    attended = attended.reshape(head_groups * 2 * piece, columns)
    groups = [
        [(a * half + i) * head_groups + h for h in range(head_groups) for a in range(2)] for i in range(half)
    ]
    return lax.all_to_all(
        attended, ("ctx", "head"), split_axis=0, concat_axis=1, axis_index_groups=groups, tiled=True
    )


def solution(mesh):
    in_specs = (
        P("ctx", "head"),
        P("ctx", "head", None),
        P("ctx", "head", None),
        P("head", None),
        P("head", None),
    )
    out_specs = P(("ctx", "head"), None)
    return jax.shard_map(body, mesh=mesh, in_specs=in_specs, out_specs=out_specs, check_vma=False)
```

```python
import functools

import jax
import jax.numpy as jnp
from jax import lax
from jax.experimental import pallas as pl
from jax.experimental.pallas import tpu as pltpu
from jax.sharding import PartitionSpec as P

BLK = 64
NV = 64
MASKED = -1e30
CHUNK = 8
LOG2E = 1.4426950408889634


def collect_kernel(owners, cap, verticals, cache, span, mine, theirs, raw, sem):
    me = lax.axis_index("ctx")
    upper = me // (owners // 2)
    cache_blocks = cache.shape[0] // BLK
    first = me * cache_blocks

    def block_copy(block, place, slot):
        return pltpu.make_async_copy(
            cache.at[pl.ds(pl.multiple_of(block * BLK, BLK), BLK)], raw.at[place, slot], sem.at[place, slot]
        )

    found = []
    for place in range(2):
        head = upper if place == 0 else 1 - upper

        def visit(n, count):
            block = verticals[head, n] - first
            hit = (block >= 0) & (block < cache_blocks) & (count < cap)

            @pl.when(hit)
            def _():
                block_copy(block, place, count).start()

            return count + hit.astype(jnp.int32)

        found.append(lax.fori_loop(0, NV, visit, jnp.int32(0)))
    for own in range(2):

        @pl.when(upper == own)
        def _():
            mine[cap * BLK :, :] = span[:, own, :]
            theirs[cap * BLK :, :] = span[:, 1 - own, :]
            for place, target in ((0, mine), (1, theirs)):
                head = own if place == 0 else 1 - own

                def unpack(slot, carry):
                    block_copy(0, place, slot).wait()
                    target[pl.ds(pl.multiple_of(slot * BLK, BLK), BLK), :] = raw[place, slot, :, head, :]
                    return carry

                lax.fori_loop(0, found[place], unpack, 0)


def attend_kernel(owners, cap, group, depth, width, pieces, known, first, last, verticals, offsets, q_near, q_far, *refs):
    refs = list(refs)
    sources = [refs.pop(0) for _ in pieces]
    before = None if first else [refs.pop(0) for _ in range(3)]
    out = refs.pop(0) if last else None
    top, total, acc = refs[:3]
    queries, keys, counts, sem = refs[3:7]
    me = lax.axis_index("ctx")
    half = owners // 2
    upper = me // half
    head = upper
    tokens = q_near.shape[0]
    blocks = tokens // BLK
    rows = group * BLK
    factor = LOG2E * depth**-0.5

    def clear(n, carry):
        counts[n] = 0
        return carry

    lax.fori_loop(0, owners, clear, 0)

    def tally(n, carry):
        owner = verticals[head, n] // width
        counts[owner] = counts[owner] + 1
        return carry

    lax.fori_loop(0, NV, tally, 0)

    def owner_of(far, m):
        return ((1 - upper) if far else upper) * half + ((me % half) ^ m)

    def live(piece):
        return jnp.minimum(counts[owner_of(*piece)], cap)

    seen = jnp.int32(0)
    for piece in pieces[:known]:
        seen = seen + live(piece)
    present = seen
    for piece in pieces[known:]:
        present = present + live(piece)
    begin = seen // CHUNK * CHUNK
    end = jnp.int32(NV) if last else present // CHUNK * CHUNK
    place = jnp.int32(0)
    for piece, source in zip(pieces, sources):
        held = live(piece)

        def fetch(n, carry, place=place, source=source):
            pltpu.make_async_copy(
                source.at[pl.ds(pl.multiple_of(n * BLK, BLK), BLK)],
                keys.at[pl.ds(pl.multiple_of((place + n - begin) * BLK, BLK), BLK)],
                sem,
            ).start()
            return carry

        lax.fori_loop(jnp.clip(begin - place, 0, held), jnp.clip(end - place, 0, held), fetch, 0)
        place = place + held

    if last:
        span, slash, bias, span_sem = refs[7:]
        for piece, source in zip(pieces, sources):
            pltpu.make_async_copy(
                source.at[pl.ds(cap * BLK, tokens)],
                span.at[pl.ds(pl.multiple_of(owner_of(*piece) * tokens, BLK), tokens)],
                span_sem,
            ).start()
    for tile in range(2 * blocks):
        q_ref, block = (q_near, tile) if tile < blocks else (q_far, tile - blocks)
        for j in range(group):
            queries[tile * rows + j * BLK : tile * rows + (j + 1) * BLK, :] = q_ref[
                block * BLK : (block + 1) * BLK, j * depth : (j + 1) * depth
            ]
    if first:
        top[...] = jnp.full(top.shape, MASKED, jnp.float32)
        total[...] = jnp.zeros(total.shape, jnp.float32)
        acc[...] = jnp.zeros(acc.shape, jnp.float32)
    else:
        top[...] = before[0][...]
        total[...] = before[1][...]
        acc[...] = before[2][...]

    def fold(at, scores, values):
        lanes = top.shape[1]
        repeat = scores.shape[1] // lanes
        old = top[at, :]
        new = jnp.maximum(old, jnp.max(scores, axis=1, keepdims=True))
        weights = jnp.exp2((scores - jnp.concatenate([new] * repeat, 1)) * factor)
        keep = jnp.exp2((old - new) * factor)
        top[at, :] = new
        total[at, :] = total[at, :] * keep + jnp.sum(weights, axis=1, keepdims=True)
        acc[at, :] = acc[at, :] * keep + jnp.dot(
            weights.astype(jnp.bfloat16), values, preferred_element_type=jnp.float32
        )

    def products(at, rows_k):
        return lax.dot_general(
            queries[at, :], rows_k, (((1,), (1,)), ((), ())), preferred_element_type=jnp.float32
        )

    tiles = [slice(tile * rows, (tile + 1) * rows) for tile in range(2 * blocks)]
    if last:
        pltpu.make_async_copy(span, span, span_sem).wait()
        slash_count = offsets.shape[1]
        q_at = lax.broadcasted_iota(jnp.int32, (BLK, BLK), 0)
        k_at = lax.broadcasted_iota(jnp.int32, (BLK, BLK), 1)
        behind = k_at <= q_at
        for tile, at in enumerate(tiles):
            index = me if tile < blocks else (me + half) % owners
            position = index * blocks + tile % blocks
            for s in range(slash_count):
                offset = offsets[head, s]
                source_block = position - offset
                start = pl.multiple_of(jnp.maximum(source_block, 0) * BLK, BLK)
                slash[tile, s * BLK : (s + 1) * BLK, :] = span[pl.ds(start, BLK), :]
                allowed = (source_block >= 0) & ((offset > 0) | behind)
                bias[tile, :, s * BLK : (s + 1) * BLK] = jnp.where(allowed, 0.0, MASKED)
            scores = products(at, slash[tile, :, :depth])
            scores = scores.reshape(group, BLK, slash_count * BLK) + bias[tile][None]
            fold(at, scores.reshape(rows, slash_count * BLK), slash[tile, :, depth:])

    def wait(n, carry):
        pltpu.make_async_copy(sources[0].at[pl.ds(0, BLK)], keys.at[pl.ds(0, BLK)], sem).wait()
        return carry

    lax.fori_loop(0, end - begin, wait, 0)

    def step(c, carry):
        part = pl.ds(pl.multiple_of(c * (CHUNK * BLK), CHUNK * BLK), CHUNK * BLK)
        for at in tiles:
            fold(at, products(at, keys[part, :depth]), keys[part, depth:])
        return carry

    lax.fori_loop(0, (end - begin) // CHUNK, step, 0)

    if last:
        piece_rows = out.shape[2]
        per_block = BLK // piece_rows
        for tile, at in enumerate(tiles):
            slot = upper if tile < blocks else 1 - upper
            result = (acc[at, :] / total[at, :]).astype(out.dtype)
            for j in range(group):
                for h in range(per_block):
                    out[tile % blocks * per_block + h, slot, :, j * depth : (j + 1) * depth] = result[
                        j * BLK + h * piece_rows : j * BLK + (h + 1) * piece_rows
                    ]


def attend(owners, cap, width, scalars, q_near, q_far, pieces, known, state, out_shape):
    verticals, offsets = scalars
    tokens, columns = q_near.shape
    row_width = next(iter(pieces.values())).shape[1]
    depth = row_width // 2
    group = columns // depth
    rows = 2 * tokens * group
    first, last = state is None, out_shape is not None
    held = jax.ShapeDtypeStruct((rows, depth), jnp.float32)
    buffers = [pltpu.VMEM((rows, depth), jnp.float32)] * 3 if last else []
    scratch = buffers + [
        pltpu.VMEM((rows, depth), q_near.dtype),
        pltpu.VMEM((NV * BLK, row_width), q_near.dtype),
        pltpu.SMEM((owners,), jnp.int32),
        pltpu.SemaphoreType.DMA,
    ]
    if last:
        keys = offsets.shape[1] * BLK
        scratch += [
            pltpu.VMEM((owners * tokens, row_width), q_near.dtype),
            pltpu.VMEM((2 * tokens // BLK, keys, row_width), q_near.dtype),
            pltpu.VMEM((2 * tokens // BLK, BLK, keys), jnp.float32),
            pltpu.SemaphoreType.DMA,
        ]
    vmem = pl.BlockSpec(memory_space=pltpu.VMEM)
    share = (len(pieces) - known) * NV // owners * BLK + (NV * BLK // 8 if last else 0)
    return pl.pallas_call(
        functools.partial(
            attend_kernel, owners, cap, group, depth, width, tuple(pieces), known, first, last
        ),
        out_shape=out_shape if last else (held,) * 3,
        grid_spec=pltpu.PrefetchScalarGridSpec(
            num_scalar_prefetch=2,
            grid=(1,),
            in_specs=[vmem] * 2
            + [pl.BlockSpec(memory_space=pl.ANY)] * len(pieces)
            + ([] if first else [vmem] * 3),
            out_specs=vmem if last else [vmem] * 3,
            scratch_shapes=scratch,
        ),
        compiler_params=pltpu.CompilerParams(vmem_limit_bytes=40 * 1024 * 1024),
        cost_estimate=pl.CostEstimate(
            flops=4 * rows * depth * share, bytes_accessed=share * row_width * 2, transcendentals=rows * share
        ),
        name="attend_first" if first else "attend_last" if last else "attend_next",
    )(verticals, offsets, q_near, q_far, *pieces.values(), *(() if first else state))


def body(queries, span_kv, cache_kv, verticals, offsets):
    tokens = queries.shape[0]
    heads_kv, row_width = span_kv.shape[1:]
    depth = row_width // 2
    columns = queries.shape[1] // heads_kv
    group = columns // depth
    owners = lax.axis_size("ctx")
    head_groups = lax.axis_size("head")
    half = owners // 2
    cache_rows = cache_kv.shape[0]
    cache_blocks = cache_rows // BLK
    cap = max(2, 2 * NV // owners)
    me = lax.axis_index("ctx")
    upper = me // half

    across = [(i, (i + half) % owners) for i in range(owners)]
    send_q = lax.dynamic_slice_in_dim(queries, (1 - upper) * columns, columns, 1)
    q_near = lax.dynamic_slice_in_dim(queries, upper * columns, columns, 1)
    rows = cap * BLK + tokens
    payload = jax.ShapeDtypeStruct((rows, row_width), queries.dtype)
    q_far = lax.ppermute(send_q, "ctx", across)
    mine, theirs = pl.pallas_call(
        functools.partial(collect_kernel, owners, cap),
        out_shape=(payload, payload),
        grid_spec=pltpu.PrefetchScalarGridSpec(
            num_scalar_prefetch=1,
            grid=(1,),
            in_specs=[pl.BlockSpec(memory_space=pl.ANY), pl.BlockSpec(memory_space=pltpu.VMEM)],
            out_specs=[pl.BlockSpec(memory_space=pltpu.VMEM)] * 2,
            scratch_shapes=[
                pltpu.VMEM((2, cap, BLK, heads_kv, row_width), queries.dtype),
                pltpu.SemaphoreType.DMA((2, cap)),
            ],
        ),
        compiler_params=pltpu.CompilerParams(vmem_limit_bytes=60 * 1024 * 1024),
        name="collect_slots",
    )(verticals, cache_kv, span_kv)
    crossed = lax.ppermute(theirs, "ctx", across)
    def swap(x, bit):
        return lax.ppermute(x, "ctx", [(i, i ^ bit) for i in range(owners)])

    near, far = {0: mine}, {0: crossed}
    bits = []
    bit = half // 2
    while bit:
        bits.append(bit)
        bit //= 2
    for pieces in (near, far):
        for bit in bits:
            if pieces is near and bit == bits[-1]:
                pieces[bit] = swap(mine, bit)
                kept = [m for m in pieces if m not in (0, bit)]
                *values, pieces[bit], q_far = lax.optimization_barrier(
                    (*[pieces[m] for m in kept], pieces[bit], q_far)
                )
                pieces.update(zip(kept, values))
                pieces.update({m | bit: swap(pieces[m], bit) for m in kept})
            else:
                pieces.update({m | bit: swap(piece, bit) for m, piece in pieces.items()})

    piece = tokens // head_groups
    stage = functools.partial(attend, owners, cap, cache_blocks, (verticals, offsets), q_near, q_far)
    arrived = {(False, m): near[m] for m in near}
    state = stage(arrived, 0, None, None)
    known = len(arrived)
    arrived.update({(True, m): far[m] for m in list(far)[:-1]})
    state = stage(arrived, known, state, None)
    known = len(arrived)
    arrived.update({(True, m): far[m] for m in list(far)[-1:]})
    attended = stage(
        arrived, known, state, jax.ShapeDtypeStruct((head_groups, 2, piece, columns), queries.dtype)
    )
    attended = attended.reshape(head_groups * 2 * piece, columns)
    groups = [
        [(a * half + i) * head_groups + h for h in range(head_groups) for a in range(2)] for i in range(half)
    ]
    return lax.all_to_all(
        attended, ("ctx", "head"), split_axis=0, concat_axis=1, axis_index_groups=groups, tiled=True
    )


def solution(mesh):
    in_specs = (
        P("ctx", "head"),
        P("ctx", "head", None),
        P("ctx", "head", None),
        P("head", None),
        P("head", None),
    )
    out_specs = P(("ctx", "head"), None)
    return jax.shard_map(body, mesh=mesh, in_specs=in_specs, out_specs=out_specs, check_vma=False)
```

```python
import functools

import jax
import jax.numpy as jnp
from jax import lax
from jax.experimental import pallas as pl
from jax.experimental.pallas import tpu as pltpu
from jax.sharding import PartitionSpec as P

BLK = 64
NV = 64
MASKED = -1e30
CHUNK = 8
LOG2E = 1.4426950408889634


def collect_kernel(owners, cap, partners, verticals, cache, span, target, raw, sem):
    me = lax.axis_index("ctx")
    upper = me // (owners // 2)
    head = 1 - upper if partners else upper
    cache_blocks = cache.shape[0] // BLK
    first = me * cache_blocks

    def block_copy(block, slot):
        return pltpu.make_async_copy(
            cache.at[pl.ds(pl.multiple_of(block * BLK, BLK), BLK)], raw.at[slot], sem.at[slot]
        )

    def visit(n, count):
        block = verticals[head, n] - first
        hit = (block >= 0) & (block < cache_blocks) & (count < cap)

        @pl.when(hit)
        def _():
            block_copy(block, count).start()

        return count + hit.astype(jnp.int32)

    found = lax.fori_loop(0, NV, visit, jnp.int32(0))
    for static_head in range(2):

        @pl.when(head == static_head)
        def _():
            target[cap * BLK :, :] = span[:, static_head, :]

            def unpack(slot, carry):
                block_copy(0, slot).wait()
                target[pl.ds(pl.multiple_of(slot * BLK, BLK), BLK), :] = raw[slot, :, static_head, :]
                return carry

            lax.fori_loop(0, found, unpack, 0)


def attend_kernel(owners, cap, group, depth, width, pieces, known, first, last, verticals, offsets, q_near, q_far, *refs):
    refs = list(refs)
    sources = [refs.pop(0) for _ in pieces]
    before = None if first else [refs.pop(0) for _ in range(3)]
    out = refs.pop(0) if last else None
    top, total, acc = refs[:3]
    queries, keys, counts, sem = refs[3:7]
    me = lax.axis_index("ctx")
    half = owners // 2
    upper = me // half
    head = upper
    tokens = q_near.shape[0]
    blocks = tokens // BLK
    rows = group * BLK
    factor = LOG2E * depth**-0.5

    def clear(n, carry):
        counts[n] = 0
        return carry

    lax.fori_loop(0, owners, clear, 0)

    def tally(n, carry):
        owner = verticals[head, n] // width
        counts[owner] = counts[owner] + 1
        return carry

    lax.fori_loop(0, NV, tally, 0)

    def owner_of(far, m):
        return ((1 - upper) if far else upper) * half + ((me % half) ^ m)

    def live(piece):
        return jnp.minimum(counts[owner_of(*piece)], cap)

    seen = jnp.int32(0)
    for piece in pieces[:known]:
        seen = seen + live(piece)
    present = seen
    for piece in pieces[known:]:
        present = present + live(piece)
    begin = seen // CHUNK * CHUNK
    end = jnp.int32(NV) if last else present // CHUNK * CHUNK
    place = jnp.int32(0)
    for piece, source in zip(pieces, sources):
        held = live(piece)

        def fetch(n, carry, place=place, source=source):
            pltpu.make_async_copy(
                source.at[pl.ds(pl.multiple_of(n * BLK, BLK), BLK)],
                keys.at[pl.ds(pl.multiple_of((place + n - begin) * BLK, BLK), BLK)],
                sem,
            ).start()
            return carry

        lax.fori_loop(jnp.clip(begin - place, 0, held), jnp.clip(end - place, 0, held), fetch, 0)
        place = place + held

    if last:
        span, slash, bias, span_sem = refs[7:]
        for piece, source in zip(pieces, sources):
            pltpu.make_async_copy(
                source.at[pl.ds(cap * BLK, tokens)],
                span.at[pl.ds(pl.multiple_of(owner_of(*piece) * tokens, BLK), tokens)],
                span_sem,
            ).start()
    for tile in range(2 * blocks):
        q_ref, block = (q_near, tile) if tile < blocks else (q_far, tile - blocks)
        for j in range(group):
            queries[tile * rows + j * BLK : tile * rows + (j + 1) * BLK, :] = q_ref[
                block * BLK : (block + 1) * BLK, j * depth : (j + 1) * depth
            ]
    if first:
        top[...] = jnp.full(top.shape, MASKED, jnp.float32)
        total[...] = jnp.zeros(total.shape, jnp.float32)
        acc[...] = jnp.zeros(acc.shape, jnp.float32)
    else:
        top[...] = before[0][...]
        total[...] = before[1][...]
        acc[...] = before[2][...]

    def fold(at, scores, values):
        lanes = top.shape[1]
        repeat = scores.shape[1] // lanes
        old = top[at, :]
        new = jnp.maximum(old, jnp.max(scores, axis=1, keepdims=True))
        weights = jnp.exp2((scores - jnp.concatenate([new] * repeat, 1)) * factor)
        keep = jnp.exp2((old - new) * factor)
        top[at, :] = new
        total[at, :] = total[at, :] * keep + jnp.sum(weights, axis=1, keepdims=True)
        acc[at, :] = acc[at, :] * keep + jnp.dot(
            weights.astype(jnp.bfloat16), values, preferred_element_type=jnp.float32
        )

    def products(at, rows_k):
        return lax.dot_general(
            queries[at, :], rows_k, (((1,), (1,)), ((), ())), preferred_element_type=jnp.float32
        )

    tiles = [slice(tile * rows, (tile + 1) * rows) for tile in range(2 * blocks)]
    if last:
        pltpu.make_async_copy(span, span, span_sem).wait()
        slash_count = offsets.shape[1]
        q_at = lax.broadcasted_iota(jnp.int32, (BLK, BLK), 0)
        k_at = lax.broadcasted_iota(jnp.int32, (BLK, BLK), 1)
        behind = k_at <= q_at
        for tile, at in enumerate(tiles):
            index = me if tile < blocks else (me + half) % owners
            position = index * blocks + tile % blocks
            for s in range(slash_count):
                offset = offsets[head, s]
                source_block = position - offset
                start = pl.multiple_of(jnp.maximum(source_block, 0) * BLK, BLK)
                slash[tile, s * BLK : (s + 1) * BLK, :] = span[pl.ds(start, BLK), :]
                allowed = (source_block >= 0) & ((offset > 0) | behind)
                bias[tile, :, s * BLK : (s + 1) * BLK] = jnp.where(allowed, 0.0, MASKED)
            scores = products(at, slash[tile, :, :depth])
            scores = scores.reshape(group, BLK, slash_count * BLK) + bias[tile][None]
            fold(at, scores.reshape(rows, slash_count * BLK), slash[tile, :, depth:])

    def wait(n, carry):
        pltpu.make_async_copy(sources[0].at[pl.ds(0, BLK)], keys.at[pl.ds(0, BLK)], sem).wait()
        return carry

    lax.fori_loop(0, end - begin, wait, 0)

    def step(c, carry):
        part = pl.ds(pl.multiple_of(c * (CHUNK * BLK), CHUNK * BLK), CHUNK * BLK)
        scores = products(tiles[0], keys[part, :depth])
        for at, following in zip(tiles, tiles[1:] + [None]):
            ahead = products(following, keys[part, :depth]) if following else None
            fold(at, scores, keys[part, depth:])
            scores = ahead
        return carry

    lax.fori_loop(0, (end - begin) // CHUNK, step, 0)

    if last:
        piece_rows = out.shape[2]
        per_block = BLK // piece_rows
        for tile, at in enumerate(tiles):
            slot = upper if tile < blocks else 1 - upper
            result = (acc[at, :] / total[at, :]).astype(out.dtype)
            for j in range(group):
                for h in range(per_block):
                    out[tile % blocks * per_block + h, slot, :, j * depth : (j + 1) * depth] = result[
                        j * BLK + h * piece_rows : j * BLK + (h + 1) * piece_rows
                    ]


def attend(owners, cap, width, scalars, q_near, q_far, pieces, known, state, out_shape):
    verticals, offsets = scalars
    tokens, columns = q_near.shape
    row_width = next(iter(pieces.values())).shape[1]
    depth = row_width // 2
    group = columns // depth
    rows = 2 * tokens * group
    first, last = state is None, out_shape is not None
    held = jax.ShapeDtypeStruct((rows, depth), jnp.float32)
    buffers = [pltpu.VMEM((rows, depth), jnp.float32)] * 3 if last else []
    scratch = buffers + [
        pltpu.VMEM((rows, depth), q_near.dtype),
        pltpu.VMEM((NV * BLK, row_width), q_near.dtype),
        pltpu.SMEM((owners,), jnp.int32),
        pltpu.SemaphoreType.DMA,
    ]
    if last:
        keys = offsets.shape[1] * BLK
        scratch += [
            pltpu.VMEM((owners * tokens, row_width), q_near.dtype),
            pltpu.VMEM((2 * tokens // BLK, keys, row_width), q_near.dtype),
            pltpu.VMEM((2 * tokens // BLK, BLK, keys), jnp.float32),
            pltpu.SemaphoreType.DMA,
        ]
    vmem = pl.BlockSpec(memory_space=pltpu.VMEM)
    share = (len(pieces) - known) * NV // owners * BLK + (NV * BLK // 8 if last else 0)
    return pl.pallas_call(
        functools.partial(
            attend_kernel, owners, cap, group, depth, width, tuple(pieces), known, first, last
        ),
        out_shape=out_shape if last else (held,) * 3,
        grid_spec=pltpu.PrefetchScalarGridSpec(
            num_scalar_prefetch=2,
            grid=(1,),
            in_specs=[vmem] * 2
            + [pl.BlockSpec(memory_space=pl.ANY)] * len(pieces)
            + ([] if first else [vmem] * 3),
            out_specs=vmem if last else [vmem] * 3,
            scratch_shapes=scratch,
        ),
        compiler_params=pltpu.CompilerParams(vmem_limit_bytes=40 * 1024 * 1024),
        cost_estimate=pl.CostEstimate(
            flops=4 * rows * depth * share, bytes_accessed=share * row_width * 2, transcendentals=rows * share
        ),
        name="attend_first" if first else "attend_last" if last else "attend_next",
    )(verticals, offsets, q_near, q_far, *pieces.values(), *(() if first else state))


def body(queries, span_kv, cache_kv, verticals, offsets):
    tokens = queries.shape[0]
    heads_kv, row_width = span_kv.shape[1:]
    depth = row_width // 2
    columns = queries.shape[1] // heads_kv
    group = columns // depth
    owners = lax.axis_size("ctx")
    head_groups = lax.axis_size("head")
    half = owners // 2
    cache_rows = cache_kv.shape[0]
    cache_blocks = cache_rows // BLK
    cap = max(2, 2 * NV // owners)
    me = lax.axis_index("ctx")
    upper = me // half

    across = [(i, (i + half) % owners) for i in range(owners)]
    send_q = lax.dynamic_slice_in_dim(queries, (1 - upper) * columns, columns, 1)
    q_near = lax.dynamic_slice_in_dim(queries, upper * columns, columns, 1)
    rows = cap * BLK + tokens
    payload = jax.ShapeDtypeStruct((rows, row_width), queries.dtype)
    q_far = lax.ppermute(send_q, "ctx", across)

    def collect(partners, verticals):
        return pl.pallas_call(
            functools.partial(collect_kernel, owners, cap, partners),
            out_shape=payload,
            grid_spec=pltpu.PrefetchScalarGridSpec(
                num_scalar_prefetch=1,
                grid=(1,),
                in_specs=[pl.BlockSpec(memory_space=pl.ANY), pl.BlockSpec(memory_space=pltpu.VMEM)],
                out_specs=pl.BlockSpec(memory_space=pltpu.VMEM),
                scratch_shapes=[
                    pltpu.VMEM((cap, BLK, heads_kv, row_width), queries.dtype),
                    pltpu.SemaphoreType.DMA((cap,)),
                ],
            ),
            compiler_params=pltpu.CompilerParams(vmem_limit_bytes=60 * 1024 * 1024),
            cost_estimate=pl.CostEstimate(
                flops=0, bytes_accessed=2 * cap * BLK * heads_kv * row_width, transcendentals=0
            ),
            name="collect_partners" if partners else "collect_own",
        )(verticals, cache_kv, span_kv)

    theirs = collect(True, verticals)
    theirs, later = lax.optimization_barrier((theirs, verticals))
    crossed = lax.ppermute(theirs, "ctx", across)
    def swap(x, bit):
        return lax.ppermute(x, "ctx", [(i, i ^ bit) for i in range(owners)])

    mine = collect(False, later)
    near, far = {0: mine}, {0: crossed}
    bits = []
    bit = half // 2
    while bit:
        bits.append(bit)
        bit //= 2
    for bit in bits[:-1]:
        near.update({m | bit: swap(piece, bit) for m, piece in near.items()})
    bit = bits[-1]
    kept = [m for m in near if m]
    *values, own = lax.optimization_barrier((*[near[m] for m in kept], swap(mine, bit)))
    near.update(zip(kept, values))
    near.update({m | bit: swap(near[m], bit) for m in kept})
    near[bit] = own
    for other in bits[:-1]:
        far.update({m | other: swap(piece, other) for m, piece in far.items()})
    last_near = near[bits[0] | bit]
    crossed, near[bits[0] | bit] = lax.optimization_barrier((crossed, last_near))
    far[bit] = swap(crossed, bit)
    kept = [m for m in far if m not in (0, bit)]
    *values, q_far = lax.optimization_barrier((*[far[m] for m in kept], q_far))
    far.update(zip(kept, values))
    far.update({m | bit: swap(far[m], bit) for m in kept})

    piece = tokens // head_groups
    stage = functools.partial(attend, owners, cap, cache_blocks, (verticals, offsets), q_near, q_far)
    arrived = {(False, m): near[m] for m in near}
    state = stage(arrived, 0, None, None)
    known = len(arrived)
    arrived.update({(True, m): far[m] for m in list(far)[:-1]})
    state = stage(arrived, known, state, None)
    known = len(arrived)
    arrived.update({(True, m): far[m] for m in list(far)[-1:]})
    attended = stage(
        arrived, known, state, jax.ShapeDtypeStruct((head_groups, 2, piece, columns), queries.dtype)
    )
    attended = attended.reshape(head_groups * 2 * piece, columns)
    groups = [
        [(a * half + i) * head_groups + h for h in range(head_groups) for a in range(2)] for i in range(half)
    ]
    return lax.all_to_all(
        attended, ("ctx", "head"), split_axis=0, concat_axis=1, axis_index_groups=groups, tiled=True
    )


def solution(mesh):
    in_specs = (
        P("ctx", "head"),
        P("ctx", "head", None),
        P("ctx", "head", None),
        P("head", None),
        P("head", None),
    )
    out_specs = P(("ctx", "head"), None)
    return jax.shard_map(body, mesh=mesh, in_specs=in_specs, out_specs=out_specs, check_vma=False)
```

```python
import functools

import jax
import jax.numpy as jnp
from jax import lax
from jax.experimental import pallas as pl
from jax.experimental.pallas import tpu as pltpu
from jax.sharding import PartitionSpec as P

BLK = 64
NV = 64
MASKED = -1e30
CHUNK = 8
LOG2E = 1.4426950408889634


def collect_kernel(owners, cap, verticals, cache, span, mine, theirs, their_span, raw, sem):
    me = lax.axis_index("ctx")
    upper = me // (owners // 2)
    cache_blocks = cache.shape[0] // BLK
    first = me * cache_blocks

    def block_copy(block, place, slot):
        return pltpu.make_async_copy(
            cache.at[pl.ds(pl.multiple_of(block * BLK, BLK), BLK)], raw.at[place, slot], sem.at[place, slot]
        )

    found = []
    for place in range(2):
        head = upper if place == 0 else 1 - upper

        def visit(n, count):
            block = verticals[head, n] - first
            hit = (block >= 0) & (block < cache_blocks) & (count < cap)

            @pl.when(hit)
            def _():
                block_copy(block, place, count).start()

            return count + hit.astype(jnp.int32)

        found.append(lax.fori_loop(0, NV, visit, jnp.int32(0)))
    for own in range(2):

        @pl.when(upper == own)
        def _():
            mine[cap * BLK :, :] = span[:, own, :]
            their_span[...] = span[:, 1 - own, :]
            for place, target in ((0, mine), (1, theirs)):
                head = own if place == 0 else 1 - own

                def unpack(slot, carry):
                    block_copy(0, place, slot).wait()
                    target[pl.ds(pl.multiple_of(slot * BLK, BLK), BLK), :] = raw[place, slot, :, head, :]
                    return carry

                lax.fori_loop(0, found[place], unpack, 0)


def attend_kernel(
    owners, cap, group, depth, width, pieces, known, spans, first, last, verticals, offsets, q_near, q_far, *refs
):
    refs = list(refs)
    sources = [refs.pop(0) for _ in pieces]
    span_sources = [refs.pop(0) for _ in spans]
    before = None if first else [refs.pop(0) for _ in range(2)]
    out = refs.pop(0) if last else None
    top, acc = refs[:2]
    queries, keys, counts, sem = refs[2:6]
    me = lax.axis_index("ctx")
    half = owners // 2
    upper = me // half
    head = upper
    tokens = q_near.shape[0]
    blocks = tokens // BLK
    rows = group * BLK
    width_kv = 2 * depth
    factor = LOG2E * depth**-0.5

    def clear(n, carry):
        counts[n] = 0
        return carry

    lax.fori_loop(0, owners, clear, 0)

    def tally(n, carry):
        owner = verticals[head, n] // width
        counts[owner] = counts[owner] + 1
        return carry

    lax.fori_loop(0, NV, tally, 0)

    def owner_of(far, m):
        return ((1 - upper) if far else upper) * half + ((me % half) ^ m)

    def live(piece):
        return jnp.minimum(counts[owner_of(*piece)], cap)

    seen = jnp.int32(0)
    for piece in pieces[:known]:
        seen = seen + live(piece)
    present = seen
    for piece in pieces[known:]:
        present = present + live(piece)
    begin = seen // CHUNK * CHUNK
    end = jnp.int32(NV) if last else present // CHUNK * CHUNK
    place = jnp.int32(0)
    for piece, source in zip(pieces, sources):
        held = live(piece)

        def fetch(n, carry, place=place, source=source):
            pltpu.make_async_copy(
                source.at[pl.ds(pl.multiple_of(n * BLK, BLK), BLK)],
                keys.at[pl.ds(pl.multiple_of((place + n - begin) * BLK, BLK), BLK), pl.ds(0, width_kv)],
                sem,
            ).start()
            return carry

        lax.fori_loop(jnp.clip(begin - place, 0, held), jnp.clip(end - place, 0, held), fetch, 0)
        place = place + held

    if spans:
        span, slash, bias, span_sem = refs[6:]
        for (far, m, start), source in zip(spans, span_sources):
            pltpu.make_async_copy(
                source.at[pl.ds(start, tokens)],
                span.at[pl.ds(pl.multiple_of(owner_of(far, m) * tokens, BLK), tokens)],
                span_sem,
            ).start()
    keys[:, width_kv:] = jnp.ones((keys.shape[0], depth), keys.dtype)
    for tile in range(2 * blocks):
        q_ref, block = (q_near, tile) if tile < blocks else (q_far, tile - blocks)
        for j in range(group):
            queries[tile * rows + j * BLK : tile * rows + (j + 1) * BLK, :] = q_ref[
                block * BLK : (block + 1) * BLK, j * depth : (j + 1) * depth
            ]
    if first:
        top[...] = jnp.full(top.shape, MASKED, jnp.float32)
        acc[...] = jnp.zeros(acc.shape, jnp.float32)
    else:
        top[...] = before[0][...]
        acc[...] = before[1][...]

    def fold(at, scores, values):
        old = top[at, :]
        new = jnp.maximum(old, jnp.max(scores, axis=1, keepdims=True))
        wide = jnp.concatenate([new] * (scores.shape[1] // depth), 1)
        weights = jnp.exp2((scores - wide) * factor).astype(jnp.bfloat16)
        keep = jnp.exp2((old - new) * factor)
        top[at, :] = new
        acc[at, :] = acc[at, :] * jnp.concatenate([keep, keep], 1) + jnp.dot(
            weights, values, preferred_element_type=jnp.float32
        )

    def products(at, rows_k):
        return lax.dot_general(
            queries[at, :], rows_k, (((1,), (1,)), ((), ())), preferred_element_type=jnp.float32
        )

    tiles = [slice(tile * rows, (tile + 1) * rows) for tile in range(2 * blocks)]
    if spans:
        pltpu.make_async_copy(span, span, span_sem).wait()
        slash_count = offsets.shape[1]
        q_at = lax.broadcasted_iota(jnp.int32, (BLK, BLK), 0)
        k_at = lax.broadcasted_iota(jnp.int32, (BLK, BLK), 1)
        behind = k_at <= q_at
        slash[:, :, width_kv:] = jnp.ones((2 * blocks, slash_count * BLK, depth), slash.dtype)
        for tile, at in enumerate(tiles):
            index = me if tile < blocks else (me + half) % owners
            position = index * blocks + tile % blocks
            for s in range(slash_count):
                offset = offsets[head, s]
                source_block = position - offset
                start = pl.multiple_of(jnp.maximum(source_block, 0) * BLK, BLK)
                slash[tile, s * BLK : (s + 1) * BLK, :width_kv] = span[pl.ds(start, BLK), :]
                allowed = (source_block >= 0) & ((offset > 0) | behind)
                bias[tile, :, s * BLK : (s + 1) * BLK] = jnp.where(allowed, 0.0, MASKED)
            scores = products(at, slash[tile, :, :depth])
            scores = scores.reshape(group, BLK, slash_count * BLK) + bias[tile][None]
            fold(at, scores.reshape(rows, slash_count * BLK), slash[tile, :, depth:])

    def wait(n, carry):
        pltpu.make_async_copy(
            sources[0].at[pl.ds(0, BLK)], keys.at[pl.ds(0, BLK), pl.ds(0, width_kv)], sem
        ).wait()
        return carry

    lax.fori_loop(0, end - begin, wait, 0)

    def step(c, carry):
        part = pl.ds(pl.multiple_of(c * (CHUNK * BLK), CHUNK * BLK), CHUNK * BLK)
        scores = products(tiles[0], keys[part, :depth])
        for at, following in zip(tiles, tiles[1:] + [None]):
            ahead = products(following, keys[part, :depth]) if following else None
            fold(at, scores, keys[part, depth:])
            scores = ahead
        return carry

    lax.fori_loop(0, (end - begin) // CHUNK, step, 0)

    if last:
        piece_rows = out.shape[2]
        per_block = BLK // piece_rows
        for tile, at in enumerate(tiles):
            slot = upper if tile < blocks else 1 - upper
            result = (acc[at, :depth] / acc[at, depth:]).astype(out.dtype)
            for j in range(group):
                for h in range(per_block):
                    out[tile % blocks * per_block + h, slot, :, j * depth : (j + 1) * depth] = result[
                        j * BLK + h * piece_rows : j * BLK + (h + 1) * piece_rows
                    ]


def attend(owners, cap, width, scalars, q_near, q_far, pieces, known, state, spans=None, out_shape=None, name=None):
    verticals, offsets = scalars
    tokens, columns = q_near.shape
    row_width = next(iter(pieces.values())).shape[1]
    depth = row_width // 2
    group = columns // depth
    rows = 2 * tokens * group
    first, last = state is None, out_shape is not None
    held = (jax.ShapeDtypeStruct((rows, depth), jnp.float32), jax.ShapeDtypeStruct((rows, 2 * depth), jnp.float32))
    scratch = [pltpu.VMEM(h.shape, h.dtype) for h in held] if last else []
    scratch += [
        pltpu.VMEM((rows, depth), q_near.dtype),
        pltpu.VMEM((NV * BLK, 3 * depth), q_near.dtype),
        pltpu.SMEM((owners,), jnp.int32),
        pltpu.SemaphoreType.DMA,
    ]
    span_places, span_values = [], []
    if spans:
        keys = offsets.shape[1] * BLK
        scratch += [
            pltpu.VMEM((owners * tokens, row_width), q_near.dtype),
            pltpu.VMEM((2 * tokens // BLK, keys, 3 * depth), q_near.dtype),
            pltpu.VMEM((2 * tokens // BLK, BLK, keys), jnp.float32),
            pltpu.SemaphoreType.DMA,
        ]
        for (far, m), value in spans.items():
            span_places.append((far, m, value.shape[0] - tokens))
            span_values.append(value)
    vmem = pl.BlockSpec(memory_space=pltpu.VMEM)
    share = (len(pieces) - known) * NV // owners * BLK + (offsets.shape[1] * BLK if spans else 0)
    return pl.pallas_call(
        functools.partial(
            attend_kernel, owners, cap, group, depth, width, tuple(pieces), known, tuple(span_places), first, last
        ),
        out_shape=out_shape if last else held,
        grid_spec=pltpu.PrefetchScalarGridSpec(
            num_scalar_prefetch=2,
            grid=(1,),
            in_specs=[vmem] * 2
            + [pl.BlockSpec(memory_space=pl.ANY)] * (len(pieces) + len(span_values))
            + ([] if first else [vmem] * 2),
            out_specs=vmem if last else [vmem] * 2,
            scratch_shapes=scratch,
        ),
        compiler_params=pltpu.CompilerParams(vmem_limit_bytes=40 * 1024 * 1024),
        cost_estimate=pl.CostEstimate(
            flops=1 * rows * depth * share // 2, bytes_accessed=share * row_width * 2, transcendentals=0
        ),
        name=name,
    )(verticals, offsets, q_near, q_far, *pieces.values(), *span_values, *(() if first else state))


def body(queries, span_kv, cache_kv, verticals, offsets):
    tokens = queries.shape[0]
    heads_kv, row_width = span_kv.shape[1:]
    depth = row_width // 2
    columns = queries.shape[1] // heads_kv
    group = columns // depth
    owners = lax.axis_size("ctx")
    head_groups = lax.axis_size("head")
    half = owners // 2
    cache_rows = cache_kv.shape[0]
    cache_blocks = cache_rows // BLK
    cap = max(2, 2 * NV // owners)
    me = lax.axis_index("ctx")
    upper = me // half

    across = [(i, (i + half) % owners) for i in range(owners)]
    send_q = lax.dynamic_slice_in_dim(queries, (1 - upper) * columns, columns, 1)
    q_near = lax.dynamic_slice_in_dim(queries, upper * columns, columns, 1)
    q_far = lax.ppermute(send_q, "ctx", across)

    def rows_of(count):
        return jax.ShapeDtypeStruct((count, row_width), queries.dtype)

    mine, theirs, their_span = pl.pallas_call(
        functools.partial(collect_kernel, owners, cap),
        out_shape=(rows_of(cap * BLK + tokens), rows_of(cap * BLK), rows_of(tokens)),
        grid_spec=pltpu.PrefetchScalarGridSpec(
            num_scalar_prefetch=1,
            grid=(1,),
            in_specs=[pl.BlockSpec(memory_space=pl.ANY), pl.BlockSpec(memory_space=pltpu.VMEM)],
            out_specs=[pl.BlockSpec(memory_space=pltpu.VMEM)] * 3,
            scratch_shapes=[
                pltpu.VMEM((2, cap, BLK, heads_kv, row_width), queries.dtype),
                pltpu.SemaphoreType.DMA((2, cap)),
            ],
        ),
        compiler_params=pltpu.CompilerParams(vmem_limit_bytes=60 * 1024 * 1024),
        cost_estimate=pl.CostEstimate(
            flops=0, bytes_accessed=4 * cap * BLK * heads_kv * row_width, transcendentals=0
        ),
        name="collect_slots",
    )(verticals, cache_kv, span_kv)

    def swap(x, bit):
        return lax.ppermute(x, "ctx", [(i, i ^ bit) for i in range(owners)])

    bits = []
    bit = half // 2
    while bit:
        bits.append(bit)
        bit //= 2
    far_spans = {0: lax.ppermute(their_span, "ctx", across)}
    theirs, q_far = lax.optimization_barrier((theirs, q_far))
    crossed = lax.ppermute(theirs, "ctx", across)
    near, far = {0: mine}, {0: crossed}
    for bit in bits[:-1]:
        near.update({m | bit: swap(piece, bit) for m, piece in near.items()})
    bit = bits[-1]
    kept = [m for m in near if m]
    *values, own, far_spans[0] = lax.optimization_barrier(
        (*[near[m] for m in kept], swap(mine, bit), far_spans[0])
    )
    near.update(zip(kept, values))
    forwarded = {m | bit: swap(near[m], bit) for m in kept}
    near[bit] = own
    for other in bits:
        far_spans.update({m | other: swap(x, other) for m, x in far_spans.items()})
    for other in bits[:-1]:
        far.update({m | other: swap(piece, other) for m, piece in far.items()})
    crossed, forwarded, far_spans = lax.optimization_barrier((crossed, forwarded, far_spans))
    far[bit] = swap(crossed, bit)
    piece = tokens // head_groups
    stage = functools.partial(attend, owners, cap, cache_blocks, (verticals, offsets), q_near, q_far)
    arrived = {(False, m): x for m, x in near.items()}
    state = stage(arrived, 0, None, name="attend_near")
    spans = {(False, m): x for m, x in (near | forwarded).items()}
    spans.update({(True, m): x for m, x in far_spans.items()})
    known = len(arrived)
    arrived.update({(False, m): x for m, x in forwarded.items()})
    state = stage(arrived, known, state, spans, name="attend_span")
    kept = {m: far[m] for m in far if m not in (0, bit)}
    kept, state = lax.optimization_barrier((kept, state))
    last_far = {m | bit: swap(x, bit) for m, x in kept.items()}
    known = len(arrived)
    arrived.update({(True, m): x for m, x in far.items()})
    state = stage(arrived, known, state, name="attend_far")
    known = len(arrived)
    arrived.update({(True, m): x for m, x in last_far.items()})
    attended = stage(
        arrived,
        known,
        state,
        out_shape=jax.ShapeDtypeStruct((head_groups, 2, piece, columns), queries.dtype),
        name="attend_last",
    )
    attended = attended.reshape(head_groups * 2 * piece, columns)
    groups = [
        [(a * half + i) * head_groups + h for h in range(head_groups) for a in range(2)] for i in range(half)
    ]
    return lax.all_to_all(
        attended, ("ctx", "head"), split_axis=0, concat_axis=1, axis_index_groups=groups, tiled=True
    )


def solution(mesh):
    in_specs = (
        P("ctx", "head"),
        P("ctx", "head", None),
        P("ctx", "head", None),
        P("head", None),
        P("head", None),
    )
    out_specs = P(("ctx", "head"), None)
    return jax.shard_map(body, mesh=mesh, in_specs=in_specs, out_specs=out_specs, check_vma=False)
```

```python
import functools

import jax
import jax.numpy as jnp
from jax import lax
from jax.experimental import pallas as pl
from jax.experimental.pallas import tpu as pltpu
from jax.sharding import PartitionSpec as P

BLK = 64
NV = 64
MASKED = -1e30
CHUNK = 8
LOG2E = 1.4426950408889634


def collect_kernel(owners, cap, verticals, cache, span, mine, theirs, raw, sem):
    me = lax.axis_index("ctx")
    upper = me // (owners // 2)
    cache_blocks = cache.shape[0] // BLK
    first = me * cache_blocks

    def block_copy(block, place, slot):
        return pltpu.make_async_copy(
            cache.at[pl.ds(pl.multiple_of(block * BLK, BLK), BLK)], raw.at[place, slot], sem.at[place, slot]
        )

    found = []
    for place in range(2):
        head = upper if place == 0 else 1 - upper

        def visit(n, count):
            block = verticals[head, n] - first
            hit = (block >= 0) & (block < cache_blocks) & (count < cap)

            @pl.when(hit)
            def _():
                block_copy(block, place, count).start()

            return count + hit.astype(jnp.int32)

        found.append(lax.fori_loop(0, NV, visit, jnp.int32(0)))
    for own in range(2):

        @pl.when(upper == own)
        def _():
            for place, target in ((0, mine), (1, theirs)):
                head = own if place == 0 else 1 - own
                target[cap * BLK :, :] = span[:, head, :]

                def unpack(slot, carry):
                    block_copy(0, place, slot).wait()
                    target[pl.ds(pl.multiple_of(slot * BLK, BLK), BLK), :] = raw[place, slot, :, head, :]
                    return carry

                lax.fori_loop(0, found[place], unpack, 0)


class Stage:
    def __init__(self, owners, cap, group, depth, tokens, width, parts, pieces, known, late, first, last):
        self.owners, self.cap, self.group, self.depth = owners, cap, group, depth
        self.tokens, self.width, self.parts = tokens, width, parts
        self.pieces, self.known, self.late = pieces, known, late
        self.first, self.last = first, last
        self.half = owners // 2
        self.blocks = tokens // BLK
        self.rows = group * BLK
        self.state_rows = 2 * self.blocks * self.rows
        self.slash = bool(late) and not last

    def owner(self, far, m):
        me = lax.axis_index("ctx")
        upper = me // self.half
        return ((1 - upper) if far else upper) * self.half + ((me % self.half) ^ m)


def attend_kernel(stage, scalars, offsets, *refs):
    refs = list(refs)

    def take(count):
        taken, refs[:count] = refs[:count], []
        return taken

    half, blocks, rows, depth, cap, tokens = (
        stage.half, stage.blocks, stage.rows, stage.depth, stage.cap, stage.tokens
    )
    me = lax.axis_index("ctx")
    upper = me // half
    head = upper
    width_kv = 2 * depth
    factor = LOG2E * depth**-0.5
    if stage.first:
        q_near, q_far = take(2)
    else:
        (queries,) = take(1)
    sources = take(len(stage.pieces))
    if stage.first:
        top, acc, queries, counts = take(4)
    else:
        take(2)
        top, acc = take(2)
        counts = scalars
    outs = take(stage.parts) if stage.last else []
    keys, sem = take(2)

    if stage.first:

        def clear(n, carry):
            counts[n] = 0
            return carry

        lax.fori_loop(0, stage.owners, clear, 0)

        def tally(n, carry):
            owner = scalars[head, n] // stage.width
            counts[owner] = counts[owner] + 1
            return carry

        lax.fori_loop(0, NV, tally, 0)

    held = [jnp.minimum(counts[stage.owner(*piece)], cap) for piece in stage.pieces]
    seen = sum(held[: stage.known], jnp.int32(0))
    present = sum(held[stage.known :], seen)
    begin = seen // CHUNK * CHUNK
    end = jnp.int32(NV) if stage.last else present // CHUNK * CHUNK
    place = jnp.int32(0)
    for source, live in zip(sources, held):

        def fetch(n, carry, place=place, source=source):
            pltpu.make_async_copy(
                source.at[pl.ds(pl.multiple_of(n * BLK, BLK), BLK)],
                keys.at[pl.ds(pl.multiple_of((place + n - begin) * BLK, BLK), BLK), pl.ds(0, width_kv)],
                sem,
            ).start()
            return carry

        lax.fori_loop(jnp.clip(begin - place, 0, live), jnp.clip(end - place, 0, live), fetch, 0)
        place = place + live

    span_copies = []
    if stage.slash or stage.last:
        span, bias, span_sem = take(3)
        wanted = stage.pieces[stage.known :] if stage.last else stage.pieces
        for n, piece in enumerate(wanted):
            at = n if stage.last else stage.owner(*piece)
            copy = pltpu.make_async_copy(
                sources[stage.pieces.index(piece)].at[pl.ds(cap * BLK, tokens)],
                span.at[pl.ds(pl.multiple_of(at * tokens, BLK), tokens), pl.ds(0, width_kv)],
                span_sem,
            )
            copy.start()
            span_copies.append(copy)
    keys[:, width_kv:] = jnp.ones((keys.shape[0], depth), keys.dtype)
    if stage.first:
        for tile in range(2 * blocks):
            q_ref, block = (q_near, tile) if tile < blocks else (q_far, tile - blocks)
            for j in range(stage.group):
                queries[tile * rows + j * BLK : tile * rows + (j + 1) * BLK, :] = q_ref[
                    block * BLK : (block + 1) * BLK, j * depth : (j + 1) * depth
                ]
        top[...] = jnp.full(top.shape, MASKED, jnp.float32)
        acc[...] = jnp.zeros(acc.shape, jnp.float32)

    def fold(at, scores, values):
        old = top[at, :]
        new = jnp.maximum(old, jnp.max(scores, axis=1, keepdims=True))
        wide = jnp.concatenate([new] * (scores.shape[1] // depth), 1)
        weights = jnp.exp2((scores - wide) * factor).astype(jnp.bfloat16)
        keep = jnp.exp2((old - new) * factor)
        top[at, :] = new
        acc[at, :] = acc[at, :] * jnp.concatenate([keep, keep], 1) + jnp.dot(
            weights, values, preferred_element_type=jnp.float32
        )

    def products(at, rows_k):
        return lax.dot_general(
            queries[at, :], rows_k, (((1,), (1,)), ((), ())), preferred_element_type=jnp.float32
        )

    tiles = [slice(tile * rows, (tile + 1) * rows) for tile in range(2 * blocks)]

    def wait(n, carry):
        pltpu.make_async_copy(
            sources[0].at[pl.ds(0, BLK)], keys.at[pl.ds(0, BLK), pl.ds(0, width_kv)], sem
        ).wait()
        return carry

    lax.fori_loop(0, end - begin, wait, 0)

    def step(c, carry):
        part = pl.ds(pl.multiple_of(c * (CHUNK * BLK), CHUNK * BLK), CHUNK * BLK)
        scores = products(tiles[0], keys[part, :depth])
        for at, following in zip(tiles, tiles[1:] + [None]):
            ahead = products(following, keys[part, :depth]) if following else None
            fold(at, scores, keys[part, depth:])
            scores = ahead
        return carry

    lax.fori_loop(0, (end - begin) // CHUNK, step, 0)

    if span_copies:
        for copy in span_copies:
            copy.wait()
        slash_count = offsets.shape[1]
        q_at = lax.broadcasted_iota(jnp.int32, (BLK, BLK), 0)
        k_at = lax.broadcasted_iota(jnp.int32, (BLK, BLK), 1)
        behind = k_at <= q_at
        late_owners = [stage.owner(*piece) for piece in stage.late]

        def masked(at, tile, rows_k, values):
            scores = products(at, rows_k)
            scores = scores.reshape(stage.group, BLK, rows_k.shape[0]) + bias[tile][None]
            fold(at, scores.reshape(rows, rows_k.shape[0]), values)

        if stage.slash:
            (slash,) = take(1)
            slash[:, :, width_kv:] = jnp.ones((2 * blocks, slash_count * BLK, depth), slash.dtype)
        else:
            span[:, width_kv:] = jnp.ones((span.shape[0], depth), span.dtype)
        for tile, at in enumerate(tiles):
            index = me if tile < blocks else (me + half) % stage.owners
            position = index * blocks + tile % blocks
            if stage.slash:
                for s in range(slash_count):
                    offset = offsets[head, s]
                    block = position - offset
                    here = block >= 0
                    for owner in late_owners:
                        here = here & (block // blocks != owner)
                    start = pl.multiple_of(jnp.where(here, block, position) * BLK, BLK)
                    slash[tile, s * BLK : (s + 1) * BLK, :width_kv] = span[pl.ds(start, BLK), :]
                    allowed = here & ((offset > 0) | behind)
                    bias[tile, :, s * BLK : (s + 1) * BLK] = jnp.where(allowed, 0.0, MASKED)
                masked(at, tile, slash[tile, :, :depth], slash[tile, :, depth:])
            else:
                for n, owner in enumerate(late_owners):
                    for k in range(blocks):
                        distance = position - (owner * blocks + k)
                        chosen = distance == offsets[head, 0]
                        for s in range(1, slash_count):
                            chosen = chosen | (distance == offsets[head, s])
                        allowed = chosen & ((distance > 0) | behind)
                        column = n * tokens + k * BLK
                        bias[tile, :, column : column + BLK] = jnp.where(allowed, 0.0, MASKED)
                masked(at, tile, span[:, :depth], span[:, depth:])

    if stage.last:
        lane = lax.axis_index("head")
        for k, out in enumerate(outs):
            part_rows = out.shape[0]
            token = (lane ^ (k >> 1)) * part_rows
            base = ((k & 1) * blocks + token // BLK) * rows + token % BLK
            for j in range(stage.group):
                at = pl.ds(pl.multiple_of(base + j * BLK, part_rows), part_rows)
                both = acc[at, :]
                out[:, j * depth : (j + 1) * depth] = (both[:, :depth] / both[:, depth:]).astype(out.dtype)


def attend(stage, scalars, offsets, queries, pieces, state, name):
    depth, rows, blocks = stage.depth, stage.state_rows, stage.blocks
    kind = jnp.bfloat16
    held = [jax.ShapeDtypeStruct((rows, depth), jnp.float32), jax.ShapeDtypeStruct((rows, 2 * depth), jnp.float32)]
    vmem, smem = pl.BlockSpec(memory_space=pltpu.VMEM), pl.BlockSpec(memory_space=pltpu.SMEM)
    out_shape, out_specs = list(held), [vmem] * 2
    if stage.first:
        out_shape += [
            jax.ShapeDtypeStruct((rows, depth), kind),
            jax.ShapeDtypeStruct((stage.owners,), jnp.int32),
        ]
        out_specs += [vmem, smem]
    if stage.last:
        part = jax.ShapeDtypeStruct((2 * stage.tokens // stage.parts, stage.group * depth), kind)
        out_shape += [part] * stage.parts
        out_specs += [vmem] * stage.parts
    scratch = [pltpu.VMEM((NV * BLK, 3 * depth), kind), pltpu.SemaphoreType.DMA]
    share = (len(stage.pieces) - stage.known) * NV // stage.owners * BLK
    if stage.slash:
        keys = offsets.shape[1] * BLK
        scratch += [
            pltpu.VMEM((stage.owners * stage.tokens, 2 * depth), kind),
            pltpu.VMEM((2 * blocks, BLK, keys), jnp.float32),
            pltpu.SemaphoreType.DMA,
            pltpu.VMEM((2 * blocks, keys, 3 * depth), kind),
        ]
        share += keys
    elif stage.last:
        keys = len(stage.late) * stage.tokens
        scratch += [
            pltpu.VMEM((keys, 3 * depth), kind),
            pltpu.VMEM((2 * blocks, BLK, keys), jnp.float32),
            pltpu.SemaphoreType.DMA,
        ]
    operands = [scalars, offsets, *queries, *pieces, *state]
    in_specs = [vmem] * len(queries) + [pl.BlockSpec(memory_space=pl.ANY)] * len(pieces) + [vmem] * len(state)
    return pl.pallas_call(
        functools.partial(attend_kernel, stage),
        out_shape=out_shape,
        grid_spec=pltpu.PrefetchScalarGridSpec(
            num_scalar_prefetch=2, grid=(1,), in_specs=in_specs, out_specs=out_specs, scratch_shapes=scratch
        ),
        input_output_aliases={len(operands) - len(state) + n: n for n in range(len(state))},
        compiler_params=pltpu.CompilerParams(vmem_limit_bytes=40 * 1024 * 1024),
        cost_estimate=pl.CostEstimate(
            flops=2 * rows * depth * share, bytes_accessed=share * 4 * depth, transcendentals=0
        ),
        name=name,
    )(*operands)


def place_kernel(head_groups, half, *refs):
    *parts, out, sem = refs
    here = lax.axis_index("head") * 2 + lax.axis_index("ctx") // half
    copies = []
    for k, part in enumerate(parts):
        columns = part.shape[1]
        start = pl.multiple_of((here ^ k) * columns, columns)
        copies.append(pltpu.make_async_copy(part, out.at[:, pl.ds(start, columns)], sem.at[k]))
        copies[-1].start()
    for copy in copies:
        copy.wait()


def body(queries, span_kv, cache_kv, verticals, offsets):
    tokens = queries.shape[0]
    heads_kv, row_width = span_kv.shape[1:]
    depth = row_width // 2
    columns = queries.shape[1] // heads_kv
    group = columns // depth
    owners = lax.axis_size("ctx")
    head_groups = lax.axis_size("head")
    half = owners // 2
    cache_blocks = cache_kv.shape[0] // BLK
    cap = max(2, 2 * NV // owners)
    upper = lax.axis_index("ctx") // half

    across = [(i, (i + half) % owners) for i in range(owners)]
    send_q = lax.dynamic_slice_in_dim(queries, (1 - upper) * columns, columns, 1)
    q_near = lax.dynamic_slice_in_dim(queries, upper * columns, columns, 1)
    q_far = lax.ppermute(send_q, "ctx", across)
    payload = jax.ShapeDtypeStruct((cap * BLK + tokens, row_width), queries.dtype)
    mine, theirs = pl.pallas_call(
        functools.partial(collect_kernel, owners, cap),
        out_shape=(payload, payload),
        grid_spec=pltpu.PrefetchScalarGridSpec(
            num_scalar_prefetch=1,
            grid=(1,),
            in_specs=[pl.BlockSpec(memory_space=pl.ANY), pl.BlockSpec(memory_space=pltpu.VMEM)],
            out_specs=[pl.BlockSpec(memory_space=pltpu.VMEM)] * 2,
            scratch_shapes=[
                pltpu.VMEM((2, cap, BLK, heads_kv, row_width), queries.dtype),
                pltpu.SemaphoreType.DMA((2, cap)),
            ],
        ),
        compiler_params=pltpu.CompilerParams(vmem_limit_bytes=16 * 1024 * 1024),
        cost_estimate=pl.CostEstimate(
            flops=0, bytes_accessed=4 * cap * BLK * heads_kv * row_width, transcendentals=0
        ),
        name="collect_slots",
    )(verticals, cache_kv, span_kv)

    def swap(x, bit):
        return lax.ppermute(x, "ctx", [(i, i ^ bit) for i in range(owners)])

    bits = []
    bit = half // 2
    while bit:
        bits.append(bit)
        bit //= 2
    theirs, q_far = lax.optimization_barrier((theirs, q_far))
    crossed = lax.ppermute(theirs, "ctx", across)
    near, far = {0: mine}, {0: crossed}
    for bit in bits[:-1]:
        near.update({m | bit: swap(piece, bit) for m, piece in near.items()})
    bit = bits[-1]
    kept = {m: x for m, x in near.items() if m}
    kept, own = lax.optimization_barrier((kept, swap(mine, bit)))
    near.update(kept)
    forwarded = {m | bit: swap(x, bit) for m, x in kept.items()}
    near[bit] = own
    for other in bits[:-1]:
        far.update({m | other: swap(x, other) for m, x in far.items()})
    crossed, forwarded = lax.optimization_barrier((crossed, forwarded))
    near.update(forwarded)
    far[bit] = swap(crossed, bit)

    parts = 2 * head_groups
    make = functools.partial(Stage, owners, cap, group, depth, tokens, cache_blocks, parts)
    kept = {m: x for m, x in far.items() if m not in (0, bit)}
    late = [(True, m | bit) for m in kept]
    places = [(False, m) for m in near]
    values = list(near.values())
    *state, rows_q, counts = attend(
        make(list(places), 0, [], True, False), verticals, offsets, [q_near, q_far], values, [], "attend_near"
    )
    kept, state = lax.optimization_barrier((kept, state))
    last_far = {m | bit: swap(x, bit) for m, x in kept.items()}
    known = len(places)
    places += [(True, m) for m in far]
    values += far.values()
    state = attend(
        make(list(places), known, late, False, False), counts, offsets, [rows_q], values, state, "attend_far"
    )
    known = len(places)
    places += [(True, m) for m in last_far]
    values += last_far.values()
    _, _, *sent = attend(
        make(list(places), known, late, False, True), counts, offsets, [rows_q], values, state, "attend_last"
    )

    def partner(device, k):
        index, lane = divmod(device, head_groups)
        place = (lane * 2 + index // half) ^ k
        return (place % 2 * half + index % half) * head_groups + place // 2

    devices = range(owners * head_groups)
    placed = {0: sent[0]}
    for k in sorted(range(1, parts), key=lambda k: (1 - k % 2, k)):
        placed[k] = lax.ppermute(sent[k], ("ctx", "head"), [(d, partner(d, k)) for d in devices])
    return pl.pallas_call(
        functools.partial(place_kernel, head_groups, half),
        out_shape=jax.ShapeDtypeStruct((tokens // head_groups, parts * columns), queries.dtype),
        in_specs=[pl.BlockSpec(memory_space=pltpu.VMEM)] * parts,
        out_specs=pl.BlockSpec(memory_space=pl.ANY),
        scratch_shapes=[pltpu.SemaphoreType.DMA((parts,))],
        name="place_parts",
    )(*[placed[k] for k in range(parts)])


def solution(mesh):
    in_specs = (
        P("ctx", "head"),
        P("ctx", "head", None),
        P("ctx", "head", None),
        P("head", None),
        P("head", None),
    )
    out_specs = P(("ctx", "head"), None)
    return jax.shard_map(body, mesh=mesh, in_specs=in_specs, out_specs=out_specs, check_vma=False)
```

```python
import functools

import jax
import jax.numpy as jnp
from jax import lax
from jax.experimental import pallas as pl
from jax.experimental.pallas import tpu as pltpu
from jax.sharding import PartitionSpec as P

BLK = 64
NV = 64
MASKED = -1e30
CHUNK = 8
LOG2E = 1.4426950408889634


def collect_kernel(owners, cap, verticals, cache, span, mine, theirs, theirs_rest, raw, sem):
    me = lax.axis_index("ctx")
    upper = me // (owners // 2)
    cache_blocks = cache.shape[0] // BLK
    first = me * cache_blocks

    def block_copy(block, place, slot):
        return pltpu.make_async_copy(
            cache.at[pl.ds(pl.multiple_of(block * BLK, BLK), BLK)], raw.at[place, slot], sem.at[place, slot]
        )

    found = []
    for place in range(2):
        head = upper if place == 0 else 1 - upper

        def visit(n, count):
            block = verticals[head, n] - first
            hit = (block >= 0) & (block < cache_blocks) & (count < cap)

            @pl.when(hit)
            def _():
                block_copy(block, place, count).start()

            return count + hit.astype(jnp.int32)

        found.append(lax.fori_loop(0, NV, visit, jnp.int32(0)))
    split = cap // 2
    for own in range(2):

        @pl.when(upper == own)
        def _():
            mine[cap * BLK :, :] = span[:, own, :]
            theirs[split * BLK :, :] = span[:, 1 - own, :]
            for place, target, start, stop in ((1, theirs, 0, split), (1, theirs_rest, split, cap), (0, mine, 0, cap)):
                head = own if place == 0 else 1 - own

                def unpack(slot, carry):
                    block_copy(0, place, slot).wait()
                    at = pl.ds(pl.multiple_of((slot - start) * BLK, BLK), BLK)
                    target[at, :] = raw[place, slot, :, head, :]
                    return carry

                lax.fori_loop(start, jnp.minimum(found[place], stop), unpack, 0)


class Stage:
    def __init__(self, owners, group, depth, tokens, width, parts, pieces, known, late, first, last):
        self.owners, self.group, self.depth = owners, group, depth
        self.tokens, self.width, self.parts = tokens, width, parts
        self.pieces, self.known, self.late = pieces, known, late
        self.first, self.last = first, last
        self.half = owners // 2
        self.blocks = tokens // BLK
        self.rows = group * BLK
        self.state_rows = 2 * self.blocks * self.rows
        self.slash = bool(late) and not last

    def owner(self, far, m, *_):
        me = lax.axis_index("ctx")
        upper = me // self.half
        return ((1 - upper) if far else upper) * self.half + ((me % self.half) ^ m)


def attend_kernel(stage, scalars, offsets, *refs):
    refs = list(refs)

    def take(count):
        taken, refs[:count] = refs[:count], []
        return taken

    half, blocks, rows, depth, tokens = stage.half, stage.blocks, stage.rows, stage.depth, stage.tokens
    me = lax.axis_index("ctx")
    upper = me // half
    head = upper
    width_kv = 2 * depth
    factor = LOG2E * depth**-0.5
    if stage.first:
        q_near, q_far = take(2)
    else:
        (queries,) = take(1)
    sources = take(len(stage.pieces))
    if stage.first:
        top, acc, queries, counts = take(4)
    else:
        take(2)
        top, acc = take(2)
        counts = scalars
    outs = take(stage.parts) if stage.last else []
    keys, sem = take(2)

    if stage.first:

        def clear(n, carry):
            counts[n] = 0
            return carry

        lax.fori_loop(0, stage.owners, clear, 0)

        def tally(n, carry):
            owner = scalars[head, n] // stage.width
            counts[owner] = counts[owner] + 1
            return carry

        lax.fori_loop(0, NV, tally, 0)

    held = [
        jnp.clip(counts[stage.owner(*piece)] - piece[2][0], 0, piece[2][1] - piece[2][0]) for piece in stage.pieces
    ]
    seen = sum(held[: stage.known], jnp.int32(0))
    present = sum(held[stage.known :], seen)
    begin = seen // CHUNK * CHUNK
    end = jnp.int32(NV) if stage.last else present // CHUNK * CHUNK
    place = jnp.int32(0)
    for source, live in zip(sources, held):

        def fetch(n, carry, place=place, source=source):
            pltpu.make_async_copy(
                source.at[pl.ds(pl.multiple_of(n * BLK, BLK), BLK)],
                keys.at[pl.ds(pl.multiple_of((place + n - begin) * BLK, BLK), BLK), pl.ds(0, width_kv)],
                sem,
            ).start()
            return carry

        lax.fori_loop(jnp.clip(begin - place, 0, live), jnp.clip(end - place, 0, live), fetch, 0)
        place = place + live

    span_copies = []
    if stage.slash or stage.last:
        span, bias, span_sem = take(3)
        wanted = stage.late if stage.last else [piece for piece in stage.pieces if piece[3]]
        for n, piece in enumerate(wanted):
            at = n if stage.last else stage.owner(*piece)
            slots = piece[2][1] - piece[2][0]
            copy = pltpu.make_async_copy(
                sources[stage.pieces.index(piece)].at[pl.ds(slots * BLK, tokens)],
                span.at[pl.ds(pl.multiple_of(at * tokens, BLK), tokens), pl.ds(0, width_kv)],
                span_sem,
            )
            copy.start()
            span_copies.append(copy)
    keys[:, width_kv:] = jnp.ones((keys.shape[0], depth), keys.dtype)
    if stage.first:
        for tile in range(2 * blocks):
            q_ref, block = (q_near, tile) if tile < blocks else (q_far, tile - blocks)
            for j in range(stage.group):
                queries[tile * rows + j * BLK : tile * rows + (j + 1) * BLK, :] = q_ref[
                    block * BLK : (block + 1) * BLK, j * depth : (j + 1) * depth
                ]
        top[...] = jnp.full(top.shape, MASKED, jnp.float32)
        acc[...] = jnp.zeros(acc.shape, jnp.float32)

    def fold(at, scores, values):
        old = top[at, :]
        new = jnp.maximum(old, jnp.max(scores, axis=1, keepdims=True))
        wide = jnp.concatenate([new] * (scores.shape[1] // depth), 1)
        weights = jnp.exp2((scores - wide) * factor).astype(jnp.bfloat16)
        keep = jnp.exp2((old - new) * factor)
        top[at, :] = new
        acc[at, :] = acc[at, :] * jnp.concatenate([keep, keep], 1) + jnp.dot(
            weights, values, preferred_element_type=jnp.float32
        )

    def products(at, rows_k):
        return lax.dot_general(
            queries[at, :], rows_k, (((1,), (1,)), ((), ())), preferred_element_type=jnp.float32
        )

    tiles = [slice(tile * rows, (tile + 1) * rows) for tile in range(2 * blocks)]

    def wait(n, carry):
        pltpu.make_async_copy(
            sources[0].at[pl.ds(0, BLK)], keys.at[pl.ds(0, BLK), pl.ds(0, width_kv)], sem
        ).wait()
        return carry

    lax.fori_loop(0, end - begin, wait, 0)

    def step(c, carry):
        part = pl.ds(pl.multiple_of(c * (CHUNK * BLK), CHUNK * BLK), CHUNK * BLK)
        scores = products(tiles[0], keys[part, :depth])
        for at, following in zip(tiles, tiles[1:] + [None]):
            ahead = products(following, keys[part, :depth]) if following else None
            fold(at, scores, keys[part, depth:])
            scores = ahead
        return carry

    lax.fori_loop(0, (end - begin) // CHUNK, step, 0)

    if span_copies:
        for copy in span_copies:
            copy.wait()
        slash_count = offsets.shape[1]
        q_at = lax.broadcasted_iota(jnp.int32, (BLK, BLK), 0)
        k_at = lax.broadcasted_iota(jnp.int32, (BLK, BLK), 1)
        behind = k_at <= q_at
        late_owners = [stage.owner(*piece) for piece in stage.late]

        def masked(at, tile, rows_k, values):
            scores = products(at, rows_k)
            scores = scores.reshape(stage.group, BLK, rows_k.shape[0]) + bias[tile][None]
            fold(at, scores.reshape(rows, rows_k.shape[0]), values)

        if stage.slash:
            (slash,) = take(1)
            slash[:, :, width_kv:] = jnp.ones((2 * blocks, slash_count * BLK, depth), slash.dtype)
        else:
            span[:, width_kv:] = jnp.ones((span.shape[0], depth), span.dtype)
        for tile, at in enumerate(tiles):
            index = me if tile < blocks else (me + half) % stage.owners
            position = index * blocks + tile % blocks
            if stage.slash:
                for s in range(slash_count):
                    offset = offsets[head, s]
                    block = position - offset
                    here = block >= 0
                    for owner in late_owners:
                        here = here & (block // blocks != owner)
                    start = pl.multiple_of(jnp.where(here, block, position) * BLK, BLK)
                    slash[tile, s * BLK : (s + 1) * BLK, :width_kv] = span[pl.ds(start, BLK), :]
                    allowed = here & ((offset > 0) | behind)
                    bias[tile, :, s * BLK : (s + 1) * BLK] = jnp.where(allowed, 0.0, MASKED)
                masked(at, tile, slash[tile, :, :depth], slash[tile, :, depth:])
            else:
                for n, owner in enumerate(late_owners):
                    for k in range(blocks):
                        distance = position - (owner * blocks + k)
                        chosen = distance == offsets[head, 0]
                        for s in range(1, slash_count):
                            chosen = chosen | (distance == offsets[head, s])
                        allowed = chosen & ((distance > 0) | behind)
                        column = n * tokens + k * BLK
                        bias[tile, :, column : column + BLK] = jnp.where(allowed, 0.0, MASKED)
                masked(at, tile, span[:, :depth], span[:, depth:])

    if stage.last:
        lane = lax.axis_index("head")
        for k, out in enumerate(outs):
            part_rows = out.shape[0]
            token = (lane ^ (k >> 1)) * part_rows
            base = ((k & 1) * blocks + token // BLK) * rows + token % BLK
            for j in range(stage.group):
                at = pl.ds(pl.multiple_of(base + j * BLK, part_rows), part_rows)
                both = acc[at, :]
                out[:, j * depth : (j + 1) * depth] = (both[:, :depth] / both[:, depth:]).astype(out.dtype)


def attend(stage, scalars, offsets, queries, pieces, state, name):
    depth, rows, blocks = stage.depth, stage.state_rows, stage.blocks
    kind = jnp.bfloat16
    held = [jax.ShapeDtypeStruct((rows, depth), jnp.float32), jax.ShapeDtypeStruct((rows, 2 * depth), jnp.float32)]
    vmem, smem = pl.BlockSpec(memory_space=pltpu.VMEM), pl.BlockSpec(memory_space=pltpu.SMEM)
    out_shape, out_specs = list(held), [vmem] * 2
    if stage.first:
        out_shape += [
            jax.ShapeDtypeStruct((rows, depth), kind),
            jax.ShapeDtypeStruct((stage.owners,), jnp.int32),
        ]
        out_specs += [vmem, smem]
    if stage.last:
        part = jax.ShapeDtypeStruct((2 * stage.tokens // stage.parts, stage.group * depth), kind)
        out_shape += [part] * stage.parts
        out_specs += [vmem] * stage.parts
    scratch = [pltpu.VMEM((NV * BLK, 3 * depth), kind), pltpu.SemaphoreType.DMA]
    share = sum(piece[3] for piece in stage.pieces[stage.known :]) * NV // stage.owners * BLK
    if stage.slash:
        keys = offsets.shape[1] * BLK
        scratch += [
            pltpu.VMEM((stage.owners * stage.tokens, 2 * depth), kind),
            pltpu.VMEM((2 * blocks, BLK, keys), jnp.float32),
            pltpu.SemaphoreType.DMA,
            pltpu.VMEM((2 * blocks, keys, 3 * depth), kind),
        ]
        share += keys
    elif stage.last:
        keys = len(stage.late) * stage.tokens
        scratch += [
            pltpu.VMEM((keys, 3 * depth), kind),
            pltpu.VMEM((2 * blocks, BLK, keys), jnp.float32),
            pltpu.SemaphoreType.DMA,
        ]
    operands = [scalars, offsets, *queries, *pieces, *state]
    in_specs = [vmem] * len(queries) + [pl.BlockSpec(memory_space=pl.ANY)] * len(pieces) + [vmem] * len(state)
    return pl.pallas_call(
        functools.partial(attend_kernel, stage),
        out_shape=out_shape,
        grid_spec=pltpu.PrefetchScalarGridSpec(
            num_scalar_prefetch=2, grid=(1,), in_specs=in_specs, out_specs=out_specs, scratch_shapes=scratch
        ),
        input_output_aliases={len(operands) - len(state) + n: n for n in range(len(state))},
        compiler_params=pltpu.CompilerParams(vmem_limit_bytes=40 * 1024 * 1024),
        cost_estimate=pl.CostEstimate(
            flops=2 * rows * depth * share // 4, bytes_accessed=share * 4 * depth, transcendentals=0
        ),
        name=name,
    )(*operands)


def place_kernel(head_groups, half, *refs):
    *parts, out, sem = refs
    here = lax.axis_index("head") * 2 + lax.axis_index("ctx") // half
    copies = []
    for k, part in enumerate(parts):
        columns = part.shape[1]
        start = pl.multiple_of((here ^ k) * columns, columns)
        copies.append(pltpu.make_async_copy(part, out.at[:, pl.ds(start, columns)], sem.at[k]))
        copies[-1].start()
    for copy in copies:
        copy.wait()


def body(queries, span_kv, cache_kv, verticals, offsets):
    tokens = queries.shape[0]
    heads_kv, row_width = span_kv.shape[1:]
    depth = row_width // 2
    columns = queries.shape[1] // heads_kv
    group = columns // depth
    owners = lax.axis_size("ctx")
    head_groups = lax.axis_size("head")
    half = owners // 2
    cache_blocks = cache_kv.shape[0] // BLK
    cap = max(2, 2 * NV // owners)
    upper = lax.axis_index("ctx") // half

    across = [(i, (i + half) % owners) for i in range(owners)]
    send_q = lax.dynamic_slice_in_dim(queries, (1 - upper) * columns, columns, 1)
    q_near = lax.dynamic_slice_in_dim(queries, upper * columns, columns, 1)
    q_far = lax.ppermute(send_q, "ctx", across)
    split = cap // 2

    def rows_of(count):
        return jax.ShapeDtypeStruct((count, row_width), queries.dtype)

    mine, theirs, theirs_rest = pl.pallas_call(
        functools.partial(collect_kernel, owners, cap),
        out_shape=(rows_of(cap * BLK + tokens), rows_of(split * BLK + tokens), rows_of((cap - split) * BLK)),
        grid_spec=pltpu.PrefetchScalarGridSpec(
            num_scalar_prefetch=1,
            grid=(1,),
            in_specs=[pl.BlockSpec(memory_space=pl.ANY), pl.BlockSpec(memory_space=pltpu.VMEM)],
            out_specs=[pl.BlockSpec(memory_space=pltpu.VMEM)] * 3,
            scratch_shapes=[
                pltpu.VMEM((2, cap, BLK, heads_kv, row_width), queries.dtype),
                pltpu.SemaphoreType.DMA((2, cap)),
            ],
        ),
        compiler_params=pltpu.CompilerParams(vmem_limit_bytes=60 * 1024 * 1024),
        cost_estimate=pl.CostEstimate(
            flops=0, bytes_accessed=4 * cap * BLK * heads_kv * row_width, transcendentals=0
        ),
        name="collect_slots",
    )(verticals, cache_kv, span_kv)

    def swap(x, bit):
        return lax.ppermute(x, "ctx", [(i, i ^ bit) for i in range(owners)])

    bits = []
    bit = half // 2
    while bit:
        bits.append(bit)
        bit //= 2
    theirs, q_far = lax.optimization_barrier((theirs, q_far))
    near = {0: mine}
    far = {0: lax.ppermute(theirs, "ctx", across)}
    rest = {0: lax.ppermute(theirs_rest, "ctx", across)}
    for bit in bits[:-1]:
        near.update({m | bit: swap(x, bit) for m, x in near.items()})
    bit = bits[-1]
    own = swap(mine, bit)
    kept = {m: x for m, x in near.items() if m}
    forwarded = {m | bit: swap(x, bit) for m, x in kept.items()}
    first_far, near[bit] = lax.optimization_barrier((far[0], own))
    far_own = swap(first_far, bit)
    rest[0], far_own = lax.optimization_barrier((rest[0], far_own))
    for other in bits[:-1]:
        far.update({m | other: swap(x, other) for m, x in far.items()})
        rest.update({m | other: swap(x, other) for m, x in rest.items()})
    kept_far = {m: x for m, x in far.items() if m}
    kept_rest = {m: x for m, x in rest.items() if m}
    far[bit] = far_own
    rest[bit] = swap(rest[0], bit)
    last_far = {m | bit: swap(x, bit) for m, x in kept_far.items()}

    parts = 2 * head_groups
    make = functools.partial(Stage, owners, group, depth, tokens, cache_blocks, parts)
    whole, low, high = (0, cap), (0, split), (split, cap)
    late = [(True, m, low, True) for m in last_far]
    places = [(False, m, whole, True) for m in near]
    values = list(near.values())
    *state, rows_q, counts = attend(
        make(list(places), 0, [], True, False), verticals, offsets, [q_near, q_far], values, [], "attend_near"
    )
    kept_rest, state = lax.optimization_barrier((kept_rest, state))
    last_rest = {m | bit: swap(x, bit) for m, x in kept_rest.items()}
    known = len(places)
    for sides, far_side, slots, tail in (
        (forwarded, False, whole, True), (far, True, low, True), (rest, True, high, False)
    ):
        places += [(far_side, m, slots, tail) for m in sides]
        values += sides.values()
    state = attend(
        make(list(places), known, late, False, False), counts, offsets, [rows_q], values, state, "attend_far"
    )
    known = len(places)
    for sides, slots, tail in ((last_far, low, True), (last_rest, high, False)):
        places += [(True, m, slots, tail) for m in sides]
        values += sides.values()
    _, _, *sent = attend(
        make(list(places), known, late, False, True), counts, offsets, [rows_q], values, state, "attend_last"
    )

    def partner(device, k):
        index, lane = divmod(device, head_groups)
        place = (lane * 2 + index // half) ^ k
        return (place % 2 * half + index % half) * head_groups + place // 2

    devices = range(owners * head_groups)
    placed = {0: sent[0]}
    for k in sorted(range(1, parts), key=lambda k: (1 - k % 2, k)):
        placed[k] = lax.ppermute(sent[k], ("ctx", "head"), [(d, partner(d, k)) for d in devices])
    return pl.pallas_call(
        functools.partial(place_kernel, head_groups, half),
        out_shape=jax.ShapeDtypeStruct((tokens // head_groups, parts * columns), queries.dtype),
        in_specs=[pl.BlockSpec(memory_space=pltpu.VMEM)] * parts,
        out_specs=pl.BlockSpec(memory_space=pl.ANY),
        scratch_shapes=[pltpu.SemaphoreType.DMA((parts,))],
        name="place_parts",
    )(*[placed[k] for k in range(parts)])


def solution(mesh):
    in_specs = (
        P("ctx", "head"),
        P("ctx", "head", None),
        P("ctx", "head", None),
        P("head", None),
        P("head", None),
    )
    out_specs = P(("ctx", "head"), None)
    return jax.shard_map(body, mesh=mesh, in_specs=in_specs, out_specs=out_specs, check_vma=False)
```

```python
import functools

import jax
import jax.numpy as jnp
from jax import lax
from jax.experimental import pallas as pl
from jax.experimental.pallas import tpu as pltpu
from jax.sharding import PartitionSpec as P

BLK = 64
NV = 64
MASKED = -1e30
CHUNK = 8
LOG2E = 1.4426950408889634


def collect_kernel(owners, cap, verticals, cache, span, mine, theirs, theirs_rest, raw, sem):
    me = lax.axis_index("ctx")
    upper = me // (owners // 2)
    cache_blocks = cache.shape[0] // BLK
    first = me * cache_blocks

    def block_copy(block, place, slot):
        return pltpu.make_async_copy(
            cache.at[pl.ds(pl.multiple_of(block * BLK, BLK), BLK)], raw.at[place, slot], sem.at[place, slot]
        )

    found = []
    for place in range(2):
        head = upper if place == 0 else 1 - upper

        def visit(n, count):
            block = verticals[head, n] - first
            hit = (block >= 0) & (block < cache_blocks) & (count < cap)

            @pl.when(hit)
            def _():
                block_copy(block, place, count).start()

            return count + hit.astype(jnp.int32)

        found.append(lax.fori_loop(0, NV, visit, jnp.int32(0)))
    split = cap // 2
    for own in range(2):

        @pl.when(upper == own)
        def _():
            mine[cap * BLK :, :] = span[:, own, :]
            theirs[split * BLK :, :] = span[:, 1 - own, :]
            for place, target, start, stop in ((1, theirs, 0, split), (1, theirs_rest, split, cap), (0, mine, 0, cap)):
                head = own if place == 0 else 1 - own

                def unpack(slot, carry):
                    block_copy(0, place, slot).wait()
                    at = pl.ds(pl.multiple_of((slot - start) * BLK, BLK), BLK)
                    target[at, :] = raw[place, slot, :, head, :]
                    return carry

                lax.fori_loop(start, jnp.minimum(found[place], stop), unpack, 0)


class Stage:
    def __init__(self, owners, group, depth, tokens, width, parts, pieces, known, late, first, last):
        self.owners, self.group, self.depth = owners, group, depth
        self.tokens, self.width, self.parts = tokens, width, parts
        self.pieces, self.known, self.late = pieces, known, late
        self.first, self.last = first, last
        self.half = owners // 2
        self.blocks = tokens // BLK
        self.rows = group * BLK
        self.state_rows = 2 * self.blocks * self.rows
        self.slash = bool(late) and not last

    def owner(self, far, m, *_):
        me = lax.axis_index("ctx")
        upper = me // self.half
        return ((1 - upper) if far else upper) * self.half + ((me % self.half) ^ m)


def attend_kernel(stage, scalars, offsets, *refs):
    refs = list(refs)

    def take(count):
        taken, refs[:count] = refs[:count], []
        return taken

    half, blocks, rows, depth, tokens = stage.half, stage.blocks, stage.rows, stage.depth, stage.tokens
    me = lax.axis_index("ctx")
    upper = me // half
    head = upper
    width_kv = 2 * depth
    factor = LOG2E * depth**-0.5
    if stage.first:
        q_near, q_far = take(2)
    else:
        (queries,) = take(1)
    sources = take(len(stage.pieces))
    if stage.first:
        top, acc, queries, counts = take(4)
    else:
        take(2)
        top, acc = take(2)
        counts = scalars
    outs = take(stage.parts) if stage.last else []
    keys, sem = take(2)

    if stage.first:

        def clear(n, carry):
            counts[n] = 0
            return carry

        lax.fori_loop(0, stage.owners, clear, 0)

        def tally(n, carry):
            owner = scalars[head, n] // stage.width
            counts[owner] = counts[owner] + 1
            return carry

        lax.fori_loop(0, NV, tally, 0)

    held = [
        jnp.clip(counts[stage.owner(*piece)] - piece[2][0], 0, piece[2][1] - piece[2][0]) for piece in stage.pieces
    ]
    seen = sum(held[: stage.known], jnp.int32(0))
    present = sum(held[stage.known :], seen)
    begin = seen // CHUNK * CHUNK
    end = jnp.int32(NV) if stage.last else present // CHUNK * CHUNK
    place = jnp.int32(0)
    for source, live in zip(sources, held):

        def fetch(n, carry, place=place, source=source):
            at = place + n - begin
            pltpu.make_async_copy(
                source.at[pl.ds(pl.multiple_of(n * BLK, BLK), BLK)],
                keys.at[pl.ds(pl.multiple_of(at * BLK, BLK), BLK), pl.ds(0, width_kv)],
                sem.at[at // CHUNK],
            ).start()
            return carry

        lax.fori_loop(jnp.clip(begin - place, 0, live), jnp.clip(end - place, 0, live), fetch, 0)
        place = place + live

    span_copies = []
    if stage.slash or stage.last:
        span, bias, span_sem = take(3)
        wanted = stage.late if stage.last else [piece for piece in stage.pieces if piece[3]]
        for n, piece in enumerate(wanted):
            at = n if stage.last else stage.owner(*piece)
            slots = piece[2][1] - piece[2][0]
            copy = pltpu.make_async_copy(
                sources[stage.pieces.index(piece)].at[pl.ds(slots * BLK, tokens)],
                span.at[pl.ds(pl.multiple_of(at * tokens, BLK), tokens), pl.ds(0, width_kv)],
                span_sem,
            )
            copy.start()
            span_copies.append(copy)
    keys[:, width_kv:] = jnp.ones((keys.shape[0], depth), keys.dtype)
    if stage.first:
        for tile in range(2 * blocks):
            q_ref, block = (q_near, tile) if tile < blocks else (q_far, tile - blocks)
            for j in range(stage.group):
                queries[tile * rows + j * BLK : tile * rows + (j + 1) * BLK, :] = q_ref[
                    block * BLK : (block + 1) * BLK, j * depth : (j + 1) * depth
                ]
        top[...] = jnp.full(top.shape, MASKED, jnp.float32)
        acc[...] = jnp.zeros(acc.shape, jnp.float32)

    def fold(at, scores, values):
        old = top[at, :]
        new = jnp.maximum(old, jnp.max(scores, axis=1, keepdims=True))
        wide = jnp.concatenate([new] * (scores.shape[1] // depth), 1)
        weights = jnp.exp2((scores - wide) * factor).astype(jnp.bfloat16)
        keep = jnp.exp2((old - new) * factor)
        top[at, :] = new
        acc[at, :] = acc[at, :] * jnp.concatenate([keep, keep], 1) + jnp.dot(
            weights, values, preferred_element_type=jnp.float32
        )

    def products(at, rows_k):
        return lax.dot_general(
            queries[at, :], rows_k, (((1,), (1,)), ((), ())), preferred_element_type=jnp.float32
        )

    tiles = [slice(tile * rows, (tile + 1) * rows) for tile in range(2 * blocks)]

    def step(c, carry):
        part = pl.ds(pl.multiple_of(c * (CHUNK * BLK), CHUNK * BLK), CHUNK * BLK)
        chunk = keys.at[part, pl.ds(0, width_kv)]
        pltpu.make_async_copy(chunk, chunk, sem.at[c]).wait()
        scores = products(tiles[0], keys[part, :depth])
        for at, following in zip(tiles, tiles[1:] + [None]):
            ahead = products(following, keys[part, :depth]) if following else None
            fold(at, scores, keys[part, depth:])
            scores = ahead
        return carry

    lax.fori_loop(0, (end - begin) // CHUNK, step, 0)

    if span_copies:
        for copy in span_copies:
            copy.wait()
        slash_count = offsets.shape[1]
        q_at = lax.broadcasted_iota(jnp.int32, (BLK, BLK), 0)
        k_at = lax.broadcasted_iota(jnp.int32, (BLK, BLK), 1)
        behind = k_at <= q_at
        late_owners = [stage.owner(*piece) for piece in stage.late]

        def masked(at, tile, rows_k, values):
            scores = products(at, rows_k)
            scores = scores.reshape(stage.group, BLK, rows_k.shape[0]) + bias[tile][None]
            fold(at, scores.reshape(rows, rows_k.shape[0]), values)

        if stage.slash:
            (slash,) = take(1)
            slash[:, :, width_kv:] = jnp.ones((2 * blocks, slash_count * BLK, depth), slash.dtype)
        else:
            span[:, width_kv:] = jnp.ones((span.shape[0], depth), span.dtype)
        for tile, at in enumerate(tiles):
            index = me if tile < blocks else (me + half) % stage.owners
            position = index * blocks + tile % blocks
            if stage.slash:
                for s in range(slash_count):
                    offset = offsets[head, s]
                    block = position - offset
                    here = block >= 0
                    for owner in late_owners:
                        here = here & (block // blocks != owner)
                    start = pl.multiple_of(jnp.where(here, block, position) * BLK, BLK)
                    slash[tile, s * BLK : (s + 1) * BLK, :width_kv] = span[pl.ds(start, BLK), :]
                    allowed = here & ((offset > 0) | behind)
                    bias[tile, :, s * BLK : (s + 1) * BLK] = jnp.where(allowed, 0.0, MASKED)
                masked(at, tile, slash[tile, :, :depth], slash[tile, :, depth:])
            else:
                for n, owner in enumerate(late_owners):
                    for k in range(blocks):
                        distance = position - (owner * blocks + k)
                        chosen = distance == offsets[head, 0]
                        for s in range(1, slash_count):
                            chosen = chosen | (distance == offsets[head, s])
                        allowed = chosen & ((distance > 0) | behind)
                        column = n * tokens + k * BLK
                        bias[tile, :, column : column + BLK] = jnp.where(allowed, 0.0, MASKED)
                masked(at, tile, span[:, :depth], span[:, depth:])

    if stage.last:
        lane = lax.axis_index("head")
        for k, out in enumerate(outs):
            part_rows = out.shape[0]
            token = (lane ^ (k >> 1)) * part_rows
            base = ((k & 1) * blocks + token // BLK) * rows + token % BLK
            for j in range(stage.group):
                at = pl.ds(pl.multiple_of(base + j * BLK, part_rows), part_rows)
                both = acc[at, :]
                out[:, j * depth : (j + 1) * depth] = (both[:, :depth] / both[:, depth:]).astype(out.dtype)


def attend(stage, scalars, offsets, queries, pieces, state, name):
    depth, rows, blocks = stage.depth, stage.state_rows, stage.blocks
    kind = jnp.bfloat16
    held = [jax.ShapeDtypeStruct((rows, depth), jnp.float32), jax.ShapeDtypeStruct((rows, 2 * depth), jnp.float32)]
    vmem, smem = pl.BlockSpec(memory_space=pltpu.VMEM), pl.BlockSpec(memory_space=pltpu.SMEM)
    out_shape, out_specs = list(held), [vmem] * 2
    if stage.first:
        out_shape += [
            jax.ShapeDtypeStruct((rows, depth), kind),
            jax.ShapeDtypeStruct((stage.owners,), jnp.int32),
        ]
        out_specs += [vmem, smem]
    if stage.last:
        part = jax.ShapeDtypeStruct((2 * stage.tokens // stage.parts, stage.group * depth), kind)
        out_shape += [part] * stage.parts
        out_specs += [vmem] * stage.parts
    scratch = [pltpu.VMEM((NV * BLK, 3 * depth), kind), pltpu.SemaphoreType.DMA((NV // CHUNK,))]
    share = sum(piece[3] for piece in stage.pieces[stage.known :]) * NV // stage.owners * BLK
    if stage.slash:
        keys = offsets.shape[1] * BLK
        scratch += [
            pltpu.VMEM((stage.owners * stage.tokens, 2 * depth), kind),
            pltpu.VMEM((2 * blocks, BLK, keys), jnp.float32),
            pltpu.SemaphoreType.DMA,
            pltpu.VMEM((2 * blocks, keys, 3 * depth), kind),
        ]
        share += keys
    elif stage.last:
        keys = len(stage.late) * stage.tokens
        scratch += [
            pltpu.VMEM((keys, 3 * depth), kind),
            pltpu.VMEM((2 * blocks, BLK, keys), jnp.float32),
            pltpu.SemaphoreType.DMA,
        ]
    operands = [scalars, offsets, *queries, *pieces, *state]
    in_specs = [vmem] * len(queries) + [pl.BlockSpec(memory_space=pl.ANY)] * len(pieces) + [vmem] * len(state)
    return pl.pallas_call(
        functools.partial(attend_kernel, stage),
        out_shape=out_shape,
        grid_spec=pltpu.PrefetchScalarGridSpec(
            num_scalar_prefetch=2, grid=(1,), in_specs=in_specs, out_specs=out_specs, scratch_shapes=scratch
        ),
        input_output_aliases={len(operands) - len(state) + n: n for n in range(len(state))},
        compiler_params=pltpu.CompilerParams(vmem_limit_bytes=28 * 1024 * 1024),
        cost_estimate=pl.CostEstimate(
            flops=2 * rows * depth * share // 4, bytes_accessed=share * 4 * depth, transcendentals=0
        ),
        name=name,
    )(*operands)


def place_kernel(head_groups, half, *refs):
    *parts, out, sem = refs
    here = lax.axis_index("head") * 2 + lax.axis_index("ctx") // half
    copies = []
    for k, part in enumerate(parts):
        columns = part.shape[1]
        start = pl.multiple_of((here ^ k) * columns, columns)
        copies.append(pltpu.make_async_copy(part, out.at[:, pl.ds(start, columns)], sem.at[k]))
        copies[-1].start()
    for copy in copies:
        copy.wait()


def body(queries, span_kv, cache_kv, verticals, offsets):
    tokens = queries.shape[0]
    heads_kv, row_width = span_kv.shape[1:]
    depth = row_width // 2
    columns = queries.shape[1] // heads_kv
    group = columns // depth
    owners = lax.axis_size("ctx")
    head_groups = lax.axis_size("head")
    half = owners // 2
    cache_blocks = cache_kv.shape[0] // BLK
    cap = max(2, 2 * NV // owners)
    upper = lax.axis_index("ctx") // half

    across = [(i, (i + half) % owners) for i in range(owners)]
    send_q = lax.dynamic_slice_in_dim(queries, (1 - upper) * columns, columns, 1)
    q_near = lax.dynamic_slice_in_dim(queries, upper * columns, columns, 1)
    q_far = lax.ppermute(send_q, "ctx", across)
    split = cap // 2

    def rows_of(count):
        return jax.ShapeDtypeStruct((count, row_width), queries.dtype)

    mine, theirs, theirs_rest = pl.pallas_call(
        functools.partial(collect_kernel, owners, cap),
        out_shape=(rows_of(cap * BLK + tokens), rows_of(split * BLK + tokens), rows_of((cap - split) * BLK)),
        grid_spec=pltpu.PrefetchScalarGridSpec(
            num_scalar_prefetch=1,
            grid=(1,),
            in_specs=[pl.BlockSpec(memory_space=pl.ANY), pl.BlockSpec(memory_space=pltpu.VMEM)],
            out_specs=[pl.BlockSpec(memory_space=pltpu.VMEM)] * 3,
            scratch_shapes=[
                pltpu.VMEM((2, cap, BLK, heads_kv, row_width), queries.dtype),
                pltpu.SemaphoreType.DMA((2, cap)),
            ],
        ),
        compiler_params=pltpu.CompilerParams(vmem_limit_bytes=60 * 1024 * 1024),
        cost_estimate=pl.CostEstimate(
            flops=0, bytes_accessed=4 * cap * BLK * heads_kv * row_width, transcendentals=0
        ),
        name="collect_slots",
    )(verticals, cache_kv, span_kv)

    def swap(x, bit):
        return lax.ppermute(x, "ctx", [(i, i ^ bit) for i in range(owners)])

    bits = []
    bit = half // 2
    while bit:
        bits.append(bit)
        bit //= 2
    parts = 2 * head_groups
    whole, low, high = (0, cap), (0, split), (split, cap)
    last_bit = bits[-1]
    late = [(True, m | last_bit, low, True) for m in range(1, half) if not m & last_bit]
    places, values = [], []
    state, operands, scalars = [], [q_near, q_far], verticals

    def stage(name, *arrived, slash=False, last=False):
        nonlocal state, operands, scalars
        known, first = len(places), not places
        for far_side, slots, tail, sides in arrived:
            places.extend((far_side, m, slots, tail) for m in sides)
            values.extend(sides.values())
        kind = Stage(
            owners, group, depth, tokens, cache_blocks, parts, list(places), known,
            late if slash or last else [], first, last,
        )
        top, acc, *more = attend(kind, scalars, offsets, operands, values, state, name)
        state = [top, acc]
        if first:
            operands, scalars = [more[0]], more[1]
        return more

    near = {0: mine}
    far = {0: lax.ppermute(theirs, "ctx", across)}
    own = swap(mine, last_bit)
    rest = {0: lax.ppermute(theirs_rest, "ctx", across)}
    for bit in bits[:-1]:
        near.update({m | bit: swap(x, bit) for m, x in near.items()})
    del near[0]
    first_far, own = lax.optimization_barrier((far[0], own))
    far_own = swap(first_far, last_bit)
    near, q_far, far_own = lax.optimization_barrier((near, q_far, far_own))
    operands[1] = q_far
    forwarded = {m | last_bit: swap(x, last_bit) for m, x in near.items()}
    stage("attend_own", (False, whole, True, {0: mine, last_bit: own}))
    stage("attend_near", (False, whole, True, near), (True, low, True, {0: first_far}))
    rest[0], state = lax.optimization_barrier((rest[0], state))
    for bit in bits[:-1]:
        far.update({m | bit: swap(x, bit) for m, x in far.items()})
        rest.update({m | bit: swap(x, bit) for m, x in rest.items()})
    far.pop(0)
    last_far = {m | last_bit: swap(x, last_bit) for m, x in far.items()}
    rest_own = swap(rest[0], last_bit)
    stage("attend_forwarded", (False, whole, True, forwarded), (True, low, True, {last_bit: far_own}))
    first_rest = rest.pop(0)
    rest, state = lax.optimization_barrier((rest, state))
    last_rest = {m | last_bit: swap(x, last_bit) for m, x in rest.items()}
    stage(
        "attend_far", (True, low, True, far), (True, high, False, {0: first_rest, last_bit: rest_own}),
        (True, high, False, rest), slash=True,
    )
    sent = stage("attend_last", (True, low, True, last_far), (True, high, False, last_rest), last=True)

    def partner(device, k):
        index, lane = divmod(device, head_groups)
        place = (lane * 2 + index // half) ^ k
        return (place % 2 * half + index % half) * head_groups + place // 2

    devices = range(owners * head_groups)
    placed = {0: sent[0]}
    for k in sorted(range(1, parts), key=lambda k: (1 - k % 2, k)):
        placed[k] = lax.ppermute(sent[k], ("ctx", "head"), [(d, partner(d, k)) for d in devices])
    return pl.pallas_call(
        functools.partial(place_kernel, head_groups, half),
        out_shape=jax.ShapeDtypeStruct((tokens // head_groups, parts * columns), queries.dtype),
        in_specs=[pl.BlockSpec(memory_space=pl.ANY)] * parts,
        out_specs=pl.BlockSpec(memory_space=pl.ANY),
        scratch_shapes=[pltpu.SemaphoreType.DMA((parts,))],
        name="place_parts",
    )(*[placed[k] for k in range(parts)])


def solution(mesh):
    in_specs = (
        P("ctx", "head"),
        P("ctx", "head", None),
        P("ctx", "head", None),
        P("head", None),
        P("head", None),
    )
    out_specs = P(("ctx", "head"), None)
    return jax.shard_map(body, mesh=mesh, in_specs=in_specs, out_specs=out_specs, check_vma=False)
```

```python
import functools

import jax
import jax.numpy as jnp
from jax import lax
from jax.experimental import pallas as pl
from jax.experimental.pallas import tpu as pltpu
from jax.sharding import PartitionSpec as P

BLK = 64
NV = 64
MASKED = -1e30
CHUNK = 8
LOG2E = 1.4426950408889634


def collect_kernel(owners, cap, verticals, cache, span, mine, theirs, theirs_rest, raw, sem):
    me = lax.axis_index("ctx")
    upper = me // (owners // 2)
    cache_blocks = cache.shape[0] // BLK
    first = me * cache_blocks

    def block_copy(block, place, slot):
        return pltpu.make_async_copy(
            cache.at[pl.ds(pl.multiple_of(block * BLK, BLK), BLK)], raw.at[place, slot], sem.at[place, slot]
        )

    found = []
    for place in range(2):
        head = upper if place == 0 else 1 - upper

        def visit(n, count):
            block = verticals[head, n] - first
            hit = (block >= 0) & (block < cache_blocks) & (count < cap)

            @pl.when(hit)
            def _():
                block_copy(block, place, count).start()

            return count + hit.astype(jnp.int32)

        found.append(lax.fori_loop(0, NV, visit, jnp.int32(0)))
    split = cap // 2
    for own in range(2):

        @pl.when(upper == own)
        def _():
            mine[cap * BLK :, :] = span[:, own, :]
            theirs[split * BLK :, :] = span[:, 1 - own, :]
            for place, target, start, stop in ((1, theirs, 0, split), (1, theirs_rest, split, cap), (0, mine, 0, cap)):
                head = own if place == 0 else 1 - own

                def unpack(slot, carry):
                    block_copy(0, place, slot).wait()
                    at = pl.ds(pl.multiple_of((slot - start) * BLK, BLK), BLK)
                    target[at, :] = raw[place, slot, :, head, :]
                    return carry

                lax.fori_loop(start, jnp.minimum(found[place], stop), unpack, 0)


class Stage:
    def __init__(self, owners, group, depth, tokens, width, parts, pieces, known, late, first, last):
        self.owners, self.group, self.depth = owners, group, depth
        self.tokens, self.width, self.parts = tokens, width, parts
        self.pieces, self.known, self.late = pieces, known, late
        self.first, self.last = first, last
        self.half = owners // 2
        self.blocks = tokens // BLK
        self.rows = group * BLK
        self.state_rows = 2 * self.blocks * self.rows
        self.slash = bool(late) and not last

    def owner(self, far, m, *_):
        me = lax.axis_index("ctx")
        upper = me // self.half
        return ((1 - upper) if far else upper) * self.half + ((me % self.half) ^ m)


def attend_kernel(stage, scalars, offsets, *refs):
    refs = list(refs)

    def take(count):
        taken, refs[:count] = refs[:count], []
        return taken

    half, blocks, rows, depth, tokens = stage.half, stage.blocks, stage.rows, stage.depth, stage.tokens
    me = lax.axis_index("ctx")
    upper = me // half
    head = upper
    width_kv = 2 * depth
    factor = LOG2E * depth**-0.5
    if stage.first:
        q_near, q_far = take(2)
    else:
        (queries,) = take(1)
    sources = take(len(stage.pieces))
    if stage.first:
        top, acc, queries, counts = take(4)
    else:
        take(2)
        top, acc = take(2)
        counts = scalars
    outs = take(stage.parts) if stage.last else []
    keys, sem = take(2)

    if stage.first:

        def clear(n, carry):
            counts[n] = 0
            return carry

        lax.fori_loop(0, stage.owners, clear, 0)

        def tally(n, carry):
            owner = scalars[head, n] // stage.width
            counts[owner] = counts[owner] + 1
            return carry

        lax.fori_loop(0, NV, tally, 0)

    held = [
        jnp.clip(counts[stage.owner(*piece)] - piece[2][0], 0, piece[2][1] - piece[2][0]) for piece in stage.pieces
    ]
    seen = sum(held[: stage.known], jnp.int32(0))
    present = sum(held[stage.known :], seen)
    begin = seen // CHUNK * CHUNK
    end = jnp.int32(NV) if stage.last else present // CHUNK * CHUNK
    place = jnp.int32(0)
    for source, live in zip(sources, held):

        def fetch(n, carry, place=place, source=source):
            at = place + n - begin
            pltpu.make_async_copy(
                source.at[pl.ds(pl.multiple_of(n * BLK, BLK), BLK)],
                keys.at[pl.ds(pl.multiple_of(at * BLK, BLK), BLK), pl.ds(0, width_kv)],
                sem.at[at // CHUNK],
            ).start()
            return carry

        lax.fori_loop(jnp.clip(begin - place, 0, live), jnp.clip(end - place, 0, live), fetch, 0)
        place = place + live

    span_copies = []
    if stage.slash or stage.last:
        span, bias, span_sem = take(3)
        wanted = stage.late if stage.last else [piece for piece in stage.pieces if piece[3]]
        for n, piece in enumerate(wanted):
            at = n if stage.last else stage.owner(*piece)
            slots = piece[2][1] - piece[2][0]
            copy = pltpu.make_async_copy(
                sources[stage.pieces.index(piece)].at[pl.ds(slots * BLK, tokens)],
                span.at[pl.ds(pl.multiple_of(at * tokens, BLK), tokens), pl.ds(0, width_kv)],
                span_sem,
            )
            copy.start()
            span_copies.append(copy)
    keys[:, width_kv:] = jnp.ones((keys.shape[0], depth), keys.dtype)
    if stage.first:
        for tile in range(2 * blocks):
            q_ref, block = (q_near, tile) if tile < blocks else (q_far, tile - blocks)
            for j in range(stage.group):
                queries[tile * rows + j * BLK : tile * rows + (j + 1) * BLK, :] = q_ref[
                    block * BLK : (block + 1) * BLK, j * depth : (j + 1) * depth
                ]
        top[...] = jnp.full(top.shape, MASKED, jnp.float32)
        acc[...] = jnp.zeros(acc.shape, jnp.float32)

    def fold(at, scores, values):
        old = top[at, :]
        new = jnp.maximum(old, jnp.max(scores, axis=1, keepdims=True))
        wide = jnp.concatenate([new] * (scores.shape[1] // depth), 1)
        weights = jnp.exp2((scores - wide) * factor).astype(jnp.bfloat16)
        keep = jnp.exp2((old - new) * factor)
        top[at, :] = new
        acc[at, :] = acc[at, :] * jnp.concatenate([keep, keep], 1) + jnp.dot(
            weights, values, preferred_element_type=jnp.float32
        )

    def products(at, rows_k):
        return lax.dot_general(
            queries[at, :], rows_k, (((1,), (1,)), ((), ())), preferred_element_type=jnp.float32
        )

    tiles = [slice(tile * rows, (tile + 1) * rows) for tile in range(2 * blocks)]

    def step(c, carry):
        part = pl.ds(pl.multiple_of(c * (CHUNK * BLK), CHUNK * BLK), CHUNK * BLK)
        chunk = keys.at[part, pl.ds(0, width_kv)]
        pltpu.make_async_copy(chunk, chunk, sem.at[c]).wait()
        scores = products(tiles[0], keys[part, :depth])
        for at, following in zip(tiles, tiles[1:] + [None]):
            ahead = products(following, keys[part, :depth]) if following else None
            fold(at, scores, keys[part, depth:])
            scores = ahead
        return carry

    lax.fori_loop(0, (end - begin) // CHUNK, step, 0)

    if span_copies:
        for copy in span_copies:
            copy.wait()
        slash_count = offsets.shape[1]
        q_at = lax.broadcasted_iota(jnp.int32, (BLK, BLK), 0)
        k_at = lax.broadcasted_iota(jnp.int32, (BLK, BLK), 1)
        behind = k_at <= q_at
        late_owners = [stage.owner(*piece) for piece in stage.late]

        def masked(at, tile, rows_k, values):
            scores = products(at, rows_k)
            scores = scores.reshape(stage.group, BLK, rows_k.shape[0]) + bias[tile][None]
            fold(at, scores.reshape(rows, rows_k.shape[0]), values)

        if stage.slash:
            (slash,) = take(1)
            slash[:, :, width_kv:] = jnp.ones((2 * blocks, slash_count * BLK, depth), slash.dtype)
        else:
            span[:, width_kv:] = jnp.ones((span.shape[0], depth), span.dtype)
        for tile, at in enumerate(tiles):
            index = me if tile < blocks else (me + half) % stage.owners
            position = index * blocks + tile % blocks
            if stage.slash:
                for s in range(slash_count):
                    offset = offsets[head, s]
                    block = position - offset
                    here = block >= 0
                    for owner in late_owners:
                        here = here & (block // blocks != owner)
                    start = pl.multiple_of(jnp.where(here, block, position) * BLK, BLK)
                    slash[tile, s * BLK : (s + 1) * BLK, :width_kv] = span[pl.ds(start, BLK), :]
                    allowed = here & ((offset > 0) | behind)
                    bias[tile, :, s * BLK : (s + 1) * BLK] = jnp.where(allowed, 0.0, MASKED)
                masked(at, tile, slash[tile, :, :depth], slash[tile, :, depth:])
            else:
                for n, owner in enumerate(late_owners):
                    for k in range(blocks):
                        distance = position - (owner * blocks + k)
                        chosen = distance == offsets[head, 0]
                        for s in range(1, slash_count):
                            chosen = chosen | (distance == offsets[head, s])
                        allowed = chosen & ((distance > 0) | behind)
                        column = n * tokens + k * BLK
                        bias[tile, :, column : column + BLK] = jnp.where(allowed, 0.0, MASKED)
                masked(at, tile, span[:, :depth], span[:, depth:])

    if stage.last:
        lane = lax.axis_index("head")
        for k, out in enumerate(outs):
            part_rows = out.shape[0]
            token = (lane ^ (k >> 1)) * part_rows
            base = ((k & 1) * blocks + token // BLK) * rows + token % BLK
            for j in range(stage.group):
                at = pl.ds(pl.multiple_of(base + j * BLK, part_rows), part_rows)
                both = acc[at, :]
                out[:, j * depth : (j + 1) * depth] = (both[:, :depth] / both[:, depth:]).astype(out.dtype)


def attend(stage, scalars, offsets, queries, pieces, state, name):
    depth, rows, blocks = stage.depth, stage.state_rows, stage.blocks
    kind = jnp.bfloat16
    held = [jax.ShapeDtypeStruct((rows, depth), jnp.float32), jax.ShapeDtypeStruct((rows, 2 * depth), jnp.float32)]
    vmem, smem = pl.BlockSpec(memory_space=pltpu.VMEM), pl.BlockSpec(memory_space=pltpu.SMEM)
    out_shape, out_specs = list(held), [vmem] * 2
    if stage.first:
        out_shape += [
            jax.ShapeDtypeStruct((rows, depth), kind),
            jax.ShapeDtypeStruct((stage.owners,), jnp.int32),
        ]
        out_specs += [vmem, smem]
    if stage.last:
        part = jax.ShapeDtypeStruct((2 * stage.tokens // stage.parts, stage.group * depth), kind)
        out_shape += [part] * stage.parts
        out_specs += [vmem] * stage.parts
    scratch = [pltpu.VMEM((NV * BLK, 3 * depth), kind), pltpu.SemaphoreType.DMA((NV // CHUNK,))]
    share = sum(piece[3] for piece in stage.pieces[stage.known :]) * NV // stage.owners * BLK
    if stage.slash:
        keys = offsets.shape[1] * BLK
        scratch += [
            pltpu.VMEM((stage.owners * stage.tokens, 2 * depth), kind),
            pltpu.VMEM((2 * blocks, BLK, keys), jnp.float32),
            pltpu.SemaphoreType.DMA,
            pltpu.VMEM((2 * blocks, keys, 3 * depth), kind),
        ]
        share += keys
    elif stage.last:
        keys = len(stage.late) * stage.tokens
        scratch += [
            pltpu.VMEM((keys, 3 * depth), kind),
            pltpu.VMEM((2 * blocks, BLK, keys), jnp.float32),
            pltpu.SemaphoreType.DMA,
        ]
    operands = [scalars, offsets, *queries, *pieces, *state]
    in_specs = [vmem] * len(queries) + [pl.BlockSpec(memory_space=pl.ANY)] * len(pieces) + [vmem] * len(state)
    return pl.pallas_call(
        functools.partial(attend_kernel, stage),
        out_shape=out_shape,
        grid_spec=pltpu.PrefetchScalarGridSpec(
            num_scalar_prefetch=2, grid=(1,), in_specs=in_specs, out_specs=out_specs, scratch_shapes=scratch
        ),
        input_output_aliases={len(operands) - len(state) + n: n for n in range(len(state))},
        compiler_params=pltpu.CompilerParams(vmem_limit_bytes=28 * 1024 * 1024),
        cost_estimate=pl.CostEstimate(
            flops=2 * rows * depth * share // 4, bytes_accessed=share * 4 * depth, transcendentals=0
        ),
        name=name,
    )(*operands)


def place_kernel(head_groups, half, *refs):
    *parts, out, sem = refs
    here = lax.axis_index("head") * 2 + lax.axis_index("ctx") // half
    copies = []
    for k, part in enumerate(parts):
        columns = part.shape[1]
        start = pl.multiple_of((here ^ k) * columns, columns)
        copies.append(pltpu.make_async_copy(part, out.at[:, pl.ds(start, columns)], sem.at[k]))
        copies[-1].start()
    for copy in copies:
        copy.wait()


def body(queries, span_kv, cache_kv, verticals, offsets):
    tokens = queries.shape[0]
    heads_kv, row_width = span_kv.shape[1:]
    depth = row_width // 2
    columns = queries.shape[1] // heads_kv
    group = columns // depth
    owners = lax.axis_size("ctx")
    head_groups = lax.axis_size("head")
    half = owners // 2
    cache_blocks = cache_kv.shape[0] // BLK
    cap = max(2, 2 * NV // owners)
    upper = lax.axis_index("ctx") // half

    across = [(i, (i + half) % owners) for i in range(owners)]
    send_q = lax.dynamic_slice_in_dim(queries, (1 - upper) * columns, columns, 1)
    q_near = lax.dynamic_slice_in_dim(queries, upper * columns, columns, 1)
    q_far = lax.ppermute(send_q, "ctx", across)
    split = cap // 2

    def rows_of(count):
        return jax.ShapeDtypeStruct((count, row_width), queries.dtype)

    mine, theirs, theirs_rest = pl.pallas_call(
        functools.partial(collect_kernel, owners, cap),
        out_shape=(rows_of(cap * BLK + tokens), rows_of(split * BLK + tokens), rows_of((cap - split) * BLK)),
        grid_spec=pltpu.PrefetchScalarGridSpec(
            num_scalar_prefetch=1,
            grid=(1,),
            in_specs=[pl.BlockSpec(memory_space=pl.ANY), pl.BlockSpec(memory_space=pltpu.VMEM)],
            out_specs=[pl.BlockSpec(memory_space=pltpu.VMEM)] * 3,
            scratch_shapes=[
                pltpu.VMEM((2, cap, BLK, heads_kv, row_width), queries.dtype),
                pltpu.SemaphoreType.DMA((2, cap)),
            ],
        ),
        compiler_params=pltpu.CompilerParams(vmem_limit_bytes=60 * 1024 * 1024),
        cost_estimate=pl.CostEstimate(
            flops=0, bytes_accessed=4 * cap * BLK * heads_kv * row_width, transcendentals=0
        ),
        name="collect_slots",
    )(verticals, cache_kv, span_kv)

    def swap(x, bit):
        return lax.ppermute(x, "ctx", [(i, i ^ bit) for i in range(owners)])

    bits = []
    bit = half // 2
    while bit:
        bits.append(bit)
        bit //= 2
    parts = 2 * head_groups
    whole, low, high = (0, cap), (0, split), (split, cap)
    last_bit = bits[-1]
    late = [(True, m | last_bit, low, True) for m in range(1, half) if not m & last_bit]
    places, values = [], []
    state, operands, scalars = [], [q_near, q_far], verticals

    def stage(name, *arrived, slash=False, last=False):
        nonlocal state, operands, scalars
        known, first = len(places), not places
        for far_side, slots, tail, sides in arrived:
            places.extend((far_side, m, slots, tail) for m in sides)
            values.extend(sides.values())
        kind = Stage(
            owners, group, depth, tokens, cache_blocks, parts, list(places), known,
            late if slash or last else [], first, last,
        )
        top, acc, *more = attend(kind, scalars, offsets, operands, values, state, name)
        state = [top, acc]
        if first:
            operands, scalars = [more[0]], more[1]
        return more

    theirs, q_far = lax.optimization_barrier((theirs, q_far))
    operands[1] = q_far
    near = {0: mine}
    far = {0: lax.ppermute(theirs, "ctx", across)}
    rest = {0: lax.ppermute(theirs_rest, "ctx", across)}
    own = swap(mine, last_bit)
    for bit in bits[:-1]:
        near.update({m | bit: swap(x, bit) for m, x in near.items()})
    del near[0]
    forwarded = {m | last_bit: swap(x, last_bit) for m, x in near.items()}
    stage("attend_own", (False, whole, True, {0: mine}))
    first_far, own, state = lax.optimization_barrier((far[0], own, state))
    far_own = swap(first_far, last_bit)
    rest[0], far_own = lax.optimization_barrier((rest[0], far_own))
    stage("attend_near", (False, whole, True, {last_bit: own} | near), (True, low, True, {0: first_far}))
    rest[0], state = lax.optimization_barrier((rest[0], state))
    for bit in bits[:-1]:
        far.update({m | bit: swap(x, bit) for m, x in far.items()})
        rest.update({m | bit: swap(x, bit) for m, x in rest.items()})
    far.pop(0)
    last_far = {m | last_bit: swap(x, last_bit) for m, x in far.items()}
    rest_own = swap(rest[0], last_bit)
    stage("attend_forwarded", (False, whole, True, forwarded), (True, low, True, {last_bit: far_own}))
    first_rest = rest.pop(0)
    last_rest = {m | last_bit: swap(x, last_bit) for m, x in rest.items()}
    stage(
        "attend_far", (True, low, True, far), (True, high, False, {0: first_rest, last_bit: rest_own}),
        (True, high, False, rest), slash=True,
    )
    sent = stage("attend_last", (True, low, True, last_far), (True, high, False, last_rest), last=True)

    def partner(device, k):
        index, lane = divmod(device, head_groups)
        place = (lane * 2 + index // half) ^ k
        return (place % 2 * half + index % half) * head_groups + place // 2

    devices = range(owners * head_groups)
    placed = {0: sent[0]}
    for k in sorted(range(1, parts), key=lambda k: (1 - k % 2, k)):
        placed[k] = lax.ppermute(sent[k], ("ctx", "head"), [(d, partner(d, k)) for d in devices])
    return pl.pallas_call(
        functools.partial(place_kernel, head_groups, half),
        out_shape=jax.ShapeDtypeStruct((tokens // head_groups, parts * columns), queries.dtype),
        in_specs=[pl.BlockSpec(memory_space=pltpu.VMEM)] * parts,
        out_specs=pl.BlockSpec(memory_space=pl.ANY),
        scratch_shapes=[pltpu.SemaphoreType.DMA((parts,))],
        name="place_parts",
    )(*[placed[k] for k in range(parts)])


def solution(mesh):
    in_specs = (
        P("ctx", "head"),
        P("ctx", "head", None),
        P("ctx", "head", None),
        P("head", None),
        P("head", None),
    )
    out_specs = P(("ctx", "head"), None)
    return jax.shard_map(body, mesh=mesh, in_specs=in_specs, out_specs=out_specs, check_vma=False)
```

```python
import functools

import jax
import jax.numpy as jnp
from jax import lax
from jax.experimental import pallas as pl
from jax.experimental.pallas import tpu as pltpu
from jax.sharding import PartitionSpec as P

BLK = 64
NV = 64
MASKED = -1e30
CHUNK = 8
LOG2E = 1.4426950408889634


def collect_kernel(owners, cap, verticals, cache, span, mine, theirs, theirs_rest, raw, sem):
    me = lax.axis_index("ctx")
    upper = me // (owners // 2)
    cache_blocks = cache.shape[0] // BLK
    first = me * cache_blocks

    def block_copy(block, place, slot):
        return pltpu.make_async_copy(
            cache.at[pl.ds(pl.multiple_of(block * BLK, BLK), BLK)], raw.at[place, slot], sem.at[place, slot]
        )

    found = []
    for place in range(2):
        head = upper if place == 0 else 1 - upper

        def visit(n, count):
            block = verticals[head, n] - first
            hit = (block >= 0) & (block < cache_blocks) & (count < cap)

            @pl.when(hit)
            def _():
                block_copy(block, place, count).start()

            return count + hit.astype(jnp.int32)

        found.append(lax.fori_loop(0, NV, visit, jnp.int32(0)))
    split = cap // 2
    for own in range(2):

        @pl.when(upper == own)
        def _():
            mine[cap * BLK :, :] = span[:, own, :]
            theirs[split * BLK :, :] = span[:, 1 - own, :]
            for place, target, start, stop in ((1, theirs, 0, split), (1, theirs_rest, split, cap), (0, mine, 0, cap)):
                head = own if place == 0 else 1 - own

                def unpack(slot, carry):
                    block_copy(0, place, slot).wait()
                    at = pl.ds(pl.multiple_of((slot - start) * BLK, BLK), BLK)
                    target[at, :] = raw[place, slot, :, head, :]
                    return carry

                lax.fori_loop(start, jnp.minimum(found[place], stop), unpack, 0)


class Stage:
    def __init__(self, owners, group, depth, tokens, width, parts, pieces, known, late, first, last):
        self.owners, self.group, self.depth = owners, group, depth
        self.tokens, self.width, self.parts = tokens, width, parts
        self.pieces, self.known, self.late = pieces, known, late
        self.first, self.last = first, last
        self.half = owners // 2
        self.blocks = tokens // BLK
        self.rows = group * BLK
        self.state_rows = 2 * self.blocks * self.rows
        self.slash = bool(late) and not last

    def owner(self, far, m, *_):
        me = lax.axis_index("ctx")
        upper = me // self.half
        return ((1 - upper) if far else upper) * self.half + ((me % self.half) ^ m)


def attend_kernel(stage, scalars, offsets, *refs):
    refs = list(refs)

    def take(count):
        taken, refs[:count] = refs[:count], []
        return taken

    half, blocks, rows, depth, tokens = stage.half, stage.blocks, stage.rows, stage.depth, stage.tokens
    me = lax.axis_index("ctx")
    upper = me // half
    head = upper
    width_kv = 2 * depth
    factor = LOG2E * depth**-0.5
    if stage.first:
        q_near, q_far = take(2)
    else:
        (queries,) = take(1)
    sources = take(len(stage.pieces))
    if stage.first:
        top, acc, queries, counts = take(4)
    else:
        take(2)
        top, acc = take(2)
        counts = scalars
    outs = take(stage.parts) if stage.last else []
    keys, sem = take(2)

    if stage.first:

        def clear(n, carry):
            counts[n] = 0
            return carry

        lax.fori_loop(0, stage.owners, clear, 0)

        def tally(n, carry):
            owner = scalars[head, n] // stage.width
            counts[owner] = counts[owner] + 1
            return carry

        lax.fori_loop(0, NV, tally, 0)

    held = [
        jnp.clip(counts[stage.owner(*piece)] - piece[2][0], 0, piece[2][1] - piece[2][0]) for piece in stage.pieces
    ]
    seen = sum(held[: stage.known], jnp.int32(0))
    present = sum(held[stage.known :], seen)
    begin = seen // CHUNK * CHUNK
    end = jnp.int32(NV) if stage.last else present // CHUNK * CHUNK
    place = jnp.int32(0)
    for source, live in zip(sources, held):

        def fetch(n, carry, place=place, source=source):
            at = place + n - begin
            pltpu.make_async_copy(
                source.at[pl.ds(pl.multiple_of(n * BLK, BLK), BLK)],
                keys.at[pl.ds(pl.multiple_of(at * BLK, BLK), BLK), pl.ds(0, width_kv)],
                sem.at[at // CHUNK],
            ).start()
            return carry

        lax.fori_loop(jnp.clip(begin - place, 0, live), jnp.clip(end - place, 0, live), fetch, 0)
        place = place + live

    span_copies = []
    if stage.slash or stage.last:
        span, bias, span_sem = take(3)
        wanted = stage.late if stage.last else [piece for piece in stage.pieces if piece[3]]
        for n, piece in enumerate(wanted):
            at = n if stage.last else stage.owner(*piece)
            slots = piece[2][1] - piece[2][0]
            copy = pltpu.make_async_copy(
                sources[stage.pieces.index(piece)].at[pl.ds(slots * BLK, tokens)],
                span.at[pl.ds(pl.multiple_of(at * tokens, BLK), tokens), pl.ds(0, width_kv)],
                span_sem,
            )
            copy.start()
            span_copies.append(copy)
    keys[:, width_kv:] = jnp.ones((keys.shape[0], depth), keys.dtype)
    if stage.first:
        for tile in range(2 * blocks):
            q_ref, block = (q_near, tile) if tile < blocks else (q_far, tile - blocks)
            for j in range(stage.group):
                queries[tile * rows + j * BLK : tile * rows + (j + 1) * BLK, :] = q_ref[
                    block * BLK : (block + 1) * BLK, j * depth : (j + 1) * depth
                ]
        top[...] = jnp.full(top.shape, MASKED, jnp.float32)
        acc[...] = jnp.zeros(acc.shape, jnp.float32)

    def fold(at, scores, values):
        old = top[at, :]
        new = jnp.maximum(old, jnp.max(scores, axis=1, keepdims=True))
        wide = jnp.concatenate([new] * (scores.shape[1] // depth), 1)
        weights = jnp.exp2((scores - wide) * factor).astype(jnp.bfloat16)
        keep = jnp.exp2((old - new) * factor)
        top[at, :] = new
        acc[at, :] = acc[at, :] * jnp.concatenate([keep, keep], 1) + jnp.dot(
            weights, values, preferred_element_type=jnp.float32
        )

    def products(at, rows_k):
        return lax.dot_general(
            queries[at, :], rows_k, (((1,), (1,)), ((), ())), preferred_element_type=jnp.float32
        )

    tiles = [slice(tile * rows, (tile + 1) * rows) for tile in range(2 * blocks)]

    def step(c, carry):
        part = pl.ds(pl.multiple_of(c * (CHUNK * BLK), CHUNK * BLK), CHUNK * BLK)
        chunk = keys.at[part, pl.ds(0, width_kv)]
        pltpu.make_async_copy(chunk, chunk, sem.at[c]).wait()
        scores = products(tiles[0], keys[part, :depth])
        for at, following in zip(tiles, tiles[1:] + [None]):
            ahead = products(following, keys[part, :depth]) if following else None
            fold(at, scores, keys[part, depth:])
            scores = ahead
        return carry

    lax.fori_loop(0, (end - begin) // CHUNK, step, 0)

    if span_copies:
        for copy in span_copies:
            copy.wait()
        slash_count = offsets.shape[1]
        q_at = lax.broadcasted_iota(jnp.int32, (BLK, BLK), 0)
        k_at = lax.broadcasted_iota(jnp.int32, (BLK, BLK), 1)
        behind = k_at <= q_at
        late_owners = [stage.owner(*piece) for piece in stage.late]

        def masked(at, tile, rows_k, values):
            scores = products(at, rows_k)
            scores = scores.reshape(stage.group, BLK, rows_k.shape[0]) + bias[tile][None]
            fold(at, scores.reshape(rows, rows_k.shape[0]), values)

        if stage.slash:
            (slash,) = take(1)
            slash[:, :, width_kv:] = jnp.ones((2 * blocks, slash_count * BLK, depth), slash.dtype)
        else:
            span[:, width_kv:] = jnp.ones((span.shape[0], depth), span.dtype)
        for tile, at in enumerate(tiles):
            index = me if tile < blocks else (me + half) % stage.owners
            position = index * blocks + tile % blocks
            if stage.slash:
                for s in range(slash_count):
                    offset = offsets[head, s]
                    block = position - offset
                    here = block >= 0
                    for owner in late_owners:
                        here = here & (block // blocks != owner)
                    start = pl.multiple_of(jnp.where(here, block, position) * BLK, BLK)
                    slash[tile, s * BLK : (s + 1) * BLK, :width_kv] = span[pl.ds(start, BLK), :]
                    allowed = here & ((offset > 0) | behind)
                    bias[tile, :, s * BLK : (s + 1) * BLK] = jnp.where(allowed, 0.0, MASKED)
                masked(at, tile, slash[tile, :, :depth], slash[tile, :, depth:])
            else:
                for n, owner in enumerate(late_owners):
                    for k in range(blocks):
                        distance = position - (owner * blocks + k)
                        chosen = distance == offsets[head, 0]
                        for s in range(1, slash_count):
                            chosen = chosen | (distance == offsets[head, s])
                        allowed = chosen & ((distance > 0) | behind)
                        column = n * tokens + k * BLK
                        bias[tile, :, column : column + BLK] = jnp.where(allowed, 0.0, MASKED)
                masked(at, tile, span[:, :depth], span[:, depth:])

    if stage.last:
        lane = lax.axis_index("head")
        for k, out in enumerate(outs):
            part_rows = out.shape[0]
            token = (lane ^ (k >> 1)) * part_rows
            base = ((k & 1) * blocks + token // BLK) * rows + token % BLK
            for j in range(stage.group):
                at = pl.ds(pl.multiple_of(base + j * BLK, part_rows), part_rows)
                both = acc[at, :]
                out[:, j * depth : (j + 1) * depth] = (both[:, :depth] / both[:, depth:]).astype(out.dtype)


def attend(stage, scalars, offsets, queries, pieces, state, name):
    depth, rows, blocks = stage.depth, stage.state_rows, stage.blocks
    kind = jnp.bfloat16
    held = [jax.ShapeDtypeStruct((rows, depth), jnp.float32), jax.ShapeDtypeStruct((rows, 2 * depth), jnp.float32)]
    vmem, smem = pl.BlockSpec(memory_space=pltpu.VMEM), pl.BlockSpec(memory_space=pltpu.SMEM)
    out_shape, out_specs = list(held), [vmem] * 2
    if stage.first:
        out_shape += [
            jax.ShapeDtypeStruct((rows, depth), kind),
            jax.ShapeDtypeStruct((stage.owners,), jnp.int32),
        ]
        out_specs += [vmem, smem]
    if stage.last:
        part = jax.ShapeDtypeStruct((2 * stage.tokens // stage.parts, stage.group * depth), kind)
        out_shape += [part] * stage.parts
        out_specs += [vmem] * stage.parts
    scratch = [pltpu.VMEM((NV * BLK, 3 * depth), kind), pltpu.SemaphoreType.DMA((NV // CHUNK,))]
    share = sum(piece[3] for piece in stage.pieces[stage.known :]) * NV // stage.owners * BLK
    if stage.slash:
        keys = offsets.shape[1] * BLK
        scratch += [
            pltpu.VMEM((stage.owners * stage.tokens, 2 * depth), kind),
            pltpu.VMEM((2 * blocks, BLK, keys), jnp.float32),
            pltpu.SemaphoreType.DMA,
            pltpu.VMEM((2 * blocks, keys, 3 * depth), kind),
        ]
        share += keys
    elif stage.last:
        keys = len(stage.late) * stage.tokens
        scratch += [
            pltpu.VMEM((keys, 3 * depth), kind),
            pltpu.VMEM((2 * blocks, BLK, keys), jnp.float32),
            pltpu.SemaphoreType.DMA,
        ]
    operands = [scalars, offsets, *queries, *pieces, *state]
    in_specs = [vmem] * len(queries) + [pl.BlockSpec(memory_space=pl.ANY)] * len(pieces) + [vmem] * len(state)
    return pl.pallas_call(
        functools.partial(attend_kernel, stage),
        out_shape=out_shape,
        grid_spec=pltpu.PrefetchScalarGridSpec(
            num_scalar_prefetch=2, grid=(1,), in_specs=in_specs, out_specs=out_specs, scratch_shapes=scratch
        ),
        input_output_aliases={len(operands) - len(state) + n: n for n in range(len(state))},
        compiler_params=pltpu.CompilerParams(vmem_limit_bytes=28 * 1024 * 1024),
        cost_estimate=pl.CostEstimate(
            flops=2 * rows * depth * share // 4, bytes_accessed=share * 4 * depth, transcendentals=0
        ),
        name=name,
    )(*operands)


def place_kernel(head_groups, half, *refs):
    *parts, out, sem = refs
    here = lax.axis_index("head") * 2 + lax.axis_index("ctx") // half
    copies = []
    for k, part in enumerate(parts):
        columns = part.shape[1]
        start = pl.multiple_of((here ^ k) * columns, columns)
        copies.append(pltpu.make_async_copy(part, out.at[:, pl.ds(start, columns)], sem.at[k]))
        copies[-1].start()
    for copy in copies:
        copy.wait()


def body(queries, span_kv, cache_kv, verticals, offsets):
    tokens = queries.shape[0]
    heads_kv, row_width = span_kv.shape[1:]
    depth = row_width // 2
    columns = queries.shape[1] // heads_kv
    group = columns // depth
    owners = lax.axis_size("ctx")
    head_groups = lax.axis_size("head")
    half = owners // 2
    cache_blocks = cache_kv.shape[0] // BLK
    cap = max(2, 2 * NV // owners)
    upper = lax.axis_index("ctx") // half

    across = [(i, (i + half) % owners) for i in range(owners)]
    send_q = lax.dynamic_slice_in_dim(queries, (1 - upper) * columns, columns, 1)
    q_near = lax.dynamic_slice_in_dim(queries, upper * columns, columns, 1)
    q_far = lax.ppermute(send_q, "ctx", across)
    split = cap // 2

    def rows_of(count):
        return jax.ShapeDtypeStruct((count, row_width), queries.dtype)

    mine, theirs, theirs_rest = pl.pallas_call(
        functools.partial(collect_kernel, owners, cap),
        out_shape=(rows_of(cap * BLK + tokens), rows_of(split * BLK + tokens), rows_of((cap - split) * BLK)),
        grid_spec=pltpu.PrefetchScalarGridSpec(
            num_scalar_prefetch=1,
            grid=(1,),
            in_specs=[pl.BlockSpec(memory_space=pl.ANY), pl.BlockSpec(memory_space=pltpu.VMEM)],
            out_specs=[pl.BlockSpec(memory_space=pltpu.VMEM)] * 3,
            scratch_shapes=[
                pltpu.VMEM((2, cap, BLK, heads_kv, row_width), queries.dtype),
                pltpu.SemaphoreType.DMA((2, cap)),
            ],
        ),
        compiler_params=pltpu.CompilerParams(vmem_limit_bytes=60 * 1024 * 1024),
        cost_estimate=pl.CostEstimate(
            flops=0, bytes_accessed=4 * cap * BLK * heads_kv * row_width, transcendentals=0
        ),
        name="collect_slots",
    )(verticals, cache_kv, span_kv)

    def swap(x, bit):
        return lax.ppermute(x, "ctx", [(i, i ^ bit) for i in range(owners)])

    bits = []
    bit = half // 2
    while bit:
        bits.append(bit)
        bit //= 2
    parts = 2 * head_groups
    whole, low, high = (0, cap), (0, split), (split, cap)
    last_bit = bits[-1]
    late = [(True, m | last_bit, low, True) for m in range(1, half) if not m & last_bit]
    places, values = [], []
    state, operands, scalars = [], [q_near, q_far], verticals

    def stage(name, *arrived, slash=False, last=False):
        nonlocal state, operands, scalars
        known, first = len(places), not places
        for far_side, slots, tail, sides in arrived:
            places.extend((far_side, m, slots, tail) for m in sides)
            values.extend(sides.values())
        kind = Stage(
            owners, group, depth, tokens, cache_blocks, parts, list(places), known,
            late if slash or last else [], first, last,
        )
        top, acc, *more = attend(kind, scalars, offsets, operands, values, state, name)
        state = [top, acc]
        if first:
            operands, scalars = [more[0]], more[1]
        return more

    near = {0: mine}
    far = {0: lax.ppermute(theirs, "ctx", across)}
    rest = {0: lax.ppermute(theirs_rest, "ctx", across)}
    own = swap(mine, last_bit)
    for bit in bits[:-1]:
        near.update({m | bit: swap(x, bit) for m, x in near.items()})
    del near[0]
    forwarded = {m | last_bit: swap(x, last_bit) for m, x in near.items()}
    first_far, own, q_far = lax.optimization_barrier((far[0], own, q_far))
    operands[1] = q_far
    far_own = swap(first_far, last_bit)
    stage("attend_near", (False, whole, True, {0: mine, last_bit: own} | near))
    rest[0], far_own, state = lax.optimization_barrier((rest[0], far_own, state))
    for bit in bits[:-1]:
        far.update({m | bit: swap(x, bit) for m, x in far.items()})
        rest.update({m | bit: swap(x, bit) for m, x in rest.items()})
    far.pop(0)
    far, forwarded = lax.optimization_barrier((far, forwarded))
    last_far = {m | last_bit: swap(x, last_bit) for m, x in far.items()}
    rest_own = swap(rest[0], last_bit)
    stage(
        "attend_forwarded", (False, whole, True, forwarded), (True, low, True, {0: first_far, last_bit: far_own})
    )
    first_rest = rest.pop(0)
    last_rest = {m | last_bit: swap(x, last_bit) for m, x in rest.items()}
    stage(
        "attend_far", (True, low, True, far), (True, high, False, {0: first_rest, last_bit: rest_own}),
        (True, high, False, rest), slash=True,
    )
    sent = stage("attend_last", (True, low, True, last_far), (True, high, False, last_rest), last=True)

    def partner(device, k):
        index, lane = divmod(device, head_groups)
        place = (lane * 2 + index // half) ^ k
        return (place % 2 * half + index % half) * head_groups + place // 2

    devices = range(owners * head_groups)
    placed = {0: sent[0]}
    for k in sorted(range(1, parts), key=lambda k: (1 - k % 2, k)):
        placed[k] = lax.ppermute(sent[k], ("ctx", "head"), [(d, partner(d, k)) for d in devices])
    return pl.pallas_call(
        functools.partial(place_kernel, head_groups, half),
        out_shape=jax.ShapeDtypeStruct((tokens // head_groups, parts * columns), queries.dtype),
        in_specs=[pl.BlockSpec(memory_space=pltpu.VMEM)] * parts,
        out_specs=pl.BlockSpec(memory_space=pl.ANY),
        scratch_shapes=[pltpu.SemaphoreType.DMA((parts,))],
        name="place_parts",
    )(*[placed[k] for k in range(parts)])


def solution(mesh):
    in_specs = (
        P("ctx", "head"),
        P("ctx", "head", None),
        P("ctx", "head", None),
        P("head", None),
        P("head", None),
    )
    out_specs = P(("ctx", "head"), None)
    return jax.shard_map(body, mesh=mesh, in_specs=in_specs, out_specs=out_specs, check_vma=False)
```

```python
import functools

import jax
import jax.numpy as jnp
from jax import lax
from jax.experimental import pallas as pl
from jax.experimental.pallas import tpu as pltpu
from jax.sharding import PartitionSpec as P

BLK = 64
NV = 64
MASKED = -1e30
CHUNK = 8
LOG2E = 1.4426950408889634


def collect_kernel(owners, cap, verticals, cache, span, mine, theirs, theirs_rest, raw, sem):
    me = lax.axis_index("ctx")
    upper = me // (owners // 2)
    cache_blocks = cache.shape[0] // BLK
    first = me * cache_blocks

    def block_copy(block, place, slot):
        return pltpu.make_async_copy(
            cache.at[pl.ds(pl.multiple_of(block * BLK, BLK), BLK)], raw.at[place, slot], sem.at[place, slot]
        )

    found = []
    for place in range(2):
        head = upper if place == 0 else 1 - upper

        def visit(n, count):
            block = verticals[head, n] - first
            hit = (block >= 0) & (block < cache_blocks) & (count < cap)

            @pl.when(hit)
            def _():
                block_copy(block, place, count).start()

            return count + hit.astype(jnp.int32)

        found.append(lax.fori_loop(0, NV, visit, jnp.int32(0)))
    split = cap // 2
    for own in range(2):

        @pl.when(upper == own)
        def _():
            mine[cap * BLK :, :] = span[:, own, :]
            theirs[split * BLK :, :] = span[:, 1 - own, :]
            for place, target, start, stop in ((1, theirs, 0, split), (1, theirs_rest, split, cap), (0, mine, 0, cap)):
                head = own if place == 0 else 1 - own

                def unpack(slot, carry):
                    block_copy(0, place, slot).wait()
                    at = pl.ds(pl.multiple_of((slot - start) * BLK, BLK), BLK)
                    target[at, :] = raw[place, slot, :, head, :]
                    return carry

                lax.fori_loop(start, jnp.minimum(found[place], stop), unpack, 0)


class Stage:
    def __init__(self, owners, group, depth, tokens, width, parts, pieces, known, late, first, last):
        self.owners, self.group, self.depth = owners, group, depth
        self.tokens, self.width, self.parts = tokens, width, parts
        self.pieces, self.known, self.late = pieces, known, late
        self.first, self.last = first, last
        self.half = owners // 2
        self.blocks = tokens // BLK
        self.rows = group * BLK
        self.state_rows = 2 * self.blocks * self.rows
        self.slash = bool(late) and not last

    def owner(self, far, m, *_):
        me = lax.axis_index("ctx")
        upper = me // self.half
        return ((1 - upper) if far else upper) * self.half + ((me % self.half) ^ m)


def attend_kernel(stage, scalars, offsets, *refs):
    refs = list(refs)

    def take(count):
        taken, refs[:count] = refs[:count], []
        return taken

    half, blocks, rows, depth, tokens = stage.half, stage.blocks, stage.rows, stage.depth, stage.tokens
    me = lax.axis_index("ctx")
    upper = me // half
    head = upper
    width_kv = 2 * depth
    factor = LOG2E * depth**-0.5
    if stage.first:
        q_near, q_far = take(2)
    else:
        (queries,) = take(1)
    sources = take(len(stage.pieces))
    if stage.first:
        top, acc, queries, counts = take(4)
    else:
        take(2)
        top, acc = take(2)
        counts = scalars
    outs = take(stage.parts) if stage.last else []
    keys, sem = take(2)

    if stage.first:

        def clear(n, carry):
            counts[n] = 0
            return carry

        lax.fori_loop(0, stage.owners, clear, 0)

        def tally(n, carry):
            owner = scalars[head, n] // stage.width
            counts[owner] = counts[owner] + 1
            return carry

        lax.fori_loop(0, NV, tally, 0)

    held = [
        jnp.clip(counts[stage.owner(*piece)] - piece[2][0], 0, piece[2][1] - piece[2][0]) for piece in stage.pieces
    ]
    seen = sum(held[: stage.known], jnp.int32(0))
    present = sum(held[stage.known :], seen)
    begin = seen // CHUNK * CHUNK
    end = jnp.int32(NV) if stage.last else present // CHUNK * CHUNK
    place = jnp.int32(0)
    for source, live in zip(sources, held):

        def fetch(n, carry, place=place, source=source):
            at = place + n - begin
            pltpu.make_async_copy(
                source.at[pl.ds(pl.multiple_of(n * BLK, BLK), BLK)],
                keys.at[pl.ds(pl.multiple_of(at * BLK, BLK), BLK), pl.ds(0, width_kv)],
                sem.at[at // CHUNK],
            ).start()
            return carry

        lax.fori_loop(jnp.clip(begin - place, 0, live), jnp.clip(end - place, 0, live), fetch, 0)
        place = place + live

    span_copies = []
    if stage.slash or stage.last:
        span, bias, span_sem = take(3)
        wanted = stage.late if stage.last else [piece for piece in stage.pieces if piece[3]]
        for n, piece in enumerate(wanted):
            at = n if stage.last else stage.owner(*piece)
            slots = piece[2][1] - piece[2][0]
            copy = pltpu.make_async_copy(
                sources[stage.pieces.index(piece)].at[pl.ds(slots * BLK, tokens)],
                span.at[pl.ds(pl.multiple_of(at * tokens, BLK), tokens), pl.ds(0, width_kv)],
                span_sem,
            )
            copy.start()
            span_copies.append(copy)
    keys[:, width_kv:] = jnp.ones((keys.shape[0], depth), keys.dtype)
    if stage.first:
        for tile in range(2 * blocks):
            q_ref, block = (q_near, tile) if tile < blocks else (q_far, tile - blocks)
            for j in range(stage.group):
                queries[tile * rows + j * BLK : tile * rows + (j + 1) * BLK, :] = q_ref[
                    block * BLK : (block + 1) * BLK, j * depth : (j + 1) * depth
                ]
        top[...] = jnp.full(top.shape, MASKED, jnp.float32)
        acc[...] = jnp.zeros(acc.shape, jnp.float32)

    def fold(at, scores, values):
        old = top[at, :]
        new = jnp.maximum(old, jnp.max(scores, axis=1, keepdims=True))
        wide = jnp.concatenate([new] * (scores.shape[1] // depth), 1)
        weights = jnp.exp2((scores - wide) * factor).astype(jnp.bfloat16)
        keep = jnp.exp2((old - new) * factor)
        top[at, :] = new
        acc[at, :] = acc[at, :] * jnp.concatenate([keep, keep], 1) + jnp.dot(
            weights, values, preferred_element_type=jnp.float32
        )

    def products(at, rows_k):
        return lax.dot_general(
            queries[at, :], rows_k, (((1,), (1,)), ((), ())), preferred_element_type=jnp.float32
        )

    tiles = [slice(tile * rows, (tile + 1) * rows) for tile in range(2 * blocks)]

    def step(c, carry):
        part = pl.ds(pl.multiple_of(c * (CHUNK * BLK), CHUNK * BLK), CHUNK * BLK)
        chunk = keys.at[part, pl.ds(0, width_kv)]
        pltpu.make_async_copy(chunk, chunk, sem.at[c]).wait()
        scores = products(tiles[0], keys[part, :depth])
        for at, following in zip(tiles, tiles[1:] + [None]):
            ahead = products(following, keys[part, :depth]) if following else None
            fold(at, scores, keys[part, depth:])
            scores = ahead
        return carry

    lax.fori_loop(0, (end - begin) // CHUNK, step, 0)

    if span_copies:
        for copy in span_copies:
            copy.wait()
        slash_count = offsets.shape[1]
        q_at = lax.broadcasted_iota(jnp.int32, (BLK, BLK), 0)
        k_at = lax.broadcasted_iota(jnp.int32, (BLK, BLK), 1)
        behind = k_at <= q_at
        late_owners = [stage.owner(*piece) for piece in stage.late]

        def masked(at, tile, rows_k, values):
            scores = products(at, rows_k)
            scores = scores.reshape(stage.group, BLK, rows_k.shape[0]) + bias[tile][None]
            fold(at, scores.reshape(rows, rows_k.shape[0]), values)

        if stage.slash:
            (slash,) = take(1)
            slash[:, :, width_kv:] = jnp.ones((2 * blocks, slash_count * BLK, depth), slash.dtype)
        else:
            span[:, width_kv:] = jnp.ones((span.shape[0], depth), span.dtype)
        for tile, at in enumerate(tiles):
            index = me if tile < blocks else (me + half) % stage.owners
            position = index * blocks + tile % blocks
            if stage.slash:
                for s in range(slash_count):
                    offset = offsets[head, s]
                    block = position - offset
                    here = block >= 0
                    for owner in late_owners:
                        here = here & (block // blocks != owner)
                    start = pl.multiple_of(jnp.where(here, block, position) * BLK, BLK)
                    slash[tile, s * BLK : (s + 1) * BLK, :width_kv] = span[pl.ds(start, BLK), :]
                    allowed = here & ((offset > 0) | behind)
                    bias[tile, :, s * BLK : (s + 1) * BLK] = jnp.where(allowed, 0.0, MASKED)
                masked(at, tile, slash[tile, :, :depth], slash[tile, :, depth:])
            else:
                for n, owner in enumerate(late_owners):
                    for k in range(blocks):
                        distance = position - (owner * blocks + k)
                        chosen = distance == offsets[head, 0]
                        for s in range(1, slash_count):
                            chosen = chosen | (distance == offsets[head, s])
                        allowed = chosen & ((distance > 0) | behind)
                        column = n * tokens + k * BLK
                        bias[tile, :, column : column + BLK] = jnp.where(allowed, 0.0, MASKED)
                masked(at, tile, span[:, :depth], span[:, depth:])

    if stage.last:
        lane = lax.axis_index("head")
        for k, out in enumerate(outs):
            part_rows = out.shape[0]
            token = (lane ^ (k >> 1)) * part_rows
            base = ((k & 1) * blocks + token // BLK) * rows + token % BLK
            for j in range(stage.group):
                at = pl.ds(pl.multiple_of(base + j * BLK, part_rows), part_rows)
                both = acc[at, :]
                out[:, j * depth : (j + 1) * depth] = (both[:, :depth] / both[:, depth:]).astype(out.dtype)


def attend(stage, scalars, offsets, queries, pieces, state, name):
    depth, rows, blocks = stage.depth, stage.state_rows, stage.blocks
    kind = jnp.bfloat16
    held = [jax.ShapeDtypeStruct((rows, depth), jnp.float32), jax.ShapeDtypeStruct((rows, 2 * depth), jnp.float32)]
    vmem, smem = pl.BlockSpec(memory_space=pltpu.VMEM), pl.BlockSpec(memory_space=pltpu.SMEM)
    out_shape, out_specs = list(held), [vmem] * 2
    if stage.first:
        out_shape += [
            jax.ShapeDtypeStruct((rows, depth), kind),
            jax.ShapeDtypeStruct((stage.owners,), jnp.int32),
        ]
        out_specs += [vmem, smem]
    if stage.last:
        part = jax.ShapeDtypeStruct((2 * stage.tokens // stage.parts, stage.group * depth), kind)
        out_shape += [part] * stage.parts
        out_specs += [vmem] * stage.parts
    scratch = [pltpu.VMEM((NV * BLK, 3 * depth), kind), pltpu.SemaphoreType.DMA((NV // CHUNK,))]
    share = sum(piece[3] for piece in stage.pieces[stage.known :]) * NV // stage.owners * BLK
    if stage.slash:
        keys = offsets.shape[1] * BLK
        scratch += [
            pltpu.VMEM((stage.owners * stage.tokens, 2 * depth), kind),
            pltpu.VMEM((2 * blocks, BLK, keys), jnp.float32),
            pltpu.SemaphoreType.DMA,
            pltpu.VMEM((2 * blocks, keys, 3 * depth), kind),
        ]
        share += keys
    elif stage.last:
        keys = len(stage.late) * stage.tokens
        scratch += [
            pltpu.VMEM((keys, 3 * depth), kind),
            pltpu.VMEM((2 * blocks, BLK, keys), jnp.float32),
            pltpu.SemaphoreType.DMA,
        ]
    operands = [scalars, offsets, *queries, *pieces, *state]
    in_specs = [vmem] * len(queries) + [pl.BlockSpec(memory_space=pl.ANY)] * len(pieces) + [vmem] * len(state)
    return pl.pallas_call(
        functools.partial(attend_kernel, stage),
        out_shape=out_shape,
        grid_spec=pltpu.PrefetchScalarGridSpec(
            num_scalar_prefetch=2, grid=(1,), in_specs=in_specs, out_specs=out_specs, scratch_shapes=scratch
        ),
        input_output_aliases={len(operands) - len(state) + n: n for n in range(len(state))},
        compiler_params=pltpu.CompilerParams(vmem_limit_bytes=28 * 1024 * 1024),
        cost_estimate=pl.CostEstimate(
            flops=2 * rows * depth * share // 4, bytes_accessed=share * 4 * depth, transcendentals=0
        ),
        name=name,
    )(*operands)


def place_kernel(head_groups, half, *refs):
    *parts, out, sem = refs
    here = lax.axis_index("head") * 2 + lax.axis_index("ctx") // half
    copies = []
    for k, part in enumerate(parts):
        columns = part.shape[1]
        start = pl.multiple_of((here ^ k) * columns, columns)
        copies.append(pltpu.make_async_copy(part, out.at[:, pl.ds(start, columns)], sem.at[k]))
        copies[-1].start()
    for copy in copies:
        copy.wait()


def body(queries, span_kv, cache_kv, verticals, offsets):
    tokens = queries.shape[0]
    heads_kv, row_width = span_kv.shape[1:]
    depth = row_width // 2
    columns = queries.shape[1] // heads_kv
    group = columns // depth
    owners = lax.axis_size("ctx")
    head_groups = lax.axis_size("head")
    half = owners // 2
    cache_blocks = cache_kv.shape[0] // BLK
    cap = max(2, 2 * NV // owners)
    upper = lax.axis_index("ctx") // half

    across = [(i, (i + half) % owners) for i in range(owners)]
    send_q = lax.dynamic_slice_in_dim(queries, (1 - upper) * columns, columns, 1)
    q_near = lax.dynamic_slice_in_dim(queries, upper * columns, columns, 1)
    q_far = lax.ppermute(send_q, "ctx", across)
    split = cap // 2

    def rows_of(count):
        return jax.ShapeDtypeStruct((count, row_width), queries.dtype)

    mine, theirs, theirs_rest = pl.pallas_call(
        functools.partial(collect_kernel, owners, cap),
        out_shape=(rows_of(cap * BLK + tokens), rows_of(split * BLK + tokens), rows_of((cap - split) * BLK)),
        grid_spec=pltpu.PrefetchScalarGridSpec(
            num_scalar_prefetch=1,
            grid=(1,),
            in_specs=[pl.BlockSpec(memory_space=pl.ANY), pl.BlockSpec(memory_space=pltpu.VMEM)],
            out_specs=[pl.BlockSpec(memory_space=pltpu.VMEM)] * 3,
            scratch_shapes=[
                pltpu.VMEM((2, cap, BLK, heads_kv, row_width), queries.dtype),
                pltpu.SemaphoreType.DMA((2, cap)),
            ],
        ),
        compiler_params=pltpu.CompilerParams(vmem_limit_bytes=60 * 1024 * 1024),
        cost_estimate=pl.CostEstimate(
            flops=0, bytes_accessed=4 * cap * BLK * heads_kv * row_width, transcendentals=0
        ),
        name="collect_slots",
    )(verticals, cache_kv, span_kv)

    def swap(x, bit):
        return lax.ppermute(x, "ctx", [(i, i ^ bit) for i in range(owners)])

    bits = []
    bit = half // 2
    while bit:
        bits.append(bit)
        bit //= 2
    parts = 2 * head_groups
    whole, low, high = (0, cap), (0, split), (split, cap)
    last_bit = bits[-1]
    late = [(True, m | last_bit, low, True) for m in range(1, half) if not m & last_bit]
    places, values = [], []
    state, operands, scalars = [], [q_near, q_far], verticals

    def stage(name, *arrived, slash=False, last=False):
        nonlocal state, operands, scalars
        known, first = len(places), not places
        for far_side, slots, tail, sides in arrived:
            places.extend((far_side, m, slots, tail) for m in sides)
            values.extend(sides.values())
        kind = Stage(
            owners, group, depth, tokens, cache_blocks, parts, list(places), known,
            late if slash or last else [], first, last,
        )
        top, acc, *more = attend(kind, scalars, offsets, operands, values, state, name)
        state = [top, acc]
        if first:
            operands, scalars = [more[0]], more[1]
        return more

    near = {0: mine}
    far = {0: lax.ppermute(theirs, "ctx", across)}
    rest = {0: lax.ppermute(theirs_rest, "ctx", across)}
    own = swap(mine, last_bit)
    for bit in bits[:-1]:
        near.update({m | bit: swap(x, bit) for m, x in near.items()})
    del near[0]
    forwarded = {m | last_bit: swap(x, last_bit) for m, x in near.items()}
    first_far, own = lax.optimization_barrier((far[0], own))
    far_own = swap(first_far, last_bit)
    stage("attend_near", (False, whole, True, {0: mine, last_bit: own} | near))
    rest[0], far_own, state = lax.optimization_barrier((rest[0], far_own, state))
    for bit in bits[:-1]:
        far.update({m | bit: swap(x, bit) for m, x in far.items()})
        rest.update({m | bit: swap(x, bit) for m, x in rest.items()})
    far.pop(0)
    far, forwarded = lax.optimization_barrier((far, forwarded))
    last_far = {m | last_bit: swap(x, last_bit) for m, x in far.items()}
    rest_own = swap(rest[0], last_bit)
    stage(
        "attend_forwarded", (False, whole, True, forwarded), (True, low, True, {0: first_far, last_bit: far_own})
    )
    first_rest = rest.pop(0)
    last_rest = {m | last_bit: swap(x, last_bit) for m, x in rest.items()}
    stage(
        "attend_far", (True, low, True, far), (True, high, False, {0: first_rest, last_bit: rest_own}),
        (True, high, False, rest), slash=True,
    )
    sent = stage("attend_last", (True, low, True, last_far), (True, high, False, last_rest), last=True)

    def partner(device, k):
        index, lane = divmod(device, head_groups)
        place = (lane * 2 + index // half) ^ k
        return (place % 2 * half + index % half) * head_groups + place // 2

    devices = range(owners * head_groups)
    placed = {0: sent[0]}
    for k in sorted(range(1, parts), key=lambda k: (1 - k % 2, k)):
        placed[k] = lax.ppermute(sent[k], ("ctx", "head"), [(d, partner(d, k)) for d in devices])
    return pl.pallas_call(
        functools.partial(place_kernel, head_groups, half),
        out_shape=jax.ShapeDtypeStruct((tokens // head_groups, parts * columns), queries.dtype),
        in_specs=[pl.BlockSpec(memory_space=pltpu.VMEM)] * parts,
        out_specs=pl.BlockSpec(memory_space=pl.ANY),
        scratch_shapes=[pltpu.SemaphoreType.DMA((parts,))],
        name="place_parts",
    )(*[placed[k] for k in range(parts)])


def solution(mesh):
    in_specs = (
        P("ctx", "head"),
        P("ctx", "head", None),
        P("ctx", "head", None),
        P("head", None),
        P("head", None),
    )
    out_specs = P(("ctx", "head"), None)
    return jax.shard_map(body, mesh=mesh, in_specs=in_specs, out_specs=out_specs, check_vma=False)
```

```python
import functools

import jax
import jax.numpy as jnp
from jax import lax
from jax.experimental import pallas as pl
from jax.experimental.pallas import tpu as pltpu
from jax.sharding import PartitionSpec as P

BLK = 64
NV = 64
MASKED = -1e30
CHUNK = 8
LOG2E = 1.4426950408889634


def collect_kernel(owners, cap, verticals, cache, span, mine, theirs, theirs_rest, raw, sem):
    me = lax.axis_index("ctx")
    upper = me // (owners // 2)
    cache_blocks = cache.shape[0] // BLK
    first = me * cache_blocks

    def block_copy(block, place, slot):
        return pltpu.make_async_copy(
            cache.at[pl.ds(pl.multiple_of(block * BLK, BLK), BLK)], raw.at[place, slot], sem.at[place, slot]
        )

    found = []
    for place in range(2):
        head = upper if place == 0 else 1 - upper

        def visit(n, count):
            block = verticals[head, n] - first
            hit = (block >= 0) & (block < cache_blocks) & (count < cap)

            @pl.when(hit)
            def _():
                block_copy(block, place, count).start()

            return count + hit.astype(jnp.int32)

        found.append(lax.fori_loop(0, NV, visit, jnp.int32(0)))
    split = cap // 2
    for own in range(2):

        @pl.when(upper == own)
        def _():
            mine[cap * BLK :, :] = span[:, own, :]
            theirs[split * BLK :, :] = span[:, 1 - own, :]
            for place, target, start, stop in ((1, theirs, 0, split), (1, theirs_rest, split, cap), (0, mine, 0, cap)):
                head = own if place == 0 else 1 - own

                def unpack(slot, carry):
                    block_copy(0, place, slot).wait()
                    at = pl.ds(pl.multiple_of((slot - start) * BLK, BLK), BLK)
                    target[at, :] = raw[place, slot, :, head, :]
                    return carry

                lax.fori_loop(start, jnp.minimum(found[place], stop), unpack, 0)


class Stage:
    def __init__(self, owners, group, depth, tokens, width, parts, pieces, known, late, first, last):
        self.owners, self.group, self.depth = owners, group, depth
        self.tokens, self.width, self.parts = tokens, width, parts
        self.pieces, self.known, self.late = pieces, known, late
        self.first, self.last = first, last
        self.half = owners // 2
        self.blocks = tokens // BLK
        self.rows = group * BLK
        self.state_rows = 2 * self.blocks * self.rows
        self.slash = bool(late) and not last

    def owner(self, far, m, *_):
        me = lax.axis_index("ctx")
        upper = me // self.half
        return ((1 - upper) if far else upper) * self.half + ((me % self.half) ^ m)


def attend_kernel(stage, scalars, offsets, *refs):
    refs = list(refs)

    def take(count):
        taken, refs[:count] = refs[:count], []
        return taken

    half, blocks, rows, depth, tokens = stage.half, stage.blocks, stage.rows, stage.depth, stage.tokens
    me = lax.axis_index("ctx")
    upper = me // half
    head = upper
    width_kv = 2 * depth
    factor = LOG2E * depth**-0.5
    if stage.first:
        q_near, q_far = take(2)
    else:
        (queries,) = take(1)
    sources = take(len(stage.pieces))
    if stage.first:
        top, acc, queries, counts = take(4)
    else:
        take(2)
        top, acc = take(2)
        counts = scalars
    outs = take(stage.parts) if stage.last else []
    keys, sem = take(2)

    if stage.first:

        def clear(n, carry):
            counts[n] = 0
            return carry

        lax.fori_loop(0, stage.owners, clear, 0)

        def tally(n, carry):
            owner = scalars[head, n] // stage.width
            counts[owner] = counts[owner] + 1
            return carry

        lax.fori_loop(0, NV, tally, 0)

    held = [
        jnp.clip(counts[stage.owner(*piece)] - piece[2][0], 0, piece[2][1] - piece[2][0]) for piece in stage.pieces
    ]
    seen = sum(held[: stage.known], jnp.int32(0))
    present = sum(held[stage.known :], seen)
    begin = seen // CHUNK * CHUNK
    end = jnp.int32(NV) if stage.last else present // CHUNK * CHUNK
    place = jnp.int32(0)
    for source, live in zip(sources, held):

        def fetch(n, carry, place=place, source=source):
            at = place + n - begin
            pltpu.make_async_copy(
                source.at[pl.ds(pl.multiple_of(n * BLK, BLK), BLK)],
                keys.at[pl.ds(pl.multiple_of(at * BLK, BLK), BLK), pl.ds(0, width_kv)],
                sem.at[at // CHUNK],
            ).start()
            return carry

        lax.fori_loop(jnp.clip(begin - place, 0, live), jnp.clip(end - place, 0, live), fetch, 0)
        place = place + live

    span_copies = []
    if stage.slash or stage.last:
        span, bias, span_sem = take(3)
        wanted = stage.late if stage.last else [piece for piece in stage.pieces if piece[3]]
        for n, piece in enumerate(wanted):
            at = n if stage.last else stage.owner(*piece)
            slots = piece[2][1] - piece[2][0]
            copy = pltpu.make_async_copy(
                sources[stage.pieces.index(piece)].at[pl.ds(slots * BLK, tokens)],
                span.at[pl.ds(pl.multiple_of(at * tokens, BLK), tokens), pl.ds(0, width_kv)],
                span_sem,
            )
            copy.start()
            span_copies.append(copy)
    keys[:, width_kv:] = jnp.ones((keys.shape[0], depth), keys.dtype)
    if stage.first:
        for tile in range(2 * blocks):
            q_ref, block = (q_near, tile) if tile < blocks else (q_far, tile - blocks)
            for j in range(stage.group):
                queries[tile * rows + j * BLK : tile * rows + (j + 1) * BLK, :] = q_ref[
                    block * BLK : (block + 1) * BLK, j * depth : (j + 1) * depth
                ]
        top[...] = jnp.full(top.shape, MASKED, jnp.float32)
        acc[...] = jnp.zeros(acc.shape, jnp.float32)

    def fold(at, scores, values):
        old = top[at, :]
        new = jnp.maximum(old, jnp.max(scores, axis=1, keepdims=True))
        wide = jnp.concatenate([new] * (scores.shape[1] // depth), 1)
        weights = jnp.exp2((scores - wide) * factor).astype(jnp.bfloat16)
        keep = jnp.exp2((old - new) * factor)
        top[at, :] = new
        acc[at, :] = acc[at, :] * jnp.concatenate([keep, keep], 1) + jnp.dot(
            weights, values, preferred_element_type=jnp.float32
        )

    def products(at, rows_k):
        return lax.dot_general(
            queries[at, :], rows_k, (((1,), (1,)), ((), ())), preferred_element_type=jnp.float32
        )

    tiles = [slice(tile * rows, (tile + 1) * rows) for tile in range(2 * blocks)]

    def step(c, carry):
        part = pl.ds(pl.multiple_of(c * (CHUNK * BLK), CHUNK * BLK), CHUNK * BLK)
        chunk = keys.at[part, pl.ds(0, width_kv)]
        pltpu.make_async_copy(chunk, chunk, sem.at[c]).wait()
        scores = products(tiles[0], keys[part, :depth])
        for at, following in zip(tiles, tiles[1:] + [None]):
            ahead = products(following, keys[part, :depth]) if following else None
            fold(at, scores, keys[part, depth:])
            scores = ahead
        return carry

    lax.fori_loop(0, (end - begin) // CHUNK, step, 0)

    if span_copies:
        for copy in span_copies:
            copy.wait()
        slash_count = offsets.shape[1]
        q_at = lax.broadcasted_iota(jnp.int32, (BLK, BLK), 0)
        k_at = lax.broadcasted_iota(jnp.int32, (BLK, BLK), 1)
        behind = k_at <= q_at
        late_owners = [stage.owner(*piece) for piece in stage.late]

        def masked(at, tile, rows_k, values):
            scores = products(at, rows_k)
            scores = scores.reshape(stage.group, BLK, rows_k.shape[0]) + bias[tile][None]
            fold(at, scores.reshape(rows, rows_k.shape[0]), values)

        if stage.slash:
            (slash,) = take(1)
            slash[:, :, width_kv:] = jnp.ones((2 * blocks, slash_count * BLK, depth), slash.dtype)
        else:
            span[:, width_kv:] = jnp.ones((span.shape[0], depth), span.dtype)
        for tile, at in enumerate(tiles):
            index = me if tile < blocks else (me + half) % stage.owners
            position = index * blocks + tile % blocks
            if stage.slash:
                for s in range(slash_count):
                    offset = offsets[head, s]
                    block = position - offset
                    here = block >= 0
                    for owner in late_owners:
                        here = here & (block // blocks != owner)
                    start = pl.multiple_of(jnp.where(here, block, position) * BLK, BLK)
                    slash[tile, s * BLK : (s + 1) * BLK, :width_kv] = span[pl.ds(start, BLK), :]
                    allowed = here & ((offset > 0) | behind)
                    bias[tile, :, s * BLK : (s + 1) * BLK] = jnp.where(allowed, 0.0, MASKED)
                masked(at, tile, slash[tile, :, :depth], slash[tile, :, depth:])
            else:
                for n, owner in enumerate(late_owners):
                    for k in range(blocks):
                        distance = position - (owner * blocks + k)
                        chosen = distance == offsets[head, 0]
                        for s in range(1, slash_count):
                            chosen = chosen | (distance == offsets[head, s])
                        allowed = chosen & ((distance > 0) | behind)
                        column = n * tokens + k * BLK
                        bias[tile, :, column : column + BLK] = jnp.where(allowed, 0.0, MASKED)
                masked(at, tile, span[:, :depth], span[:, depth:])

    if stage.last:
        lane = lax.axis_index("head")
        for k, out in enumerate(outs):
            part_rows = out.shape[0]
            token = (lane ^ (k >> 1)) * part_rows
            base = ((k & 1) * blocks + token // BLK) * rows + token % BLK
            for j in range(stage.group):
                at = pl.ds(pl.multiple_of(base + j * BLK, part_rows), part_rows)
                both = acc[at, :]
                out[:, j * depth : (j + 1) * depth] = (both[:, :depth] / both[:, depth:]).astype(out.dtype)


def attend(stage, scalars, offsets, queries, pieces, state, name):
    depth, rows, blocks = stage.depth, stage.state_rows, stage.blocks
    kind = jnp.bfloat16
    held = [jax.ShapeDtypeStruct((rows, depth), jnp.float32), jax.ShapeDtypeStruct((rows, 2 * depth), jnp.float32)]
    vmem, smem = pl.BlockSpec(memory_space=pltpu.VMEM), pl.BlockSpec(memory_space=pltpu.SMEM)
    out_shape, out_specs = list(held), [vmem] * 2
    if stage.first:
        out_shape += [
            jax.ShapeDtypeStruct((rows, depth), kind),
            jax.ShapeDtypeStruct((stage.owners,), jnp.int32),
        ]
        out_specs += [vmem, smem]
    if stage.last:
        part = jax.ShapeDtypeStruct((2 * stage.tokens // stage.parts, stage.group * depth), kind)
        out_shape += [part] * stage.parts
        out_specs += [vmem] * stage.parts
    scratch = [pltpu.VMEM((NV * BLK, 3 * depth), kind), pltpu.SemaphoreType.DMA((NV // CHUNK,))]
    share = sum(piece[3] for piece in stage.pieces[stage.known :]) * NV // stage.owners * BLK
    if stage.slash:
        keys = offsets.shape[1] * BLK
        scratch += [
            pltpu.VMEM((stage.owners * stage.tokens, 2 * depth), kind),
            pltpu.VMEM((2 * blocks, BLK, keys), jnp.float32),
            pltpu.SemaphoreType.DMA,
            pltpu.VMEM((2 * blocks, keys, 3 * depth), kind),
        ]
        share += keys
    elif stage.last:
        keys = len(stage.late) * stage.tokens
        scratch += [
            pltpu.VMEM((keys, 3 * depth), kind),
            pltpu.VMEM((2 * blocks, BLK, keys), jnp.float32),
            pltpu.SemaphoreType.DMA,
        ]
    operands = [scalars, offsets, *queries, *pieces, *state]
    in_specs = [vmem] * len(queries) + [pl.BlockSpec(memory_space=pl.ANY)] * len(pieces) + [vmem] * len(state)
    return pl.pallas_call(
        functools.partial(attend_kernel, stage),
        out_shape=out_shape,
        grid_spec=pltpu.PrefetchScalarGridSpec(
            num_scalar_prefetch=2, grid=(1,), in_specs=in_specs, out_specs=out_specs, scratch_shapes=scratch
        ),
        input_output_aliases={len(operands) - len(state) + n: n for n in range(len(state))},
        compiler_params=pltpu.CompilerParams(vmem_limit_bytes=28 * 1024 * 1024),
        cost_estimate=pl.CostEstimate(
            flops=2 * rows * depth * share // 4, bytes_accessed=share * 4 * depth, transcendentals=0
        ),
        name=name,
    )(*operands)


def place_kernel(head_groups, half, *refs):
    *parts, out, sem = refs
    here = lax.axis_index("head") * 2 + lax.axis_index("ctx") // half
    copies = []
    for k, part in enumerate(parts):
        columns = part.shape[1]
        start = pl.multiple_of((here ^ k) * columns, columns)
        copies.append(pltpu.make_async_copy(part, out.at[:, pl.ds(start, columns)], sem.at[k]))
        copies[-1].start()
    for copy in copies:
        copy.wait()


def body(queries, span_kv, cache_kv, verticals, offsets):
    tokens = queries.shape[0]
    heads_kv, row_width = span_kv.shape[1:]
    depth = row_width // 2
    columns = queries.shape[1] // heads_kv
    group = columns // depth
    owners = lax.axis_size("ctx")
    head_groups = lax.axis_size("head")
    half = owners // 2
    cache_blocks = cache_kv.shape[0] // BLK
    cap = max(2, 2 * NV // owners)
    upper = lax.axis_index("ctx") // half

    across = [(i, (i + half) % owners) for i in range(owners)]
    send_q = lax.dynamic_slice_in_dim(queries, (1 - upper) * columns, columns, 1)
    q_near = lax.dynamic_slice_in_dim(queries, upper * columns, columns, 1)
    split = cap // 2

    def rows_of(count):
        return jax.ShapeDtypeStruct((count, row_width), queries.dtype)

    mine, theirs, theirs_rest = pl.pallas_call(
        functools.partial(collect_kernel, owners, cap),
        out_shape=(rows_of(cap * BLK + tokens), rows_of(split * BLK + tokens), rows_of((cap - split) * BLK)),
        grid_spec=pltpu.PrefetchScalarGridSpec(
            num_scalar_prefetch=1,
            grid=(1,),
            in_specs=[pl.BlockSpec(memory_space=pl.ANY), pl.BlockSpec(memory_space=pltpu.VMEM)],
            out_specs=[pl.BlockSpec(memory_space=pltpu.VMEM)] * 3,
            scratch_shapes=[
                pltpu.VMEM((2, cap, BLK, heads_kv, row_width), queries.dtype),
                pltpu.SemaphoreType.DMA((2, cap)),
            ],
        ),
        compiler_params=pltpu.CompilerParams(vmem_limit_bytes=60 * 1024 * 1024),
        cost_estimate=pl.CostEstimate(
            flops=0, bytes_accessed=4 * cap * BLK * heads_kv * row_width, transcendentals=0
        ),
        name="collect_slots",
    )(verticals, cache_kv, span_kv)

    def swap(x, bit):
        return lax.ppermute(x, "ctx", [(i, i ^ bit) for i in range(owners)])

    bits = []
    bit = half // 2
    while bit:
        bits.append(bit)
        bit //= 2
    parts = 2 * head_groups
    whole, low, high = (0, cap), (0, split), (split, cap)
    last_bit = bits[-1]
    late = [(True, m | last_bit, low, True) for m in range(1, half) if not m & last_bit]
    places, values = [], []
    state, operands, scalars = [], [], verticals

    def stage(name, *arrived, slash=False, last=False):
        nonlocal state, operands, scalars
        known, first = len(places), not places
        for far_side, slots, tail, sides in arrived:
            places.extend((far_side, m, slots, tail) for m in sides)
            values.extend(sides.values())
        kind = Stage(
            owners, group, depth, tokens, cache_blocks, parts, list(places), known,
            late if slash or last else [], first, last,
        )
        top, acc, *more = attend(kind, scalars, offsets, operands, values, state, name)
        state = [top, acc]
        if first:
            operands, scalars = [more[0]], more[1]
        return more

    near = {0: mine}
    far = {0: lax.ppermute(theirs, "ctx", across)}
    own = swap(mine, last_bit)
    for bit in bits[:-1]:
        near.update({m | bit: swap(x, bit) for m, x in near.items()})
    del near[0]
    forwarded = {m | last_bit: swap(x, last_bit) for m, x in near.items()}
    far[0], send_q = lax.optimization_barrier((far[0], send_q))
    q_far = lax.ppermute(send_q, "ctx", across)
    theirs_rest, q_far = lax.optimization_barrier((theirs_rest, q_far))
    rest = {0: lax.ppermute(theirs_rest, "ctx", across)}
    operands = [q_near, q_far]
    first_far, own = lax.optimization_barrier((far[0], own))
    far_own = swap(first_far, last_bit)
    stage("attend_near", (False, whole, True, {0: mine, last_bit: own} | near))
    rest[0], far_own, state = lax.optimization_barrier((rest[0], far_own, state))
    for bit in bits[:-1]:
        far.update({m | bit: swap(x, bit) for m, x in far.items()})
        rest.update({m | bit: swap(x, bit) for m, x in rest.items()})
    far.pop(0)
    far, forwarded = lax.optimization_barrier((far, forwarded))
    last_far = {m | last_bit: swap(x, last_bit) for m, x in far.items()}
    rest_own = swap(rest[0], last_bit)
    stage(
        "attend_forwarded", (False, whole, True, forwarded), (True, low, True, {0: first_far, last_bit: far_own})
    )
    first_rest = rest.pop(0)
    last_rest = {m | last_bit: swap(x, last_bit) for m, x in rest.items()}
    stage(
        "attend_far", (True, low, True, far), (True, high, False, {0: first_rest, last_bit: rest_own}),
        (True, high, False, rest), slash=True,
    )
    sent = stage("attend_last", (True, low, True, last_far), (True, high, False, last_rest), last=True)

    def partner(device, k):
        index, lane = divmod(device, head_groups)
        place = (lane * 2 + index // half) ^ k
        return (place % 2 * half + index % half) * head_groups + place // 2

    devices = range(owners * head_groups)
    placed = {0: sent[0]}
    for k in sorted(range(1, parts), key=lambda k: (1 - k % 2, k)):
        placed[k] = lax.ppermute(sent[k], ("ctx", "head"), [(d, partner(d, k)) for d in devices])
    return pl.pallas_call(
        functools.partial(place_kernel, head_groups, half),
        out_shape=jax.ShapeDtypeStruct((tokens // head_groups, parts * columns), queries.dtype),
        in_specs=[pl.BlockSpec(memory_space=pltpu.VMEM)] * parts,
        out_specs=pl.BlockSpec(memory_space=pl.ANY),
        scratch_shapes=[pltpu.SemaphoreType.DMA((parts,))],
        compiler_params=pltpu.CompilerParams(vmem_limit_bytes=8 * 1024 * 1024),
        name="place_parts",
    )(*[placed[k] for k in range(parts)])


def solution(mesh):
    in_specs = (
        P("ctx", "head"),
        P("ctx", "head", None),
        P("ctx", "head", None),
        P("head", None),
        P("head", None),
    )
    out_specs = P(("ctx", "head"), None)
    return jax.shard_map(body, mesh=mesh, in_specs=in_specs, out_specs=out_specs, check_vma=False)
```

```python
import functools

import jax
import jax.numpy as jnp
from jax import lax
from jax.experimental import pallas as pl
from jax.experimental.pallas import tpu as pltpu
from jax.sharding import PartitionSpec as P

BLK = 64
NV = 64
MASKED = -1e30
CHUNK = 8
LOG2E = 1.4426950408889634


def collect_kernel(owners, cap, verticals, cache, span, mine, theirs, theirs_rest, raw, sem):
    me = lax.axis_index("ctx")
    upper = me // (owners // 2)
    cache_blocks = cache.shape[0] // BLK
    first = me * cache_blocks

    def block_copy(block, place, slot):
        return pltpu.make_async_copy(
            cache.at[pl.ds(pl.multiple_of(block * BLK, BLK), BLK)], raw.at[place, slot], sem.at[place, slot]
        )

    found = []
    for place in range(2):
        head = upper if place == 0 else 1 - upper

        def visit(n, count):
            block = verticals[head, n] - first
            hit = (block >= 0) & (block < cache_blocks) & (count < cap)

            @pl.when(hit)
            def _():
                block_copy(block, place, count).start()

            return count + hit.astype(jnp.int32)

        found.append(lax.fori_loop(0, NV, visit, jnp.int32(0)))
    split = cap // 2
    for own in range(2):

        @pl.when(upper == own)
        def _():
            mine[cap * BLK :, :] = span[:, own, :]
            theirs[split * BLK :, :] = span[:, 1 - own, :]
            for place, target, start, stop in ((1, theirs, 0, split), (1, theirs_rest, split, cap), (0, mine, 0, cap)):
                head = own if place == 0 else 1 - own

                def unpack(slot, carry):
                    block_copy(0, place, slot).wait()
                    at = pl.ds(pl.multiple_of((slot - start) * BLK, BLK), BLK)
                    target[at, :] = raw[place, slot, :, head, :]
                    return carry

                lax.fori_loop(start, jnp.minimum(found[place], stop), unpack, 0)


class Stage:
    def __init__(self, owners, group, depth, tokens, width, parts, pieces, known, late, first, last):
        self.owners, self.group, self.depth = owners, group, depth
        self.tokens, self.width, self.parts = tokens, width, parts
        self.pieces, self.known, self.late = pieces, known, late
        self.first, self.last = first, last
        self.half = owners // 2
        self.blocks = tokens // BLK
        self.rows = group * BLK
        self.state_rows = 2 * self.blocks * self.rows
        self.slash = bool(late) and not last

    def owner(self, far, m, *_):
        me = lax.axis_index("ctx")
        upper = me // self.half
        return ((1 - upper) if far else upper) * self.half + ((me % self.half) ^ m)


def attend_kernel(stage, scalars, offsets, *refs):
    refs = list(refs)

    def take(count):
        taken, refs[:count] = refs[:count], []
        return taken

    half, blocks, rows, depth, tokens = stage.half, stage.blocks, stage.rows, stage.depth, stage.tokens
    me = lax.axis_index("ctx")
    upper = me // half
    head = upper
    width_kv = 2 * depth
    factor = LOG2E * depth**-0.5
    if stage.first:
        q_near, q_far = take(2)
    else:
        (queries,) = take(1)
    sources = take(len(stage.pieces))
    if stage.first:
        top, acc, queries, counts = take(4)
    else:
        take(2)
        top, acc = take(2)
        counts = scalars
    outs = take(stage.parts) if stage.last else []
    keys, sem = take(2)

    if stage.first:

        def clear(n, carry):
            counts[n] = 0
            return carry

        lax.fori_loop(0, stage.owners, clear, 0)

        def tally(n, carry):
            owner = scalars[head, n] // stage.width
            counts[owner] = counts[owner] + 1
            return carry

        lax.fori_loop(0, NV, tally, 0)

    held = [
        jnp.clip(counts[stage.owner(*piece)] - piece[2][0], 0, piece[2][1] - piece[2][0]) for piece in stage.pieces
    ]
    seen = sum(held[: stage.known], jnp.int32(0))
    present = sum(held[stage.known :], seen)
    begin = seen // CHUNK * CHUNK
    end = jnp.int32(NV) if stage.last else present // CHUNK * CHUNK
    place = jnp.int32(0)
    for source, live in zip(sources, held):

        def fetch(n, carry, place=place, source=source):
            at = place + n - begin
            pltpu.make_async_copy(
                source.at[pl.ds(pl.multiple_of(n * BLK, BLK), BLK)],
                keys.at[pl.ds(pl.multiple_of(at * BLK, BLK), BLK), pl.ds(0, width_kv)],
                sem.at[at // CHUNK],
            ).start()
            return carry

        lax.fori_loop(jnp.clip(begin - place, 0, live), jnp.clip(end - place, 0, live), fetch, 0)
        place = place + live

    span_copies = []
    if stage.slash or stage.last:
        span, bias, span_sem = take(3)
        wanted = stage.late if stage.last else [piece for piece in stage.pieces if piece[3]]
        for n, piece in enumerate(wanted):
            at = n if stage.last else stage.owner(*piece)
            slots = piece[2][1] - piece[2][0]
            copy = pltpu.make_async_copy(
                sources[stage.pieces.index(piece)].at[pl.ds(slots * BLK, tokens)],
                span.at[pl.ds(pl.multiple_of(at * tokens, BLK), tokens), pl.ds(0, width_kv)],
                span_sem,
            )
            copy.start()
            span_copies.append(copy)
    keys[:, width_kv:] = jnp.ones((keys.shape[0], depth), keys.dtype)
    if stage.first:
        for tile in range(2 * blocks):
            q_ref, block = (q_near, tile) if tile < blocks else (q_far, tile - blocks)
            for j in range(stage.group):
                queries[tile * rows + j * BLK : tile * rows + (j + 1) * BLK, :] = q_ref[
                    block * BLK : (block + 1) * BLK, j * depth : (j + 1) * depth
                ]
        top[...] = jnp.full(top.shape, MASKED, jnp.float32)
        acc[...] = jnp.zeros(acc.shape, jnp.float32)

    def fold(at, scores, values):
        old = top[at, :]
        new = jnp.maximum(old, jnp.max(scores, axis=1, keepdims=True))
        wide = jnp.concatenate([new] * (scores.shape[1] // depth), 1)
        weights = jnp.exp2((scores - wide) * factor).astype(jnp.bfloat16)
        keep = jnp.exp2((old - new) * factor)
        top[at, :] = new
        acc[at, :] = acc[at, :] * jnp.concatenate([keep, keep], 1) + jnp.dot(
            weights, values, preferred_element_type=jnp.float32
        )

    def products(at, rows_k):
        return lax.dot_general(
            queries[at, :], rows_k, (((1,), (1,)), ((), ())), preferred_element_type=jnp.float32
        )

    tiles = [slice(tile * rows, (tile + 1) * rows) for tile in range(2 * blocks)]

    def step(c, carry):
        part = pl.ds(pl.multiple_of(c * (CHUNK * BLK), CHUNK * BLK), CHUNK * BLK)
        chunk = keys.at[part, pl.ds(0, width_kv)]
        pltpu.make_async_copy(chunk, chunk, sem.at[c]).wait()
        scores = products(tiles[0], keys[part, :depth])
        for at, following in zip(tiles, tiles[1:] + [None]):
            ahead = products(following, keys[part, :depth]) if following else None
            fold(at, scores, keys[part, depth:])
            scores = ahead
        return carry

    lax.fori_loop(0, (end - begin) // CHUNK, step, 0)

    if span_copies:
        for copy in span_copies:
            copy.wait()
        slash_count = offsets.shape[1]
        q_at = lax.broadcasted_iota(jnp.int32, (BLK, BLK), 0)
        k_at = lax.broadcasted_iota(jnp.int32, (BLK, BLK), 1)
        behind = k_at <= q_at
        late_owners = [stage.owner(*piece) for piece in stage.late]

        def masked(at, tile, rows_k, values):
            scores = products(at, rows_k)
            scores = scores.reshape(stage.group, BLK, rows_k.shape[0]) + bias[tile][None]
            fold(at, scores.reshape(rows, rows_k.shape[0]), values)

        if stage.slash:
            (slash,) = take(1)
            slash[:, :, width_kv:] = jnp.ones((2 * blocks, slash_count * BLK, depth), slash.dtype)
        else:
            span[:, width_kv:] = jnp.ones((span.shape[0], depth), span.dtype)
        for tile, at in enumerate(tiles):
            index = me if tile < blocks else (me + half) % stage.owners
            position = index * blocks + tile % blocks
            if stage.slash:
                for s in range(slash_count):
                    offset = offsets[head, s]
                    block = position - offset
                    here = block >= 0
                    for owner in late_owners:
                        here = here & (block // blocks != owner)
                    start = pl.multiple_of(jnp.where(here, block, position) * BLK, BLK)
                    slash[tile, s * BLK : (s + 1) * BLK, :width_kv] = span[pl.ds(start, BLK), :]
                    allowed = here & ((offset > 0) | behind)
                    bias[tile, :, s * BLK : (s + 1) * BLK] = jnp.where(allowed, 0.0, MASKED)
                masked(at, tile, slash[tile, :, :depth], slash[tile, :, depth:])
            else:
                for n, owner in enumerate(late_owners):
                    for k in range(blocks):
                        distance = position - (owner * blocks + k)
                        chosen = distance == offsets[head, 0]
                        for s in range(1, slash_count):
                            chosen = chosen | (distance == offsets[head, s])
                        allowed = chosen & ((distance > 0) | behind)
                        column = n * tokens + k * BLK
                        bias[tile, :, column : column + BLK] = jnp.where(allowed, 0.0, MASKED)
                masked(at, tile, span[:, :depth], span[:, depth:])

    if stage.last:
        lane = lax.axis_index("head")
        for k, out in enumerate(outs):
            part_rows = out.shape[0]
            token = (lane ^ (k >> 1)) * part_rows
            base = ((k & 1) * blocks + token // BLK) * rows + token % BLK
            for j in range(stage.group):
                at = pl.ds(pl.multiple_of(base + j * BLK, part_rows), part_rows)
                both = acc[at, :]
                out[:, j * depth : (j + 1) * depth] = (both[:, :depth] / both[:, depth:]).astype(out.dtype)


def attend(stage, scalars, offsets, queries, pieces, state, name):
    depth, rows, blocks = stage.depth, stage.state_rows, stage.blocks
    kind = jnp.bfloat16
    held = [jax.ShapeDtypeStruct((rows, depth), jnp.float32), jax.ShapeDtypeStruct((rows, 2 * depth), jnp.float32)]
    vmem, smem = pl.BlockSpec(memory_space=pltpu.VMEM), pl.BlockSpec(memory_space=pltpu.SMEM)
    out_shape, out_specs = list(held), [vmem] * 2
    if stage.first:
        out_shape += [
            jax.ShapeDtypeStruct((rows, depth), kind),
            jax.ShapeDtypeStruct((stage.owners,), jnp.int32),
        ]
        out_specs += [vmem, smem]
    if stage.last:
        part = jax.ShapeDtypeStruct((2 * stage.tokens // stage.parts, stage.group * depth), kind)
        out_shape += [part] * stage.parts
        out_specs += [vmem] * stage.parts
    scratch = [pltpu.VMEM((NV * BLK, 3 * depth), kind), pltpu.SemaphoreType.DMA((NV // CHUNK,))]
    share = sum(piece[3] for piece in stage.pieces[stage.known :]) * NV // stage.owners * BLK
    if stage.slash:
        keys = offsets.shape[1] * BLK
        scratch += [
            pltpu.VMEM((stage.owners * stage.tokens, 2 * depth), kind),
            pltpu.VMEM((2 * blocks, BLK, keys), jnp.float32),
            pltpu.SemaphoreType.DMA,
            pltpu.VMEM((2 * blocks, keys, 3 * depth), kind),
        ]
        share += keys
    elif stage.last:
        keys = len(stage.late) * stage.tokens
        scratch += [
            pltpu.VMEM((keys, 3 * depth), kind),
            pltpu.VMEM((2 * blocks, BLK, keys), jnp.float32),
            pltpu.SemaphoreType.DMA,
        ]
    operands = [scalars, offsets, *queries, *pieces, *state]
    in_specs = [vmem] * len(queries) + [pl.BlockSpec(memory_space=pl.ANY)] * len(pieces) + [vmem] * len(state)
    return pl.pallas_call(
        functools.partial(attend_kernel, stage),
        out_shape=out_shape,
        grid_spec=pltpu.PrefetchScalarGridSpec(
            num_scalar_prefetch=2, grid=(1,), in_specs=in_specs, out_specs=out_specs, scratch_shapes=scratch
        ),
        input_output_aliases={len(operands) - len(state) + n: n for n in range(len(state))},
        compiler_params=pltpu.CompilerParams(vmem_limit_bytes=28 * 1024 * 1024),
        cost_estimate=pl.CostEstimate(
            flops=8 * rows * depth * share, bytes_accessed=share * 4 * depth, transcendentals=0
        ),
        name=name,
    )(*operands)


def place_kernel(head_groups, half, *refs):
    *parts, out, sem = refs
    here = lax.axis_index("head") * 2 + lax.axis_index("ctx") // half
    copies = []
    for k, part in enumerate(parts):
        columns = part.shape[1]
        start = pl.multiple_of((here ^ k) * columns, columns)
        copies.append(pltpu.make_async_copy(part, out.at[:, pl.ds(start, columns)], sem.at[k]))
        copies[-1].start()
    for copy in copies:
        copy.wait()


def body(queries, span_kv, cache_kv, verticals, offsets):
    tokens = queries.shape[0]
    heads_kv, row_width = span_kv.shape[1:]
    depth = row_width // 2
    columns = queries.shape[1] // heads_kv
    group = columns // depth
    owners = lax.axis_size("ctx")
    head_groups = lax.axis_size("head")
    half = owners // 2
    cache_blocks = cache_kv.shape[0] // BLK
    cap = max(2, 2 * NV // owners)
    upper = lax.axis_index("ctx") // half

    across = [(i, (i + half) % owners) for i in range(owners)]
    send_q = lax.dynamic_slice_in_dim(queries, (1 - upper) * columns, columns, 1)
    q_near = lax.dynamic_slice_in_dim(queries, upper * columns, columns, 1)
    q_far = lax.ppermute(send_q, "ctx", across)
    split = cap // 2

    def rows_of(count):
        return jax.ShapeDtypeStruct((count, row_width), queries.dtype)

    mine, theirs, theirs_rest = pl.pallas_call(
        functools.partial(collect_kernel, owners, cap),
        out_shape=(rows_of(cap * BLK + tokens), rows_of(split * BLK + tokens), rows_of((cap - split) * BLK)),
        grid_spec=pltpu.PrefetchScalarGridSpec(
            num_scalar_prefetch=1,
            grid=(1,),
            in_specs=[pl.BlockSpec(memory_space=pl.ANY), pl.BlockSpec(memory_space=pltpu.VMEM)],
            out_specs=[pl.BlockSpec(memory_space=pltpu.VMEM)] * 3,
            scratch_shapes=[
                pltpu.VMEM((2, cap, BLK, heads_kv, row_width), queries.dtype),
                pltpu.SemaphoreType.DMA((2, cap)),
            ],
        ),
        compiler_params=pltpu.CompilerParams(vmem_limit_bytes=60 * 1024 * 1024),
        cost_estimate=pl.CostEstimate(
            flops=0, bytes_accessed=4 * cap * BLK * heads_kv * row_width, transcendentals=0
        ),
        name="collect_slots",
    )(verticals, cache_kv, span_kv)

    def swap(x, bit):
        return lax.ppermute(x, "ctx", [(i, i ^ bit) for i in range(owners)])

    bits = []
    bit = half // 2
    while bit:
        bits.append(bit)
        bit //= 2
    parts = 2 * head_groups
    whole, low, high = (0, cap), (0, split), (split, cap)
    last_bit = bits[-1]
    late = [(True, m | last_bit, low, True) for m in range(1, half) if not m & last_bit]
    places, values = [], []
    state, operands, scalars = [], [q_near, q_far], verticals

    def stage(name, *arrived, slash=False, last=False):
        nonlocal state, operands, scalars
        known, first = len(places), not places
        for far_side, slots, tail, sides in arrived:
            places.extend((far_side, m, slots, tail) for m in sides)
            values.extend(sides.values())
        kind = Stage(
            owners, group, depth, tokens, cache_blocks, parts, list(places), known,
            late if slash or last else [], first, last,
        )
        top, acc, *more = attend(kind, scalars, offsets, operands, values, state, name)
        state = [top, acc]
        if first:
            operands, scalars = [more[0]], more[1]
        return more

    theirs, q_far = lax.optimization_barrier((theirs, q_far))
    operands[1] = q_far
    near = {0: mine}
    far = {0: lax.ppermute(theirs, "ctx", across)}
    rest = {0: lax.ppermute(theirs_rest, "ctx", across)}
    own = swap(mine, last_bit)
    for bit in bits[:-1]:
        near.update({m | bit: swap(x, bit) for m, x in near.items()})
    del near[0]
    forwarded = {m | last_bit: swap(x, last_bit) for m, x in near.items()}
    stage("attend_own", (False, whole, True, {0: mine}))
    first_far, own, state = lax.optimization_barrier((far[0], own, state))
    far_own = swap(first_far, last_bit)
    rest[0], far_own = lax.optimization_barrier((rest[0], far_own))
    stage("attend_near", (False, whole, True, {last_bit: own} | near), (True, low, True, {0: first_far}))
    rest[0], state = lax.optimization_barrier((rest[0], state))
    for bit in bits[:-1]:
        far.update({m | bit: swap(x, bit) for m, x in far.items()})
        rest.update({m | bit: swap(x, bit) for m, x in rest.items()})
    far.pop(0)
    last_far = {m | last_bit: swap(x, last_bit) for m, x in far.items()}
    rest_own = swap(rest[0], last_bit)
    first_rest = rest.pop(0)
    last_rest = {m | last_bit: swap(x, last_bit) for m, x in rest.items()}
    stage(
        "attend_far", (False, whole, True, forwarded), (True, low, True, {last_bit: far_own} | far),
        (True, high, False, {0: first_rest} | rest), slash=True,
    )
    sent = stage(
        "attend_last", (True, low, True, last_far), (True, high, False, {last_bit: rest_own} | last_rest), last=True
    )

    def partner(device, k):
        index, lane = divmod(device, head_groups)
        place = (lane * 2 + index // half) ^ k
        return (place % 2 * half + index % half) * head_groups + place // 2

    devices = range(owners * head_groups)
    placed = {0: sent[0]}
    for k in sorted(range(1, parts), key=lambda k: (1 - k % 2, k)):
        placed[k] = lax.ppermute(sent[k], ("ctx", "head"), [(d, partner(d, k)) for d in devices])
    return pl.pallas_call(
        functools.partial(place_kernel, head_groups, half),
        out_shape=jax.ShapeDtypeStruct((tokens // head_groups, parts * columns), queries.dtype),
        in_specs=[pl.BlockSpec(memory_space=pltpu.VMEM)] * parts,
        out_specs=pl.BlockSpec(memory_space=pl.ANY),
        scratch_shapes=[pltpu.SemaphoreType.DMA((parts,))],
        compiler_params=pltpu.CompilerParams(vmem_limit_bytes=8 * 1024 * 1024),
        name="place_parts",
    )(*[placed[k] for k in range(parts)])


def solution(mesh):
    in_specs = (
        P("ctx", "head"),
        P("ctx", "head", None),
        P("ctx", "head", None),
        P("head", None),
        P("head", None),
    )
    out_specs = P(("ctx", "head"), None)
    return jax.shard_map(body, mesh=mesh, in_specs=in_specs, out_specs=out_specs, check_vma=False)
```

```python
import functools

import jax
import jax.numpy as jnp
from jax import lax
from jax.experimental import pallas as pl
from jax.experimental.pallas import tpu as pltpu
from jax.sharding import PartitionSpec as P

BLK = 64
NV = 64
MASKED = -1e30
CHUNK = 8
LOG2E = 1.4426950408889634


def collect_kernel(owners, cap, verticals, cache, span, mine, mine_rest, theirs, theirs_rest, raw, sem):
    me = lax.axis_index("ctx")
    upper = me // (owners // 2)
    cache_blocks = cache.shape[0] // BLK
    first = me * cache_blocks

    def block_copy(block, place, slot):
        return pltpu.make_async_copy(
            cache.at[pl.ds(pl.multiple_of(block * BLK, BLK), BLK)], raw.at[place, slot], sem.at[place, slot]
        )

    found = []
    for place in range(2):
        head = upper if place == 0 else 1 - upper

        def visit(n, count):
            block = verticals[head, n] - first
            hit = (block >= 0) & (block < cache_blocks) & (count < cap)

            @pl.when(hit)
            def _():
                block_copy(block, place, count).start()

            return count + hit.astype(jnp.int32)

        found.append(lax.fori_loop(0, NV, visit, jnp.int32(0)))
    split = cap // 2
    for own in range(2):

        @pl.when(upper == own)
        def _():
            mine[split * BLK :, :] = span[:, own, :]
            theirs[split * BLK :, :] = span[:, 1 - own, :]
            for place, target, start, stop in (
                (0, mine, 0, split), (0, mine_rest, split, cap), (1, theirs, 0, split), (1, theirs_rest, split, cap)
            ):
                head = own if place == 0 else 1 - own

                def unpack(slot, carry):
                    block_copy(0, place, slot).wait()
                    at = pl.ds(pl.multiple_of((slot - start) * BLK, BLK), BLK)
                    target[at, :] = raw[place, slot, :, head, :]
                    return carry

                lax.fori_loop(start, jnp.minimum(found[place], stop), unpack, 0)


class Stage:
    def __init__(self, owners, group, depth, tokens, width, parts, pieces, known, late, first, last):
        self.owners, self.group, self.depth = owners, group, depth
        self.tokens, self.width, self.parts = tokens, width, parts
        self.pieces, self.known, self.late = pieces, known, late
        self.first, self.last = first, last
        self.half = owners // 2
        self.blocks = tokens // BLK
        self.rows = group * BLK
        self.state_rows = 2 * self.blocks * self.rows
        self.slash = bool(late) and not last

    def owner(self, far, m, *_):
        me = lax.axis_index("ctx")
        upper = me // self.half
        return ((1 - upper) if far else upper) * self.half + ((me % self.half) ^ m)


def attend_kernel(stage, scalars, offsets, *refs):
    refs = list(refs)

    def take(count):
        taken, refs[:count] = refs[:count], []
        return taken

    half, blocks, rows, depth, tokens = stage.half, stage.blocks, stage.rows, stage.depth, stage.tokens
    me = lax.axis_index("ctx")
    upper = me // half
    head = upper
    width_kv = 2 * depth
    factor = LOG2E * depth**-0.5
    if stage.first:
        q_near, q_far = take(2)
    else:
        (queries,) = take(1)
    sources = take(len(stage.pieces))
    if stage.first:
        top, acc, queries, counts = take(4)
    else:
        take(2)
        top, acc = take(2)
        counts = scalars
    outs = take(stage.parts) if stage.last else []
    keys, sem = take(2)

    if stage.first:

        def clear(n, carry):
            counts[n] = 0
            return carry

        lax.fori_loop(0, stage.owners, clear, 0)

        def tally(n, carry):
            owner = scalars[head, n] // stage.width
            counts[owner] = counts[owner] + 1
            return carry

        lax.fori_loop(0, NV, tally, 0)

    held = [
        jnp.clip(counts[stage.owner(*piece)] - piece[2][0], 0, piece[2][1] - piece[2][0]) for piece in stage.pieces
    ]
    seen = sum(held[: stage.known], jnp.int32(0))
    present = sum(held[stage.known :], seen)
    begin = seen // CHUNK * CHUNK
    end = jnp.int32(NV) if stage.last else present // CHUNK * CHUNK
    place = jnp.int32(0)
    for source, live in zip(sources, held):

        def fetch(n, carry, place=place, source=source):
            at = place + n - begin
            pltpu.make_async_copy(
                source.at[pl.ds(pl.multiple_of(n * BLK, BLK), BLK)],
                keys.at[pl.ds(pl.multiple_of(at * BLK, BLK), BLK), pl.ds(0, width_kv)],
                sem.at[at // CHUNK],
            ).start()
            return carry

        lax.fori_loop(jnp.clip(begin - place, 0, live), jnp.clip(end - place, 0, live), fetch, 0)
        place = place + live

    span_copies = []
    if stage.slash or stage.last:
        span, bias, span_sem = take(3)
        wanted = stage.late if stage.last else [piece for piece in stage.pieces if piece[3]]
        for n, piece in enumerate(wanted):
            at = n if stage.last else stage.owner(*piece)
            slots = piece[2][1] - piece[2][0]
            copy = pltpu.make_async_copy(
                sources[stage.pieces.index(piece)].at[pl.ds(slots * BLK, tokens)],
                span.at[pl.ds(pl.multiple_of(at * tokens, BLK), tokens), pl.ds(0, width_kv)],
                span_sem,
            )
            copy.start()
            span_copies.append(copy)
    keys[:, width_kv:] = jnp.ones((keys.shape[0], depth), keys.dtype)
    if stage.first:
        for tile in range(2 * blocks):
            q_ref, block = (q_near, tile) if tile < blocks else (q_far, tile - blocks)
            for j in range(stage.group):
                queries[tile * rows + j * BLK : tile * rows + (j + 1) * BLK, :] = q_ref[
                    block * BLK : (block + 1) * BLK, j * depth : (j + 1) * depth
                ]
        top[...] = jnp.full(top.shape, MASKED, jnp.float32)
        acc[...] = jnp.zeros(acc.shape, jnp.float32)

    def fold(at, scores, values):
        old = top[at, :]
        new = jnp.maximum(old, jnp.max(scores, axis=1, keepdims=True))
        wide = jnp.concatenate([new] * (scores.shape[1] // depth), 1)
        weights = jnp.exp2((scores - wide) * factor).astype(jnp.bfloat16)
        keep = jnp.exp2((old - new) * factor)
        top[at, :] = new
        acc[at, :] = acc[at, :] * jnp.concatenate([keep, keep], 1) + jnp.dot(
            weights, values, preferred_element_type=jnp.float32
        )

    def products(at, rows_k):
        return lax.dot_general(
            queries[at, :], rows_k, (((1,), (1,)), ((), ())), preferred_element_type=jnp.float32
        )

    tiles = [slice(tile * rows, (tile + 1) * rows) for tile in range(2 * blocks)]

    def step(c, carry):
        part = pl.ds(pl.multiple_of(c * (CHUNK * BLK), CHUNK * BLK), CHUNK * BLK)
        chunk = keys.at[part, pl.ds(0, width_kv)]
        pltpu.make_async_copy(chunk, chunk, sem.at[c]).wait()
        scores = products(tiles[0], keys[part, :depth])
        for at, following in zip(tiles, tiles[1:] + [None]):
            ahead = products(following, keys[part, :depth]) if following else None
            fold(at, scores, keys[part, depth:])
            scores = ahead
        return carry

    lax.fori_loop(0, (end - begin) // CHUNK, step, 0)

    if span_copies:
        for copy in span_copies:
            copy.wait()
        slash_count = offsets.shape[1]
        q_at = lax.broadcasted_iota(jnp.int32, (BLK, BLK), 0)
        k_at = lax.broadcasted_iota(jnp.int32, (BLK, BLK), 1)
        behind = k_at <= q_at
        late_owners = [stage.owner(*piece) for piece in stage.late]

        def masked(at, tile, rows_k, values):
            scores = products(at, rows_k)
            scores = scores.reshape(stage.group, BLK, rows_k.shape[0]) + bias[tile][None]
            fold(at, scores.reshape(rows, rows_k.shape[0]), values)

        if stage.slash:
            (slash,) = take(1)
            slash[:, :, width_kv:] = jnp.ones((2 * blocks, slash_count * BLK, depth), slash.dtype)
        else:
            span[:, width_kv:] = jnp.ones((span.shape[0], depth), span.dtype)
        for tile, at in enumerate(tiles):
            index = me if tile < blocks else (me + half) % stage.owners
            position = index * blocks + tile % blocks
            if stage.slash:
                for s in range(slash_count):
                    offset = offsets[head, s]
                    block = position - offset
                    here = block >= 0
                    for owner in late_owners:
                        here = here & (block // blocks != owner)
                    start = pl.multiple_of(jnp.where(here, block, position) * BLK, BLK)
                    slash[tile, s * BLK : (s + 1) * BLK, :width_kv] = span[pl.ds(start, BLK), :]
                    allowed = here & ((offset > 0) | behind)
                    bias[tile, :, s * BLK : (s + 1) * BLK] = jnp.where(allowed, 0.0, MASKED)
                masked(at, tile, slash[tile, :, :depth], slash[tile, :, depth:])
            else:
                for n, owner in enumerate(late_owners):
                    for k in range(blocks):
                        distance = position - (owner * blocks + k)
                        chosen = distance == offsets[head, 0]
                        for s in range(1, slash_count):
                            chosen = chosen | (distance == offsets[head, s])
                        allowed = chosen & ((distance > 0) | behind)
                        column = n * tokens + k * BLK
                        bias[tile, :, column : column + BLK] = jnp.where(allowed, 0.0, MASKED)
                masked(at, tile, span[:, :depth], span[:, depth:])

    if stage.last:
        lane = lax.axis_index("head")
        for k, out in enumerate(outs):
            part_rows = out.shape[0]
            token = (lane ^ (k >> 1)) * part_rows
            base = ((k & 1) * blocks + token // BLK) * rows + token % BLK
            for j in range(stage.group):
                at = pl.ds(pl.multiple_of(base + j * BLK, part_rows), part_rows)
                both = acc[at, :]
                out[:, j * depth : (j + 1) * depth] = (both[:, :depth] / both[:, depth:]).astype(out.dtype)


def attend(stage, scalars, offsets, queries, pieces, state, name):
    depth, rows, blocks = stage.depth, stage.state_rows, stage.blocks
    kind = jnp.bfloat16
    held = [jax.ShapeDtypeStruct((rows, depth), jnp.float32), jax.ShapeDtypeStruct((rows, 2 * depth), jnp.float32)]
    vmem, smem = pl.BlockSpec(memory_space=pltpu.VMEM), pl.BlockSpec(memory_space=pltpu.SMEM)
    out_shape, out_specs = list(held), [vmem] * 2
    if stage.first:
        out_shape += [
            jax.ShapeDtypeStruct((rows, depth), kind),
            jax.ShapeDtypeStruct((stage.owners,), jnp.int32),
        ]
        out_specs += [vmem, smem]
    if stage.last:
        part = jax.ShapeDtypeStruct((2 * stage.tokens // stage.parts, stage.group * depth), kind)
        out_shape += [part] * stage.parts
        out_specs += [vmem] * stage.parts
    scratch = [pltpu.VMEM((NV * BLK, 3 * depth), kind), pltpu.SemaphoreType.DMA((NV // CHUNK,))]
    share = sum(piece[3] for piece in stage.pieces[stage.known :]) * NV // stage.owners * BLK
    if stage.slash:
        keys = offsets.shape[1] * BLK
        scratch += [
            pltpu.VMEM((stage.owners * stage.tokens, 2 * depth), kind),
            pltpu.VMEM((2 * blocks, BLK, keys), jnp.float32),
            pltpu.SemaphoreType.DMA,
            pltpu.VMEM((2 * blocks, keys, 3 * depth), kind),
        ]
        share += keys
    elif stage.last:
        keys = len(stage.late) * stage.tokens
        scratch += [
            pltpu.VMEM((keys, 3 * depth), kind),
            pltpu.VMEM((2 * blocks, BLK, keys), jnp.float32),
            pltpu.SemaphoreType.DMA,
        ]
    operands = [scalars, offsets, *queries, *pieces, *state]
    in_specs = [vmem] * len(queries) + [pl.BlockSpec(memory_space=pl.ANY)] * len(pieces) + [vmem] * len(state)
    return pl.pallas_call(
        functools.partial(attend_kernel, stage),
        out_shape=out_shape,
        grid_spec=pltpu.PrefetchScalarGridSpec(
            num_scalar_prefetch=2, grid=(1,), in_specs=in_specs, out_specs=out_specs, scratch_shapes=scratch
        ),
        input_output_aliases={len(operands) - len(state) + n: n for n in range(len(state))},
        compiler_params=pltpu.CompilerParams(vmem_limit_bytes=28 * 1024 * 1024),
        cost_estimate=pl.CostEstimate(
            flops=2 * rows * depth * share, bytes_accessed=share * 4 * depth, transcendentals=0
        ),
        name=name,
    )(*operands)


def place_kernel(head_groups, half, *refs):
    *parts, out, sem = refs
    here = lax.axis_index("head") * 2 + lax.axis_index("ctx") // half
    copies = []
    for k, part in enumerate(parts):
        columns = part.shape[1]
        start = pl.multiple_of((here ^ k) * columns, columns)
        copies.append(pltpu.make_async_copy(part, out.at[:, pl.ds(start, columns)], sem.at[k]))
        copies[-1].start()
    for copy in copies:
        copy.wait()


def body(queries, span_kv, cache_kv, verticals, offsets):
    tokens = queries.shape[0]
    heads_kv, row_width = span_kv.shape[1:]
    depth = row_width // 2
    columns = queries.shape[1] // heads_kv
    group = columns // depth
    owners = lax.axis_size("ctx")
    head_groups = lax.axis_size("head")
    half = owners // 2
    cache_blocks = cache_kv.shape[0] // BLK
    cap = max(2, 2 * NV // owners)
    upper = lax.axis_index("ctx") // half

    across = [(i, (i + half) % owners) for i in range(owners)]
    send_q = lax.dynamic_slice_in_dim(queries, (1 - upper) * columns, columns, 1)
    q_near = lax.dynamic_slice_in_dim(queries, upper * columns, columns, 1)
    q_far = lax.ppermute(send_q, "ctx", across)
    split = cap // 2

    def rows_of(count):
        return jax.ShapeDtypeStruct((count, row_width), queries.dtype)

    mine, mine_rest, theirs, theirs_rest = pl.pallas_call(
        functools.partial(collect_kernel, owners, cap),
        out_shape=(rows_of(split * BLK + tokens), rows_of((cap - split) * BLK)) * 2,
        grid_spec=pltpu.PrefetchScalarGridSpec(
            num_scalar_prefetch=1,
            grid=(1,),
            in_specs=[pl.BlockSpec(memory_space=pl.ANY), pl.BlockSpec(memory_space=pltpu.VMEM)],
            out_specs=[pl.BlockSpec(memory_space=pltpu.VMEM)] * 4,
            scratch_shapes=[
                pltpu.VMEM((2, cap, BLK, heads_kv, row_width), queries.dtype),
                pltpu.SemaphoreType.DMA((2, cap)),
            ],
        ),
        compiler_params=pltpu.CompilerParams(vmem_limit_bytes=60 * 1024 * 1024),
        cost_estimate=pl.CostEstimate(
            flops=0, bytes_accessed=4 * cap * BLK * heads_kv * row_width, transcendentals=0
        ),
        name="collect_slots",
    )(verticals, cache_kv, span_kv)

    def swap(x, bit):
        return lax.ppermute(x, "ctx", [(i, i ^ bit) for i in range(owners)])

    bits = []
    bit = half // 2
    while bit:
        bits.append(bit)
        bit //= 2
    parts = 2 * head_groups
    low, high = (0, split), (split, cap)
    last_bit = bits[-1]
    late = [(True, m | last_bit, low, True) for m in range(1, half) if not m & last_bit]
    places, values = [], []
    state, operands, scalars = [], [q_near, q_far], verticals

    def stage(name, *arrived, slash=False, last=False):
        nonlocal state, operands, scalars
        known, first = len(places), not places
        for far_side, slots, tail, sides in arrived:
            places.extend((far_side, m, slots, tail) for m in sides)
            values.extend(sides.values())
        kind = Stage(
            owners, group, depth, tokens, cache_blocks, parts, list(places), known,
            late if slash or last else [], first, last,
        )
        top, acc, *more = attend(kind, scalars, offsets, operands, values, state, name)
        state = [top, acc]
        if first:
            operands, scalars = [more[0]], more[1]
        return more

    theirs, q_far = lax.optimization_barrier((theirs, q_far))
    operands[1] = q_far
    near, near_rest = {0: mine}, {0: mine_rest}
    far = {0: lax.ppermute(theirs, "ctx", across)}
    rest = {0: lax.ppermute(theirs_rest, "ctx", across)}
    own, own_rest = swap(mine, last_bit), swap(mine_rest, last_bit)
    for bit in bits[:-1]:
        near.update({m | bit: swap(x, bit) for m, x in near.items()})
        near_rest.update({m | bit: swap(x, bit) for m, x in near_rest.items()})
    del near[0], near_rest[0]
    forwarded = {m | last_bit: swap(x, last_bit) for m, x in near.items()}
    forwarded_rest = {m | last_bit: swap(x, last_bit) for m, x in near_rest.items()}
    stage("attend_own", (False, low, True, {0: mine}), (False, high, False, {0: mine_rest}))
    first_far, own, own_rest, state = lax.optimization_barrier((far[0], own, own_rest, state))
    far_own = swap(first_far, last_bit)
    rest[0], far_own = lax.optimization_barrier((rest[0], far_own))
    stage(
        "attend_near", (False, low, True, {last_bit: own} | near | forwarded),
        (False, high, False, {last_bit: own_rest} | near_rest | forwarded_rest), (True, low, True, {0: first_far}),
    )
    rest[0], state = lax.optimization_barrier((rest[0], state))
    for bit in bits[:-1]:
        far.update({m | bit: swap(x, bit) for m, x in far.items()})
        rest.update({m | bit: swap(x, bit) for m, x in rest.items()})
    far.pop(0)
    last_far = {m | last_bit: swap(x, last_bit) for m, x in far.items()}
    rest_own = swap(rest[0], last_bit)
    first_rest = rest.pop(0)
    last_rest = {m | last_bit: swap(x, last_bit) for m, x in rest.items()}
    stage(
        "attend_far", (True, low, True, {last_bit: far_own} | far), (True, high, False, {0: first_rest} | rest),
        slash=True,
    )
    sent = stage(
        "attend_last", (True, low, True, last_far), (True, high, False, {last_bit: rest_own} | last_rest), last=True
    )

    def partner(device, k):
        index, lane = divmod(device, head_groups)
        place = (lane * 2 + index // half) ^ k
        return (place % 2 * half + index % half) * head_groups + place // 2

    devices = range(owners * head_groups)
    placed = {0: sent[0]}
    for k in sorted(range(1, parts), key=lambda k: (1 - k % 2, k)):
        placed[k] = lax.ppermute(sent[k], ("ctx", "head"), [(d, partner(d, k)) for d in devices])
    return pl.pallas_call(
        functools.partial(place_kernel, head_groups, half),
        out_shape=jax.ShapeDtypeStruct((tokens // head_groups, parts * columns), queries.dtype),
        in_specs=[pl.BlockSpec(memory_space=pltpu.VMEM)] * parts,
        out_specs=pl.BlockSpec(memory_space=pl.ANY),
        scratch_shapes=[pltpu.SemaphoreType.DMA((parts,))],
        compiler_params=pltpu.CompilerParams(vmem_limit_bytes=8 * 1024 * 1024),
        name="place_parts",
    )(*[placed[k] for k in range(parts)])


def solution(mesh):
    in_specs = (
        P("ctx", "head"),
        P("ctx", "head", None),
        P("ctx", "head", None),
        P("head", None),
        P("head", None),
    )
    out_specs = P(("ctx", "head"), None)
    return jax.shard_map(body, mesh=mesh, in_specs=in_specs, out_specs=out_specs, check_vma=False)
```

```python
import functools

import jax
import jax.numpy as jnp
from jax import lax
from jax.experimental import pallas as pl
from jax.experimental.pallas import tpu as pltpu
from jax.sharding import PartitionSpec as P

BLK = 64
NV = 64
MASKED = -1e30
CHUNK = 8
LOG2E = 1.4426950408889634


def collect_kernel(owners, cap, verticals, cache, span, mine, theirs, theirs_rest, raw, sem):
    me = lax.axis_index("ctx")
    upper = me // (owners // 2)
    cache_blocks = cache.shape[0] // BLK
    first = me * cache_blocks

    def block_copy(block, place, slot):
        return pltpu.make_async_copy(
            cache.at[pl.ds(pl.multiple_of(block * BLK, BLK), BLK)], raw.at[place, slot], sem.at[place, slot]
        )

    found = []
    for place in range(2):
        head = upper if place == 0 else 1 - upper

        def visit(n, count):
            block = verticals[head, n] - first
            hit = (block >= 0) & (block < cache_blocks) & (count < cap)

            @pl.when(hit)
            def _():
                block_copy(block, place, count).start()

            return count + hit.astype(jnp.int32)

        found.append(lax.fori_loop(0, NV, visit, jnp.int32(0)))
    split = cap // 2
    for own in range(2):

        @pl.when(upper == own)
        def _():
            mine[cap * BLK :, :] = span[:, own, :]
            theirs[split * BLK :, :] = span[:, 1 - own, :]
            for place, target, start, stop in ((1, theirs, 0, split), (1, theirs_rest, split, cap), (0, mine, 0, cap)):
                head = own if place == 0 else 1 - own

                def unpack(slot, carry):
                    block_copy(0, place, slot).wait()
                    at = pl.ds(pl.multiple_of((slot - start) * BLK, BLK), BLK)
                    target[at, :] = raw[place, slot, :, head, :]
                    return carry

                lax.fori_loop(start, jnp.minimum(found[place], stop), unpack, 0)


class Stage:
    def __init__(self, owners, group, depth, tokens, width, parts, pieces, known, late, first, slash, tail, last):
        self.owners, self.group, self.depth = owners, group, depth
        self.tokens, self.width, self.parts = tokens, width, parts
        self.pieces, self.known, self.late = pieces, known, late
        self.first, self.slash, self.tail, self.last = first, slash, tail, last
        self.half = owners // 2
        self.blocks = tokens // BLK
        self.rows = group * BLK
        self.state_rows = 2 * self.blocks * self.rows

    def owner(self, far, m, *_):
        me = lax.axis_index("ctx")
        upper = me // self.half
        return ((1 - upper) if far else upper) * self.half + ((me % self.half) ^ m)


def attend_kernel(stage, scalars, offsets, *refs):
    refs = list(refs)

    def take(count):
        taken, refs[:count] = refs[:count], []
        return taken

    half, blocks, rows, depth, tokens = stage.half, stage.blocks, stage.rows, stage.depth, stage.tokens
    me = lax.axis_index("ctx")
    upper = me // half
    head = upper
    width_kv = 2 * depth
    factor = LOG2E * depth**-0.5
    if stage.first:
        q_near, q_far = take(2)
    else:
        (queries,) = take(1)
    sources = take(len(stage.pieces))
    if stage.first:
        top, acc, queries, counts = take(4)
    else:
        take(2)
        top, acc = take(2)
        counts = scalars
    outs = take(stage.parts) if stage.last else []
    keys, sem = take(2)

    if stage.first:

        def clear(n, carry):
            counts[n] = 0
            return carry

        lax.fori_loop(0, stage.owners, clear, 0)

        def tally(n, carry):
            owner = scalars[head, n] // stage.width
            counts[owner] = counts[owner] + 1
            return carry

        lax.fori_loop(0, NV, tally, 0)

    held = [
        jnp.clip(counts[stage.owner(*piece)] - piece[2][0], 0, piece[2][1] - piece[2][0]) for piece in stage.pieces
    ]
    seen = sum(held[: stage.known], jnp.int32(0))
    present = sum(held[stage.known :], seen)
    begin = seen // CHUNK * CHUNK
    end = jnp.int32(NV) if stage.last else present // CHUNK * CHUNK
    place = jnp.int32(0)
    for source, live in zip(sources, held):

        def fetch(n, carry, place=place, source=source):
            at = place + n - begin
            pltpu.make_async_copy(
                source.at[pl.ds(pl.multiple_of(n * BLK, BLK), BLK)],
                keys.at[pl.ds(pl.multiple_of(at * BLK, BLK), BLK), pl.ds(0, width_kv)],
                sem.at[at // CHUNK],
            ).start()
            return carry

        lax.fori_loop(jnp.clip(begin - place, 0, live), jnp.clip(end - place, 0, live), fetch, 0)
        place = place + live

    span_copies = []
    if stage.slash or stage.tail:
        span, bias, span_sem = take(3)
        wanted = stage.late if stage.tail else [piece for piece in stage.pieces if piece[3]]
        for n, piece in enumerate(wanted):
            at = n if stage.tail else stage.owner(*piece)
            slots = piece[2][1] - piece[2][0]
            copy = pltpu.make_async_copy(
                sources[stage.pieces.index(piece)].at[pl.ds(slots * BLK, tokens)],
                span.at[pl.ds(pl.multiple_of(at * tokens, BLK), tokens), pl.ds(0, width_kv)],
                span_sem,
            )
            copy.start()
            span_copies.append(copy)
    keys[:, width_kv:] = jnp.ones((keys.shape[0], depth), keys.dtype)
    if stage.first:
        for tile in range(2 * blocks):
            q_ref, block = (q_near, tile) if tile < blocks else (q_far, tile - blocks)
            for j in range(stage.group):
                queries[tile * rows + j * BLK : tile * rows + (j + 1) * BLK, :] = q_ref[
                    block * BLK : (block + 1) * BLK, j * depth : (j + 1) * depth
                ]
        top[...] = jnp.full(top.shape, MASKED, jnp.float32)
        acc[...] = jnp.zeros(acc.shape, jnp.float32)

    def fold(at, scores, values):
        old = top[at, :]
        new = jnp.maximum(old, jnp.max(scores, axis=1, keepdims=True))
        wide = jnp.concatenate([new] * (scores.shape[1] // depth), 1)
        weights = jnp.exp2((scores - wide) * factor).astype(jnp.bfloat16)
        keep = jnp.exp2((old - new) * factor)
        top[at, :] = new
        acc[at, :] = acc[at, :] * jnp.concatenate([keep, keep], 1) + jnp.dot(
            weights, values, preferred_element_type=jnp.float32
        )

    def products(at, rows_k):
        return lax.dot_general(
            queries[at, :], rows_k, (((1,), (1,)), ((), ())), preferred_element_type=jnp.float32
        )

    tiles = [slice(tile * rows, (tile + 1) * rows) for tile in range(2 * blocks)]

    def step(c, carry):
        part = pl.ds(pl.multiple_of(c * (CHUNK * BLK), CHUNK * BLK), CHUNK * BLK)
        chunk = keys.at[part, pl.ds(0, width_kv)]
        pltpu.make_async_copy(chunk, chunk, sem.at[c]).wait()
        scores = products(tiles[0], keys[part, :depth])
        for at, following in zip(tiles, tiles[1:] + [None]):
            ahead = products(following, keys[part, :depth]) if following else None
            fold(at, scores, keys[part, depth:])
            scores = ahead
        return carry

    lax.fori_loop(0, (end - begin) // CHUNK, step, 0)

    if span_copies:
        for copy in span_copies:
            copy.wait()
        slash_count = offsets.shape[1]
        q_at = lax.broadcasted_iota(jnp.int32, (BLK, BLK), 0)
        k_at = lax.broadcasted_iota(jnp.int32, (BLK, BLK), 1)
        behind = k_at <= q_at
        late_owners = [stage.owner(*piece) for piece in stage.late]

        def masked(at, tile, rows_k, values):
            scores = products(at, rows_k)
            scores = scores.reshape(stage.group, BLK, rows_k.shape[0]) + bias[tile][None]
            fold(at, scores.reshape(rows, rows_k.shape[0]), values)

        if stage.slash:
            (slash,) = take(1)
            slash[:, :, width_kv:] = jnp.ones((2 * blocks, slash_count * BLK, depth), slash.dtype)
        else:
            span[:, width_kv:] = jnp.ones((span.shape[0], depth), span.dtype)
        for tile, at in enumerate(tiles):
            index = me if tile < blocks else (me + half) % stage.owners
            position = index * blocks + tile % blocks
            if stage.slash:
                for s in range(slash_count):
                    offset = offsets[head, s]
                    block = position - offset
                    here = block >= 0
                    for owner in late_owners:
                        here = here & (block // blocks != owner)
                    start = pl.multiple_of(jnp.where(here, block, position) * BLK, BLK)
                    slash[tile, s * BLK : (s + 1) * BLK, :width_kv] = span[pl.ds(start, BLK), :]
                    allowed = here & ((offset > 0) | behind)
                    bias[tile, :, s * BLK : (s + 1) * BLK] = jnp.where(allowed, 0.0, MASKED)
                masked(at, tile, slash[tile, :, :depth], slash[tile, :, depth:])
            else:
                for n, owner in enumerate(late_owners):
                    for k in range(blocks):
                        distance = position - (owner * blocks + k)
                        chosen = distance == offsets[head, 0]
                        for s in range(1, slash_count):
                            chosen = chosen | (distance == offsets[head, s])
                        allowed = chosen & ((distance > 0) | behind)
                        column = n * tokens + k * BLK
                        bias[tile, :, column : column + BLK] = jnp.where(allowed, 0.0, MASKED)
                masked(at, tile, span[:, :depth], span[:, depth:])

    if stage.last:
        lane = lax.axis_index("head")
        for k, out in enumerate(outs):
            part_rows = out.shape[0]
            token = (lane ^ (k >> 1)) * part_rows
            base = ((k & 1) * blocks + token // BLK) * rows + token % BLK
            for j in range(stage.group):
                at = pl.ds(pl.multiple_of(base + j * BLK, part_rows), part_rows)
                both = acc[at, :]
                out[:, j * depth : (j + 1) * depth] = (both[:, :depth] / both[:, depth:]).astype(out.dtype)


def attend(stage, scalars, offsets, queries, pieces, state, name):
    depth, rows, blocks = stage.depth, stage.state_rows, stage.blocks
    kind = jnp.bfloat16
    held = [jax.ShapeDtypeStruct((rows, depth), jnp.float32), jax.ShapeDtypeStruct((rows, 2 * depth), jnp.float32)]
    vmem, smem = pl.BlockSpec(memory_space=pltpu.VMEM), pl.BlockSpec(memory_space=pltpu.SMEM)
    out_shape, out_specs = list(held), [vmem] * 2
    if stage.first:
        out_shape += [
            jax.ShapeDtypeStruct((rows, depth), kind),
            jax.ShapeDtypeStruct((stage.owners,), jnp.int32),
        ]
        out_specs += [vmem, smem]
    if stage.last:
        part = jax.ShapeDtypeStruct((2 * stage.tokens // stage.parts, stage.group * depth), kind)
        out_shape += [part] * stage.parts
        out_specs += [vmem] * stage.parts
    scratch = [pltpu.VMEM((NV * BLK, 3 * depth), kind), pltpu.SemaphoreType.DMA((NV // CHUNK,))]
    share = sum(piece[3] for piece in stage.pieces[stage.known :]) * NV // stage.owners * BLK
    if stage.slash:
        keys = offsets.shape[1] * BLK
        scratch += [
            pltpu.VMEM((stage.owners * stage.tokens, 2 * depth), kind),
            pltpu.VMEM((2 * blocks, BLK, keys), jnp.float32),
            pltpu.SemaphoreType.DMA,
            pltpu.VMEM((2 * blocks, keys, 3 * depth), kind),
        ]
        share += keys
    elif stage.tail:
        keys = len(stage.late) * stage.tokens
        scratch += [
            pltpu.VMEM((keys, 3 * depth), kind),
            pltpu.VMEM((2 * blocks, BLK, keys), jnp.float32),
            pltpu.SemaphoreType.DMA,
        ]
    operands = [scalars, offsets, *queries, *pieces, *state]
    in_specs = [vmem] * len(queries) + [pl.BlockSpec(memory_space=pl.ANY)] * len(pieces) + [vmem] * len(state)
    return pl.pallas_call(
        functools.partial(attend_kernel, stage),
        out_shape=out_shape,
        grid_spec=pltpu.PrefetchScalarGridSpec(
            num_scalar_prefetch=2, grid=(1,), in_specs=in_specs, out_specs=out_specs, scratch_shapes=scratch
        ),
        input_output_aliases={len(operands) - len(state) + n: n for n in range(len(state))},
        compiler_params=pltpu.CompilerParams(vmem_limit_bytes=28 * 1024 * 1024),
        cost_estimate=pl.CostEstimate(
            flops=2 * rows * depth * share, bytes_accessed=share * 4 * depth, transcendentals=0
        ),
        name=name,
    )(*operands)


def place_kernel(head_groups, half, *refs):
    *parts, out, sem = refs
    here = lax.axis_index("head") * 2 + lax.axis_index("ctx") // half
    copies = []
    for k, part in enumerate(parts):
        columns = part.shape[1]
        start = pl.multiple_of((here ^ k) * columns, columns)
        copies.append(pltpu.make_async_copy(part, out.at[:, pl.ds(start, columns)], sem.at[k]))
        copies[-1].start()
    for copy in copies:
        copy.wait()


def body(queries, span_kv, cache_kv, verticals, offsets):
    tokens = queries.shape[0]
    heads_kv, row_width = span_kv.shape[1:]
    depth = row_width // 2
    columns = queries.shape[1] // heads_kv
    group = columns // depth
    owners = lax.axis_size("ctx")
    head_groups = lax.axis_size("head")
    half = owners // 2
    cache_blocks = cache_kv.shape[0] // BLK
    cap = max(2, 2 * NV // owners)
    upper = lax.axis_index("ctx") // half

    across = [(i, (i + half) % owners) for i in range(owners)]
    send_q = lax.dynamic_slice_in_dim(queries, (1 - upper) * columns, columns, 1)
    q_near = lax.dynamic_slice_in_dim(queries, upper * columns, columns, 1)
    q_far = lax.ppermute(send_q, "ctx", across)
    split = cap // 2

    def rows_of(count):
        return jax.ShapeDtypeStruct((count, row_width), queries.dtype)

    mine, theirs, theirs_rest = pl.pallas_call(
        functools.partial(collect_kernel, owners, cap),
        out_shape=(rows_of(cap * BLK + tokens), rows_of(split * BLK + tokens), rows_of((cap - split) * BLK)),
        grid_spec=pltpu.PrefetchScalarGridSpec(
            num_scalar_prefetch=1,
            grid=(1,),
            in_specs=[pl.BlockSpec(memory_space=pl.ANY), pl.BlockSpec(memory_space=pltpu.VMEM)],
            out_specs=[pl.BlockSpec(memory_space=pltpu.VMEM)] * 3,
            scratch_shapes=[
                pltpu.VMEM((2, cap, BLK, heads_kv, row_width), queries.dtype),
                pltpu.SemaphoreType.DMA((2, cap)),
            ],
        ),
        compiler_params=pltpu.CompilerParams(vmem_limit_bytes=60 * 1024 * 1024),
        cost_estimate=pl.CostEstimate(
            flops=0, bytes_accessed=4 * cap * BLK * heads_kv * row_width, transcendentals=0
        ),
        name="collect_slots",
    )(verticals, cache_kv, span_kv)

    def swap(x, bit):
        return lax.ppermute(x, "ctx", [(i, i ^ bit) for i in range(owners)])

    bits = []
    bit = half // 2
    while bit:
        bits.append(bit)
        bit //= 2
    parts = 2 * head_groups
    whole, low, high = (0, cap), (0, split), (split, cap)
    last_bit = bits[-1]
    late = [(True, m | last_bit, low, True) for m in range(1, half) if not m & last_bit]
    places, values = [], []
    state, operands, scalars = [], [q_near, q_far], verticals

    def stage(name, *arrived, slash=False, late_span=False, last=False):
        nonlocal state, operands, scalars
        known, first = len(places), not places
        for far_side, slots, tail, sides in arrived:
            places.extend((far_side, m, slots, tail) for m in sides)
            values.extend(sides.values())
        kind = Stage(
            owners, group, depth, tokens, cache_blocks, parts, list(places), known,
            late if slash or late_span else [], first, slash, late_span, last,
        )
        top, acc, *more = attend(kind, scalars, offsets, operands, values, state, name)
        state = [top, acc]
        if first:
            operands, scalars = [more[0]], more[1]
        return more

    theirs, q_far = lax.optimization_barrier((theirs, q_far))
    operands[1] = q_far
    near = {0: mine}
    far = {0: lax.ppermute(theirs, "ctx", across)}
    rest = {0: lax.ppermute(theirs_rest, "ctx", across)}
    own = swap(mine, last_bit)
    for bit in bits[:-1]:
        near.update({m | bit: swap(x, bit) for m, x in near.items()})
    del near[0]
    forwarded = {m | last_bit: swap(x, last_bit) for m, x in near.items()}
    stage("attend_own", (False, whole, True, {0: mine}))
    first_far, own, state = lax.optimization_barrier((far[0], own, state))
    far_own = swap(first_far, last_bit)
    rest[0], far_own = lax.optimization_barrier((rest[0], far_own))
    stage("attend_near", (False, whole, True, {last_bit: own} | near), (True, low, True, {0: first_far}))
    rest[0], state = lax.optimization_barrier((rest[0], state))
    for bit in bits[:-1]:
        far.update({m | bit: swap(x, bit) for m, x in far.items()})
        rest.update({m | bit: swap(x, bit) for m, x in rest.items()})
    far.pop(0)
    last_far = {m | last_bit: swap(x, last_bit) for m, x in far.items()}
    rest_own = swap(rest[0], last_bit)
    first_rest = rest.pop(0)
    last_rest = {m | last_bit: swap(x, last_bit) for m, x in rest.items()}
    stage(
        "attend_far", (False, whole, True, forwarded), (True, low, True, {last_bit: far_own} | far),
        (True, high, False, {0: first_rest} | rest), slash=True,
    )
    stage("attend_tail", (True, low, True, last_far), (True, high, False, {last_bit: rest_own}), late_span=True)
    sent = stage("attend_last", (True, high, False, last_rest), last=True)

    def partner(device, k):
        index, lane = divmod(device, head_groups)
        place = (lane * 2 + index // half) ^ k
        return (place % 2 * half + index % half) * head_groups + place // 2

    devices = range(owners * head_groups)
    placed = {0: sent[0]}
    for k in sorted(range(1, parts), key=lambda k: (1 - k % 2, k)):
        placed[k] = lax.ppermute(sent[k], ("ctx", "head"), [(d, partner(d, k)) for d in devices])
    return pl.pallas_call(
        functools.partial(place_kernel, head_groups, half),
        out_shape=jax.ShapeDtypeStruct((tokens // head_groups, parts * columns), queries.dtype),
        in_specs=[pl.BlockSpec(memory_space=pltpu.VMEM)] * parts,
        out_specs=pl.BlockSpec(memory_space=pl.ANY),
        scratch_shapes=[pltpu.SemaphoreType.DMA((parts,))],
        compiler_params=pltpu.CompilerParams(vmem_limit_bytes=8 * 1024 * 1024),
        name="place_parts",
    )(*[placed[k] for k in range(parts)])


def solution(mesh):
    in_specs = (
        P("ctx", "head"),
        P("ctx", "head", None),
        P("ctx", "head", None),
        P("head", None),
        P("head", None),
    )
    out_specs = P(("ctx", "head"), None)
    return jax.shard_map(body, mesh=mesh, in_specs=in_specs, out_specs=out_specs, check_vma=False)
```

```python
import functools

import jax
import jax.numpy as jnp
from jax import lax
from jax.experimental import pallas as pl
from jax.experimental.pallas import tpu as pltpu
from jax.sharding import PartitionSpec as P

BLK = 64
NV = 64
MASKED = -1e30
CHUNK = 8
LOG2E = 1.4426950408889634


def collect_kernel(owners, cap, verticals, cache, span, mine, theirs, theirs_rest, raw, sem):
    me = lax.axis_index("ctx")
    upper = me // (owners // 2)
    cache_blocks = cache.shape[0] // BLK
    first = me * cache_blocks

    def block_copy(block, place, slot):
        return pltpu.make_async_copy(
            cache.at[pl.ds(pl.multiple_of(block * BLK, BLK), BLK)], raw.at[place, slot], sem.at[place, slot]
        )

    found = []
    for place in range(2):
        head = upper if place == 0 else 1 - upper

        def visit(n, count):
            block = verticals[head, n] - first
            hit = (block >= 0) & (block < cache_blocks) & (count < cap)

            @pl.when(hit)
            def _():
                block_copy(block, place, count).start()

            return count + hit.astype(jnp.int32)

        found.append(lax.fori_loop(0, NV, visit, jnp.int32(0)))
    split = cap // 2
    for own in range(2):

        @pl.when(upper == own)
        def _():
            mine[cap * BLK :, :] = span[:, own, :]
            theirs[split * BLK :, :] = span[:, 1 - own, :]
            for place, target, start, stop in ((1, theirs, 0, split), (1, theirs_rest, split, cap), (0, mine, 0, cap)):
                head = own if place == 0 else 1 - own

                def unpack(slot, carry):
                    block_copy(0, place, slot).wait()
                    at = pl.ds(pl.multiple_of((slot - start) * BLK, BLK), BLK)
                    target[at, :] = raw[place, slot, :, head, :]
                    return carry

                lax.fori_loop(start, jnp.minimum(found[place], stop), unpack, 0)


class Stage:
    def __init__(self, owners, group, depth, tokens, width, parts, pieces, known, late, first, slash, tail, last):
        self.owners, self.group, self.depth = owners, group, depth
        self.tokens, self.width, self.parts = tokens, width, parts
        self.pieces, self.known, self.late = pieces, known, late
        self.first, self.slash, self.tail, self.last = first, slash, tail, last
        self.half = owners // 2
        self.blocks = tokens // BLK
        self.rows = group * BLK
        self.state_rows = 2 * self.blocks * self.rows

    def owner(self, far, m, *_):
        me = lax.axis_index("ctx")
        upper = me // self.half
        return ((1 - upper) if far else upper) * self.half + ((me % self.half) ^ m)


def attend_kernel(stage, scalars, offsets, *refs):
    refs = list(refs)

    def take(count):
        taken, refs[:count] = refs[:count], []
        return taken

    half, blocks, rows, depth, tokens = stage.half, stage.blocks, stage.rows, stage.depth, stage.tokens
    me = lax.axis_index("ctx")
    upper = me // half
    head = upper
    width_kv = 2 * depth
    factor = LOG2E * depth**-0.5
    if stage.first:
        q_near, q_far = take(2)
    else:
        (queries,) = take(1)
    sources = take(len(stage.pieces))
    if stage.first:
        top, acc, queries, counts = take(4)
    else:
        take(2)
        top, acc = take(2)
        counts = scalars
    outs = take(stage.parts) if stage.last else []
    keys, sem = take(2)

    if stage.first:

        def clear(n, carry):
            counts[n] = 0
            return carry

        lax.fori_loop(0, stage.owners, clear, 0)

        def tally(n, carry):
            owner = scalars[head, n] // stage.width
            counts[owner] = counts[owner] + 1
            return carry

        lax.fori_loop(0, NV, tally, 0)

    held = [
        jnp.clip(counts[stage.owner(*piece)] - piece[2][0], 0, piece[2][1] - piece[2][0]) for piece in stage.pieces
    ]
    seen = sum(held[: stage.known], jnp.int32(0))
    present = sum(held[stage.known :], seen)
    begin = seen // CHUNK * CHUNK
    end = jnp.int32(NV) if stage.last else present // CHUNK * CHUNK
    place = jnp.int32(0)
    for source, live in zip(sources, held):

        def fetch(n, carry, place=place, source=source):
            at = place + n - begin
            pltpu.make_async_copy(
                source.at[pl.ds(pl.multiple_of(n * BLK, BLK), BLK)],
                keys.at[pl.ds(pl.multiple_of(at * BLK, BLK), BLK), pl.ds(0, width_kv)],
                sem.at[at // CHUNK],
            ).start()
            return carry

        lax.fori_loop(jnp.clip(begin - place, 0, live), jnp.clip(end - place, 0, live), fetch, 0)
        place = place + live

    span_copies = []
    if stage.slash or stage.tail:
        span, bias, span_sem = take(3)
        wanted = stage.late if stage.tail else [piece for piece in stage.pieces if piece[3]]
        for n, piece in enumerate(wanted):
            at = n if stage.tail else stage.owner(*piece)
            slots = piece[2][1] - piece[2][0]
            copy = pltpu.make_async_copy(
                sources[stage.pieces.index(piece)].at[pl.ds(slots * BLK, tokens)],
                span.at[pl.ds(pl.multiple_of(at * tokens, BLK), tokens), pl.ds(0, width_kv)],
                span_sem,
            )
            copy.start()
            span_copies.append(copy)
    keys[:, width_kv:] = jnp.ones((keys.shape[0], depth), keys.dtype)
    if stage.first:
        for tile in range(2 * blocks):
            q_ref, block = (q_near, tile) if tile < blocks else (q_far, tile - blocks)
            for j in range(stage.group):
                queries[tile * rows + j * BLK : tile * rows + (j + 1) * BLK, :] = q_ref[
                    block * BLK : (block + 1) * BLK, j * depth : (j + 1) * depth
                ]
        top[...] = jnp.full(top.shape, MASKED, jnp.float32)
        acc[...] = jnp.zeros(acc.shape, jnp.float32)

    def fold(at, scores, values):
        old = top[at, :]
        new = jnp.maximum(old, jnp.max(scores, axis=1, keepdims=True))
        wide = jnp.concatenate([new] * (scores.shape[1] // depth), 1)
        weights = jnp.exp2((scores - wide) * factor).astype(jnp.bfloat16)
        keep = jnp.exp2((old - new) * factor)
        top[at, :] = new
        acc[at, :] = acc[at, :] * jnp.concatenate([keep, keep], 1) + jnp.dot(
            weights, values, preferred_element_type=jnp.float32
        )

    def products(at, rows_k):
        return lax.dot_general(
            queries[at, :], rows_k, (((1,), (1,)), ((), ())), preferred_element_type=jnp.float32
        )

    tiles = [slice(tile * rows, (tile + 1) * rows) for tile in range(2 * blocks)]

    def step(c, carry):
        part = pl.ds(pl.multiple_of(c * (CHUNK * BLK), CHUNK * BLK), CHUNK * BLK)
        chunk = keys.at[part, pl.ds(0, width_kv)]
        pltpu.make_async_copy(chunk, chunk, sem.at[c]).wait()
        scores = products(tiles[0], keys[part, :depth])
        for at, following in zip(tiles, tiles[1:] + [None]):
            ahead = products(following, keys[part, :depth]) if following else None
            fold(at, scores, keys[part, depth:])
            scores = ahead
        return carry

    lax.fori_loop(0, (end - begin) // CHUNK, step, 0)

    if span_copies:
        for copy in span_copies:
            copy.wait()
        slash_count = offsets.shape[1]
        q_at = lax.broadcasted_iota(jnp.int32, (BLK, BLK), 0)
        k_at = lax.broadcasted_iota(jnp.int32, (BLK, BLK), 1)
        behind = k_at <= q_at
        late_owners = [stage.owner(*piece) for piece in stage.late]

        def masked(at, tile, rows_k, values):
            scores = products(at, rows_k)
            scores = scores.reshape(stage.group, BLK, rows_k.shape[0]) + bias[tile][None]
            fold(at, scores.reshape(rows, rows_k.shape[0]), values)

        if stage.slash:
            (slash,) = take(1)
            slash[:, :, width_kv:] = jnp.ones((2 * blocks, slash_count * BLK, depth), slash.dtype)
        else:
            span[:, width_kv:] = jnp.ones((span.shape[0], depth), span.dtype)
        for tile, at in enumerate(tiles):
            index = me if tile < blocks else (me + half) % stage.owners
            position = index * blocks + tile % blocks
            if stage.slash:
                for s in range(slash_count):
                    offset = offsets[head, s]
                    block = position - offset
                    here = block >= 0
                    for owner in late_owners:
                        here = here & (block // blocks != owner)
                    start = pl.multiple_of(jnp.where(here, block, position) * BLK, BLK)
                    slash[tile, s * BLK : (s + 1) * BLK, :width_kv] = span[pl.ds(start, BLK), :]
                    allowed = here & ((offset > 0) | behind)
                    bias[tile, :, s * BLK : (s + 1) * BLK] = jnp.where(allowed, 0.0, MASKED)
                masked(at, tile, slash[tile, :, :depth], slash[tile, :, depth:])
            else:
                for n, owner in enumerate(late_owners):
                    for k in range(blocks):
                        distance = position - (owner * blocks + k)
                        chosen = distance == offsets[head, 0]
                        for s in range(1, slash_count):
                            chosen = chosen | (distance == offsets[head, s])
                        allowed = chosen & ((distance > 0) | behind)
                        column = n * tokens + k * BLK
                        bias[tile, :, column : column + BLK] = jnp.where(allowed, 0.0, MASKED)
                masked(at, tile, span[:, :depth], span[:, depth:])

    if stage.last:
        lane = lax.axis_index("head")
        for k, out in enumerate(outs):
            part_rows = out.shape[0]
            token = (lane ^ (k >> 1)) * part_rows
            base = ((k & 1) * blocks + token // BLK) * rows + token % BLK
            for j in range(stage.group):
                at = pl.ds(pl.multiple_of(base + j * BLK, part_rows), part_rows)
                both = acc[at, :]
                out[:, j * depth : (j + 1) * depth] = (both[:, :depth] / both[:, depth:]).astype(out.dtype)


def attend(stage, scalars, offsets, queries, pieces, state, name):
    depth, rows, blocks = stage.depth, stage.state_rows, stage.blocks
    kind = jnp.bfloat16
    held = [jax.ShapeDtypeStruct((rows, depth), jnp.float32), jax.ShapeDtypeStruct((rows, 2 * depth), jnp.float32)]
    vmem, smem = pl.BlockSpec(memory_space=pltpu.VMEM), pl.BlockSpec(memory_space=pltpu.SMEM)
    out_shape, out_specs = list(held), [vmem] * 2
    if stage.first:
        out_shape += [
            jax.ShapeDtypeStruct((rows, depth), kind),
            jax.ShapeDtypeStruct((stage.owners,), jnp.int32),
        ]
        out_specs += [vmem, smem]
    if stage.last:
        part = jax.ShapeDtypeStruct((2 * stage.tokens // stage.parts, stage.group * depth), kind)
        out_shape += [part] * stage.parts
        out_specs += [vmem] * stage.parts
    scratch = [pltpu.VMEM((NV * BLK, 3 * depth), kind), pltpu.SemaphoreType.DMA((NV // CHUNK,))]
    share = sum(piece[3] for piece in stage.pieces[stage.known :]) * NV // stage.owners * BLK
    if stage.slash:
        keys = offsets.shape[1] * BLK
        scratch += [
            pltpu.VMEM((stage.owners * stage.tokens, 2 * depth), kind),
            pltpu.VMEM((2 * blocks, BLK, keys), jnp.float32),
            pltpu.SemaphoreType.DMA,
            pltpu.VMEM((2 * blocks, keys, 3 * depth), kind),
        ]
        share += keys
    elif stage.tail:
        keys = len(stage.late) * stage.tokens
        scratch += [
            pltpu.VMEM((keys, 3 * depth), kind),
            pltpu.VMEM((2 * blocks, BLK, keys), jnp.float32),
            pltpu.SemaphoreType.DMA,
        ]
    operands = [scalars, offsets, *queries, *pieces, *state]
    in_specs = [vmem] * len(queries) + [pl.BlockSpec(memory_space=pl.ANY)] * len(pieces) + [vmem] * len(state)
    return pl.pallas_call(
        functools.partial(attend_kernel, stage),
        out_shape=out_shape,
        grid_spec=pltpu.PrefetchScalarGridSpec(
            num_scalar_prefetch=2, grid=(1,), in_specs=in_specs, out_specs=out_specs, scratch_shapes=scratch
        ),
        input_output_aliases={len(operands) - len(state) + n: n for n in range(len(state))},
        compiler_params=pltpu.CompilerParams(vmem_limit_bytes=28 * 1024 * 1024),
        cost_estimate=pl.CostEstimate(
            flops=8 * rows * depth * share, bytes_accessed=share * 4 * depth, transcendentals=0
        ),
        name=name,
    )(*operands)


def place_kernel(head_groups, half, *refs):
    *parts, out, sem = refs
    here = lax.axis_index("head") * 2 + lax.axis_index("ctx") // half
    copies = []
    for k, part in enumerate(parts):
        columns = part.shape[1]
        start = pl.multiple_of((here ^ k) * columns, columns)
        copies.append(pltpu.make_async_copy(part, out.at[:, pl.ds(start, columns)], sem.at[k]))
        copies[-1].start()
    for copy in copies:
        copy.wait()


def body(queries, span_kv, cache_kv, verticals, offsets):
    tokens = queries.shape[0]
    heads_kv, row_width = span_kv.shape[1:]
    depth = row_width // 2
    columns = queries.shape[1] // heads_kv
    group = columns // depth
    owners = lax.axis_size("ctx")
    head_groups = lax.axis_size("head")
    half = owners // 2
    cache_blocks = cache_kv.shape[0] // BLK
    cap = max(2, 2 * NV // owners)
    upper = lax.axis_index("ctx") // half

    across = [(i, (i + half) % owners) for i in range(owners)]
    send_q = lax.dynamic_slice_in_dim(queries, (1 - upper) * columns, columns, 1)
    q_near = lax.dynamic_slice_in_dim(queries, upper * columns, columns, 1)
    q_far = lax.ppermute(send_q, "ctx", across)
    split = cap // 2

    def rows_of(count):
        return jax.ShapeDtypeStruct((count, row_width), queries.dtype)

    mine, theirs, theirs_rest = pl.pallas_call(
        functools.partial(collect_kernel, owners, cap),
        out_shape=(rows_of(cap * BLK + tokens), rows_of(split * BLK + tokens), rows_of((cap - split) * BLK)),
        grid_spec=pltpu.PrefetchScalarGridSpec(
            num_scalar_prefetch=1,
            grid=(1,),
            in_specs=[pl.BlockSpec(memory_space=pl.ANY), pl.BlockSpec(memory_space=pltpu.VMEM)],
            out_specs=[pl.BlockSpec(memory_space=pltpu.VMEM)] * 3,
            scratch_shapes=[
                pltpu.VMEM((2, cap, BLK, heads_kv, row_width), queries.dtype),
                pltpu.SemaphoreType.DMA((2, cap)),
            ],
        ),
        compiler_params=pltpu.CompilerParams(vmem_limit_bytes=60 * 1024 * 1024),
        cost_estimate=pl.CostEstimate(
            flops=0, bytes_accessed=4 * cap * BLK * heads_kv * row_width, transcendentals=0
        ),
        name="collect_slots",
    )(verticals, cache_kv, span_kv)

    def swap(x, bit):
        return lax.ppermute(x, "ctx", [(i, i ^ bit) for i in range(owners)])

    bits = []
    bit = half // 2
    while bit:
        bits.append(bit)
        bit //= 2
    parts = 2 * head_groups
    whole, low, high = (0, cap), (0, split), (split, cap)
    last_bit = bits[-1]
    late = [(True, m | last_bit, low, True) for m in range(1, half) if not m & last_bit]
    places, values = [], []
    state, operands, scalars = [], [q_near, q_far], verticals

    def stage(name, *arrived, slash=False, late_span=False, last=False):
        nonlocal state, operands, scalars
        known, first = len(places), not places
        for far_side, slots, tail, sides in arrived:
            places.extend((far_side, m, slots, tail) for m in sides)
            values.extend(sides.values())
        kind = Stage(
            owners, group, depth, tokens, cache_blocks, parts, list(places), known,
            late if slash or late_span else [], first, slash, late_span, last,
        )
        top, acc, *more = attend(kind, scalars, offsets, operands, values, state, name)
        state = [top, acc]
        if first:
            operands, scalars = [more[0]], more[1]
        return more

    theirs, q_far = lax.optimization_barrier((theirs, q_far))
    operands[1] = q_far
    near = {0: mine}
    far = {0: lax.ppermute(theirs, "ctx", across)}
    rest = {0: lax.ppermute(theirs_rest, "ctx", across)}
    own = swap(mine, last_bit)
    for bit in bits[:-1]:
        near.update({m | bit: swap(x, bit) for m, x in near.items()})
    del near[0]
    near, far[0] = lax.optimization_barrier((near, far[0]))
    forwarded = {m | last_bit: swap(x[split * BLK :], last_bit) for m, x in near.items()}
    turned = {last_bit: own[: split * BLK]}
    for bit in bits[:-1]:
        turned.update({m | bit: swap(x, bit) for m, x in turned.items()})
    del turned[last_bit]
    stage("attend_own", (False, whole, True, {0: mine}))
    first_far, own, state = lax.optimization_barrier((far[0], own, state))
    far_own = swap(first_far, last_bit)
    rest[0], far_own, turned = lax.optimization_barrier((rest[0], far_own, turned))
    stage("attend_near", (False, whole, True, {last_bit: own} | near), (True, low, True, {0: first_far}))
    rest[0], state = lax.optimization_barrier((rest[0], state))
    for bit in bits[:-1]:
        far.update({m | bit: swap(x, bit) for m, x in far.items()})
        rest.update({m | bit: swap(x, bit) for m, x in rest.items()})
    far.pop(0)
    last_far = {m | last_bit: swap(x, last_bit) for m, x in far.items()}
    rest_own = swap(rest[0], last_bit)
    first_rest = rest.pop(0)
    last_rest = {m | last_bit: swap(x, last_bit) for m, x in rest.items()}
    stage(
        "attend_far", (False, high, True, forwarded), (False, low, False, turned),
        (True, low, True, {last_bit: far_own} | far),
        (True, high, False, {0: first_rest} | rest), slash=True,
    )
    stage("attend_tail", (True, low, True, last_far), (True, high, False, {last_bit: rest_own}), late_span=True)
    sent = stage("attend_last", (True, high, False, last_rest), last=True)

    def partner(device, k):
        index, lane = divmod(device, head_groups)
        place = (lane * 2 + index // half) ^ k
        return (place % 2 * half + index % half) * head_groups + place // 2

    devices = range(owners * head_groups)
    placed = {0: sent[0]}
    for k in sorted(range(1, parts), key=lambda k: (1 - k % 2, k)):
        placed[k] = lax.ppermute(sent[k], ("ctx", "head"), [(d, partner(d, k)) for d in devices])
    return pl.pallas_call(
        functools.partial(place_kernel, head_groups, half),
        out_shape=jax.ShapeDtypeStruct((tokens // head_groups, parts * columns), queries.dtype),
        in_specs=[pl.BlockSpec(memory_space=pltpu.VMEM)] * parts,
        out_specs=pl.BlockSpec(memory_space=pl.ANY),
        scratch_shapes=[pltpu.SemaphoreType.DMA((parts,))],
        compiler_params=pltpu.CompilerParams(vmem_limit_bytes=8 * 1024 * 1024),
        name="place_parts",
    )(*[placed[k] for k in range(parts)])


def solution(mesh):
    in_specs = (
        P("ctx", "head"),
        P("ctx", "head", None),
        P("ctx", "head", None),
        P("head", None),
        P("head", None),
    )
    out_specs = P(("ctx", "head"), None)
    return jax.shard_map(body, mesh=mesh, in_specs=in_specs, out_specs=out_specs, check_vma=False)
```

```python
import functools

import jax
import jax.numpy as jnp
from jax import lax
from jax.experimental import pallas as pl
from jax.experimental.pallas import tpu as pltpu
from jax.sharding import PartitionSpec as P

BLK = 64
NV = 64
MASKED = -1e30
CHUNK = 8
LOG2E = 1.4426950408889634


def collect_kernel(owners, cap, verticals, cache, span, mine, theirs, theirs_rest, raw, sem):
    me = lax.axis_index("ctx")
    upper = me // (owners // 2)
    cache_blocks = cache.shape[0] // BLK
    first = me * cache_blocks

    def block_copy(block, place, slot):
        return pltpu.make_async_copy(
            cache.at[pl.ds(pl.multiple_of(block * BLK, BLK), BLK)], raw.at[place, slot], sem.at[place, slot]
        )

    found = []
    for place in range(2):
        head = upper if place == 0 else 1 - upper

        def visit(n, count):
            block = verticals[head, n] - first
            hit = (block >= 0) & (block < cache_blocks) & (count < cap)

            @pl.when(hit)
            def _():
                block_copy(block, place, count).start()

            return count + hit.astype(jnp.int32)

        found.append(lax.fori_loop(0, NV, visit, jnp.int32(0)))
    split = cap // 2
    for own in range(2):

        @pl.when(upper == own)
        def _():
            mine[cap * BLK :, :] = span[:, own, :]
            theirs[split * BLK :, :] = span[:, 1 - own, :]
            for place, target, start, stop in ((1, theirs, 0, split), (1, theirs_rest, split, cap), (0, mine, 0, cap)):
                head = own if place == 0 else 1 - own

                def unpack(slot, carry):
                    block_copy(0, place, slot).wait()
                    at = pl.ds(pl.multiple_of((slot - start) * BLK, BLK), BLK)
                    target[at, :] = raw[place, slot, :, head, :]
                    return carry

                lax.fori_loop(start, jnp.minimum(found[place], stop), unpack, 0)


class Stage:
    def __init__(self, owners, group, depth, tokens, width, parts, pieces, known, late, first, slash, tail, last):
        self.owners, self.group, self.depth = owners, group, depth
        self.tokens, self.width, self.parts = tokens, width, parts
        self.pieces, self.known, self.late = pieces, known, late
        self.first, self.slash, self.tail, self.last = first, slash, tail, last
        self.half = owners // 2
        self.blocks = tokens // BLK
        self.rows = group * BLK
        self.state_rows = 2 * self.blocks * self.rows

    def owner(self, far, m, *_):
        me = lax.axis_index("ctx")
        upper = me // self.half
        return ((1 - upper) if far else upper) * self.half + ((me % self.half) ^ m)


def attend_kernel(stage, scalars, offsets, *refs):
    refs = list(refs)

    def take(count):
        taken, refs[:count] = refs[:count], []
        return taken

    half, blocks, rows, depth, tokens = stage.half, stage.blocks, stage.rows, stage.depth, stage.tokens
    me = lax.axis_index("ctx")
    upper = me // half
    head = upper
    width_kv = 2 * depth
    factor = LOG2E * depth**-0.5
    if stage.first:
        q_near, q_far = take(2)
    else:
        (queries,) = take(1)
    sources = take(len(stage.pieces))
    if stage.first:
        top, acc, queries, counts = take(4)
    else:
        take(2)
        top, acc = take(2)
        counts = scalars
    outs = take(stage.parts) if stage.last else []
    keys, sem = take(2)

    if stage.first:

        def clear(n, carry):
            counts[n] = 0
            return carry

        lax.fori_loop(0, stage.owners, clear, 0)

        def tally(n, carry):
            owner = scalars[head, n] // stage.width
            counts[owner] = counts[owner] + 1
            return carry

        lax.fori_loop(0, NV, tally, 0)

    held = [
        jnp.clip(counts[stage.owner(*piece)] - piece[2][0], 0, piece[2][1] - piece[2][0]) for piece in stage.pieces
    ]
    seen = sum(held[: stage.known], jnp.int32(0))
    present = sum(held[stage.known :], seen)
    begin = seen // CHUNK * CHUNK
    end = jnp.int32(NV) if stage.last else present // CHUNK * CHUNK
    place = jnp.int32(0)
    for source, live in zip(sources, held):

        def fetch(n, carry, place=place, source=source):
            at = place + n - begin
            pltpu.make_async_copy(
                source.at[pl.ds(pl.multiple_of(n * BLK, BLK), BLK)],
                keys.at[pl.ds(pl.multiple_of(at * BLK, BLK), BLK), pl.ds(0, width_kv)],
                sem.at[at // CHUNK],
            ).start()
            return carry

        lax.fori_loop(jnp.clip(begin - place, 0, live), jnp.clip(end - place, 0, live), fetch, 0)
        place = place + live

    span_copies = []
    if stage.slash or stage.tail:
        span, bias, span_sem = take(3)
        wanted = stage.late if stage.tail else [piece for piece in stage.pieces if piece[3]]
        for n, piece in enumerate(wanted):
            at = n if stage.tail else stage.owner(*piece)
            slots = piece[2][1] - piece[2][0]
            copy = pltpu.make_async_copy(
                sources[stage.pieces.index(piece)].at[pl.ds(slots * BLK, tokens)],
                span.at[pl.ds(pl.multiple_of(at * tokens, BLK), tokens), pl.ds(0, width_kv)],
                span_sem,
            )
            copy.start()
            span_copies.append(copy)
    keys[:, width_kv:] = jnp.ones((keys.shape[0], depth), keys.dtype)
    if stage.first:
        for tile in range(2 * blocks):
            q_ref, block = (q_near, tile) if tile < blocks else (q_far, tile - blocks)
            for j in range(stage.group):
                queries[tile * rows + j * BLK : tile * rows + (j + 1) * BLK, :] = q_ref[
                    block * BLK : (block + 1) * BLK, j * depth : (j + 1) * depth
                ]
        top[...] = jnp.full(top.shape, MASKED, jnp.float32)
        acc[...] = jnp.zeros(acc.shape, jnp.float32)

    def fold(at, scores, values):
        old = top[at, :]
        new = jnp.maximum(old, jnp.max(scores, axis=1, keepdims=True))
        wide = jnp.concatenate([new] * (scores.shape[1] // depth), 1)
        weights = jnp.exp2((scores - wide) * factor).astype(jnp.bfloat16)
        keep = jnp.exp2((old - new) * factor)
        top[at, :] = new
        acc[at, :] = acc[at, :] * jnp.concatenate([keep, keep], 1) + jnp.dot(
            weights, values, preferred_element_type=jnp.float32
        )

    def products(at, rows_k):
        return lax.dot_general(
            queries[at, :], rows_k, (((1,), (1,)), ((), ())), preferred_element_type=jnp.float32
        )

    tiles = [slice(tile * rows, (tile + 1) * rows) for tile in range(2 * blocks)]

    def step(c, carry):
        part = pl.ds(pl.multiple_of(c * (CHUNK * BLK), CHUNK * BLK), CHUNK * BLK)
        chunk = keys.at[part, pl.ds(0, width_kv)]
        pltpu.make_async_copy(chunk, chunk, sem.at[c]).wait()
        scores = products(tiles[0], keys[part, :depth])
        for at, following in zip(tiles, tiles[1:] + [None]):
            ahead = products(following, keys[part, :depth]) if following else None
            fold(at, scores, keys[part, depth:])
            scores = ahead
        return carry

    lax.fori_loop(0, (end - begin) // CHUNK, step, 0)

    if span_copies:
        for copy in span_copies:
            copy.wait()
        slash_count = offsets.shape[1]
        q_at = lax.broadcasted_iota(jnp.int32, (BLK, BLK), 0)
        k_at = lax.broadcasted_iota(jnp.int32, (BLK, BLK), 1)
        behind = k_at <= q_at
        late_owners = [stage.owner(*piece) for piece in stage.late]

        def masked(at, tile, rows_k, values):
            scores = products(at, rows_k)
            scores = scores.reshape(stage.group, BLK, rows_k.shape[0]) + bias[tile][None]
            fold(at, scores.reshape(rows, rows_k.shape[0]), values)

        if stage.slash:
            (slash,) = take(1)
            slash[:, :, width_kv:] = jnp.ones((2 * blocks, slash_count * BLK, depth), slash.dtype)
        else:
            span[:, width_kv:] = jnp.ones((span.shape[0], depth), span.dtype)
        for tile, at in enumerate(tiles):
            index = me if tile < blocks else (me + half) % stage.owners
            position = index * blocks + tile % blocks
            if stage.slash:
                for s in range(slash_count):
                    offset = offsets[head, s]
                    block = position - offset
                    here = block >= 0
                    for owner in late_owners:
                        here = here & (block // blocks != owner)
                    start = pl.multiple_of(jnp.where(here, block, position) * BLK, BLK)
                    slash[tile, s * BLK : (s + 1) * BLK, :width_kv] = span[pl.ds(start, BLK), :]
                    allowed = here & ((offset > 0) | behind)
                    bias[tile, :, s * BLK : (s + 1) * BLK] = jnp.where(allowed, 0.0, MASKED)
                masked(at, tile, slash[tile, :, :depth], slash[tile, :, depth:])
            else:
                for n, owner in enumerate(late_owners):
                    for k in range(blocks):
                        distance = position - (owner * blocks + k)
                        chosen = distance == offsets[head, 0]
                        for s in range(1, slash_count):
                            chosen = chosen | (distance == offsets[head, s])
                        allowed = chosen & ((distance > 0) | behind)
                        column = n * tokens + k * BLK
                        bias[tile, :, column : column + BLK] = jnp.where(allowed, 0.0, MASKED)
                masked(at, tile, span[:, :depth], span[:, depth:])

    if stage.last:
        lane = lax.axis_index("head")
        for k, out in enumerate(outs):
            part_rows = out.shape[0]
            token = (lane ^ (k >> 1)) * part_rows
            base = ((k & 1) * blocks + token // BLK) * rows + token % BLK
            for j in range(stage.group):
                at = pl.ds(pl.multiple_of(base + j * BLK, part_rows), part_rows)
                both = acc[at, :]
                out[:, j * depth : (j + 1) * depth] = (both[:, :depth] / both[:, depth:]).astype(out.dtype)


def attend(stage, scalars, offsets, queries, pieces, state, name):
    depth, rows, blocks = stage.depth, stage.state_rows, stage.blocks
    kind = jnp.bfloat16
    held = [jax.ShapeDtypeStruct((rows, depth), jnp.float32), jax.ShapeDtypeStruct((rows, 2 * depth), jnp.float32)]
    vmem, smem = pl.BlockSpec(memory_space=pltpu.VMEM), pl.BlockSpec(memory_space=pltpu.SMEM)
    out_shape, out_specs = list(held), [vmem] * 2
    if stage.first:
        out_shape += [
            jax.ShapeDtypeStruct((rows, depth), kind),
            jax.ShapeDtypeStruct((stage.owners,), jnp.int32),
        ]
        out_specs += [vmem, smem]
    if stage.last:
        part = jax.ShapeDtypeStruct((2 * stage.tokens // stage.parts, stage.group * depth), kind)
        out_shape += [part] * stage.parts
        out_specs += [vmem] * stage.parts
    scratch = [pltpu.VMEM((NV * BLK, 3 * depth), kind), pltpu.SemaphoreType.DMA((NV // CHUNK,))]
    share = sum(piece[3] for piece in stage.pieces[stage.known :]) * NV // stage.owners * BLK
    if stage.slash:
        keys = offsets.shape[1] * BLK
        scratch += [
            pltpu.VMEM((stage.owners * stage.tokens, 2 * depth), kind),
            pltpu.VMEM((2 * blocks, BLK, keys), jnp.float32),
            pltpu.SemaphoreType.DMA,
            pltpu.VMEM((2 * blocks, keys, 3 * depth), kind),
        ]
        share += keys
    elif stage.tail:
        keys = len(stage.late) * stage.tokens
        scratch += [
            pltpu.VMEM((keys, 3 * depth), kind),
            pltpu.VMEM((2 * blocks, BLK, keys), jnp.float32),
            pltpu.SemaphoreType.DMA,
        ]
    operands = [scalars, offsets, *queries, *pieces, *state]
    in_specs = [vmem] * len(queries) + [pl.BlockSpec(memory_space=pl.ANY)] * len(pieces) + [vmem] * len(state)
    return pl.pallas_call(
        functools.partial(attend_kernel, stage),
        out_shape=out_shape,
        grid_spec=pltpu.PrefetchScalarGridSpec(
            num_scalar_prefetch=2, grid=(1,), in_specs=in_specs, out_specs=out_specs, scratch_shapes=scratch
        ),
        input_output_aliases={len(operands) - len(state) + n: n for n in range(len(state))},
        compiler_params=pltpu.CompilerParams(vmem_limit_bytes=28 * 1024 * 1024),
        cost_estimate=pl.CostEstimate(
            flops=2 * rows * depth * share, bytes_accessed=share * 4 * depth, transcendentals=0
        ),
        name=name,
    )(*operands)


def place_kernel(head_groups, half, *refs):
    *parts, out, sem = refs
    here = lax.axis_index("head") * 2 + lax.axis_index("ctx") // half
    copies = []
    for k, part in enumerate(parts):
        columns = part.shape[1]
        start = pl.multiple_of((here ^ k) * columns, columns)
        copies.append(pltpu.make_async_copy(part, out.at[:, pl.ds(start, columns)], sem.at[k]))
        copies[-1].start()
    for copy in copies:
        copy.wait()


def body(queries, span_kv, cache_kv, verticals, offsets):
    tokens = queries.shape[0]
    heads_kv, row_width = span_kv.shape[1:]
    depth = row_width // 2
    columns = queries.shape[1] // heads_kv
    group = columns // depth
    owners = lax.axis_size("ctx")
    head_groups = lax.axis_size("head")
    half = owners // 2
    cache_blocks = cache_kv.shape[0] // BLK
    cap = max(2, 2 * NV // owners)
    upper = lax.axis_index("ctx") // half

    across = [(i, (i + half) % owners) for i in range(owners)]
    send_q = lax.dynamic_slice_in_dim(queries, (1 - upper) * columns, columns, 1)
    q_near = lax.dynamic_slice_in_dim(queries, upper * columns, columns, 1)
    q_far = lax.ppermute(send_q, "ctx", across)
    split = cap // 2

    def rows_of(count):
        return jax.ShapeDtypeStruct((count, row_width), queries.dtype)

    mine, theirs, theirs_rest = pl.pallas_call(
        functools.partial(collect_kernel, owners, cap),
        out_shape=(rows_of(cap * BLK + tokens), rows_of(split * BLK + tokens), rows_of((cap - split) * BLK)),
        grid_spec=pltpu.PrefetchScalarGridSpec(
            num_scalar_prefetch=1,
            grid=(1,),
            in_specs=[pl.BlockSpec(memory_space=pl.ANY), pl.BlockSpec(memory_space=pltpu.VMEM)],
            out_specs=[pl.BlockSpec(memory_space=pltpu.VMEM)] * 3,
            scratch_shapes=[
                pltpu.VMEM((2, cap, BLK, heads_kv, row_width), queries.dtype),
                pltpu.SemaphoreType.DMA((2, cap)),
            ],
        ),
        compiler_params=pltpu.CompilerParams(vmem_limit_bytes=60 * 1024 * 1024),
        cost_estimate=pl.CostEstimate(
            flops=0, bytes_accessed=4 * cap * BLK * heads_kv * row_width, transcendentals=0
        ),
        name="collect_slots",
    )(verticals, cache_kv, span_kv)

    def swap(x, bit):
        return lax.ppermute(x, "ctx", [(i, i ^ bit) for i in range(owners)])

    bits = []
    bit = half // 2
    while bit:
        bits.append(bit)
        bit //= 2
    parts = 2 * head_groups
    whole, low, high = (0, cap), (0, split), (split, cap)
    last_bit = bits[-1]
    late = [(True, m | last_bit, low, True) for m in range(1, half) if not m & last_bit]
    places, values = [], []
    state, operands, scalars = [], [q_near, q_far], verticals

    def stage(name, *arrived, slash=False, late_span=False, last=False):
        nonlocal state, operands, scalars
        known, first = len(places), not places
        for far_side, slots, tail, sides in arrived:
            places.extend((far_side, m, slots, tail) for m in sides)
            values.extend(sides.values())
        kind = Stage(
            owners, group, depth, tokens, cache_blocks, parts, list(places), known,
            late if slash or late_span else [], first, slash, late_span, last,
        )
        top, acc, *more = attend(kind, scalars, offsets, operands, values, state, name)
        state = [top, acc]
        if first:
            operands, scalars = [more[0]], more[1]
        return more

    theirs, q_far = lax.optimization_barrier((theirs, q_far))
    operands[1] = q_far
    near = {0: mine}
    far = {0: lax.ppermute(theirs, "ctx", across)}
    rest = {0: lax.ppermute(theirs_rest, "ctx", across)}
    own = swap(mine, last_bit)
    for bit in bits[:-1]:
        near.update({m | bit: swap(x, bit) for m, x in near.items()})
    del near[0]
    forwarded = {m | last_bit: swap(x, last_bit) for m, x in near.items()}
    stage("attend_own", (False, whole, True, {0: mine}))
    first_far, own, state = lax.optimization_barrier((far[0], own, state))
    far_own = swap(first_far, last_bit)
    rest[0], far_own = lax.optimization_barrier((rest[0], far_own))
    stage("attend_near", (False, whole, True, {last_bit: own} | near), (True, low, True, {0: first_far}))
    rest[0], state = lax.optimization_barrier((rest[0], state))
    for bit in bits[:-1]:
        far.update({m | bit: swap(x, bit) for m, x in far.items()})
        rest.update({m | bit: swap(x, bit) for m, x in rest.items()})
    far.pop(0)
    last_far = {m | last_bit: swap(x, last_bit) for m, x in far.items()}
    rest_own = swap(rest[0], last_bit)
    first_rest = rest.pop(0)
    last_rest = {m | last_bit: swap(x, last_bit) for m, x in rest.items()}
    stage(
        "attend_far", (False, whole, True, forwarded), (True, low, True, {last_bit: far_own} | far),
        (True, high, False, {0: first_rest} | rest), slash=True,
    )
    stage("attend_tail", (True, low, True, last_far), (True, high, False, {last_bit: rest_own}), late_span=True)
    sent = stage("attend_last", (True, high, False, last_rest), last=True)

    def partner(device, k):
        index, lane = divmod(device, head_groups)
        place = (lane * 2 + index // half) ^ k
        return (place % 2 * half + index % half) * head_groups + place // 2

    devices = range(owners * head_groups)
    placed = {0: sent[0]}
    for k in sorted(range(1, parts), key=lambda k: (1 - k % 2, -k)):
        placed[k] = lax.ppermute(sent[k], ("ctx", "head"), [(d, partner(d, k)) for d in devices])
    return pl.pallas_call(
        functools.partial(place_kernel, head_groups, half),
        out_shape=jax.ShapeDtypeStruct((tokens // head_groups, parts * columns), queries.dtype),
        in_specs=[pl.BlockSpec(memory_space=pltpu.VMEM)] * parts,
        out_specs=pl.BlockSpec(memory_space=pl.ANY),
        scratch_shapes=[pltpu.SemaphoreType.DMA((parts,))],
        compiler_params=pltpu.CompilerParams(vmem_limit_bytes=8 * 1024 * 1024),
        name="place_parts",
    )(*[placed[k] for k in range(parts)])


def solution(mesh):
    in_specs = (
        P("ctx", "head"),
        P("ctx", "head", None),
        P("ctx", "head", None),
        P("head", None),
        P("head", None),
    )
    out_specs = P(("ctx", "head"), None)
    return jax.shard_map(body, mesh=mesh, in_specs=in_specs, out_specs=out_specs, check_vma=False)
```
